32 devices in a mesh: section: 2 (over core), group: 2 (over x), replica: 8 (over z, y).
Axes of the slice: x: 2, y: 2, z: 4, core: 2. Of those that a mesh axis runs over, the one named last changes fastest.
Arguments:
- first_layer_input: bfloat16 [2, 8, 512, 1024], P(None, 'replica', 'group'), may hold values from -6 to 6
- boundary: int32 [2, 8], P(None, 'replica'), may hold values from 0 to 512, as said below
- input_gain: bfloat16 [2, 1024], P('section', 'group'), may hold values from 0.25 to 1.75
- in_proj: bfloat16 [2, 1024, 4384], P('section', 'group'), may hold values from -0.1875 to 0.1875
- conv_weight: bfloat16 [2, 2304, 4], P('section', 'group'), may hold values from -3 to 3
- conv_bias: bfloat16 [2, 2304], P('section', 'group'), may hold values from -3 to 3
- head_params: bfloat16 [2, 32, 3], P('section', 'group'), may hold values from -7 to 1.5, as said below
- output_gain: bfloat16 [2, 2048], P('section', 'group'), may hold values from 0.25 to 1.75
- out_proj: bfloat16 [2, 2048, 1024], P('section', 'group'), may hold values from -0.125 to 0.125
- cotangent: bfloat16 [2, 8, 512, 1024], P(None, 'replica', 'group'), may hold values from -6 to 6
Outputs:
- segment_output: bfloat16 [2, 2, 8, 512, 1024], P('section', None, 'replica', 'group')
- input_grad: bfloat16 [2, 2, 8, 512, 1024], P('section', None, 'replica', 'group')
- grad_input_gain: float32 [2, 1024], P('section', 'group')
- grad_in_proj: float32 [2, 1024, 4384], P('section', 'group')
- grad_conv_weight: float32 [2, 2304, 4], P('section', 'group')
- grad_conv_bias: float32 [2, 2304], P('section', 'group')
- grad_head_params: float32 [2, 32, 3], P('section', 'group')
- grad_output_gain: float32 [2, 2048], P('section', 'group')
- grad_out_proj: float32 [2, 2048, 1024], P('section', 'group')
The draws below stay inside these ranges and needn't reach their ends.
Inputs may be any that keep to these rules, and one draw needn't show every extreme that they name: `boundary`: one of the row's two sequences is longer than 256 tokens; 0 and 512 mean a single sequence; some row of each micro-batch holds a single sequence. `head_params`: column 0 is a bias added before softplus, column 1 the logarithm of a decay rate, column 2 a skip gain.
All inputs are finite; a program needn't handle non-finite values.
Results may differ from the reference program's by a relative error of at most 0.015.
The reference program's roundings to bfloat16 on the way count: a program that leaves them out, or rounds other values in their place, can miss the bound.
Values may be sent and summed in bfloat16 or wider, within the bound.
No kernel may reach another device: no remote copies, remote signals or barrier semaphores. Data moves between devices by JAX's collectives and lax.ppermute only.
A program may use at most 256 MiB of HBM per device.

```python
import math
import jax
import jax.numpy as jnp
from jax import lax

MODEL_WIDTH = 1024
HEADS = 32
HDIM = 64
NS = 128
KW = 4
SPAN = 256
MICRO_BATCHES = 2
DEVICE_TOKENS = 256
DI = 2048
CONVC = 2304
DIN = 4384
ROW_TOKENS = 512
BATCH_ROWS = 8


def draw_boundary(key, part):
    key = jax.random.fold_in(key, 5)
    random_keys = jax.random.split(key, 3)
    longest_sequence = jax.random.randint(random_keys[0], (MICRO_BATCHES, BATCH_ROWS), ROW_TOKENS - DEVICE_TOKENS + 1, ROW_TOKENS + 1)
    device_placement = jax.random.randint(random_keys[1], (MICRO_BATCHES, BATCH_ROWS), 0, 2)
    sampled_lengths = jnp.where(device_placement == 1, longest_sequence, ROW_TOKENS - longest_sequence)
    chosen = jax.random.randint(random_keys[2], (MICRO_BATCHES,), 0, BATCH_ROWS)
    forced = jnp.arange(BATCH_ROWS, dtype=jnp.int32)[None, :] == chosen[:, None]
    whole_sequence = jnp.where(jnp.arange(MICRO_BATCHES, dtype=jnp.int32) % 2 == 0, ROW_TOKENS, 0)[:, None]
    return jnp.where(forced, whole_sequence, sampled_lengths).astype(jnp.int32)


def draw_head_params(key, part):
    key = jax.random.fold_in(key, 11)
    random_keys = jax.random.split(key, 3)
    biases = jax.random.uniform(random_keys[0], (2, HEADS), jnp.float32, -2.0, 0.5)
    rates = jax.random.uniform(random_keys[1], (2, HEADS), jnp.float32, math.log(0.001), math.log(0.3))
    skips = jax.random.uniform(random_keys[2], (2, HEADS), jnp.float32, 0.5, 1.5)
    return jnp.stack([biases, rates, skips], axis=-1).astype(jnp.bfloat16)


def block_scale(key, extent, pieces, least, top_value):
    loudness = 1.0
    for axis_at, shards_of in pieces:
        draws = jax.random.uniform(jax.random.fold_in(jax.random.fold_in(key, 6), axis_at), (shards_of,), jnp.float32, least / len(pieces), top_value / len(pieces))
        loudness = loudness * jnp.repeat(jnp.exp(draws), extent[axis_at] // shards_of).reshape((-1,) + (1,) * (len(extent) - 1 - axis_at))
    return loudness


def noise(rng, extent, scale, reach, shards=(), held_as=jnp.bfloat16):
    result = scale * jax.random.normal(rng, extent, jnp.float32)
    if shards:
        result = result * block_scale(rng, extent, shards, -0.22, 0.18)
    return jnp.clip(result, -reach, reach).astype(held_as)


def setup_inputs(seed: int = 0) -> dict:
    arg_keys = jax.random.split(jax.random.key(seed), 11)
    return {
        "first_layer_input": noise(arg_keys[0], (MICRO_BATCHES, BATCH_ROWS, ROW_TOKENS, MODEL_WIDTH), 1.0, 6.0, ((1, 8), (2, 2))),
        "boundary": draw_boundary(jax.random.fold_in(arg_keys[10], 71), 0),
        "input_gain": jnp.clip(1.0 + 0.15 * jax.random.normal(arg_keys[2], (2, MODEL_WIDTH), jnp.float32), 0.25, 1.75).astype(jnp.bfloat16),
        "in_proj": noise(arg_keys[3], (2, MODEL_WIDTH, DIN), MODEL_WIDTH ** -0.5, 0.1875, ((0, 2), (1, 2))),
        "conv_weight": noise(arg_keys[4], (2, CONVC, KW), KW ** -0.5, 3.0, ((0, 2), (1, 2))),
        "conv_bias": noise(arg_keys[5], (2, CONVC), 0.5, 3.0, ((0, 2), (1, 2))),
        "head_params": draw_head_params(jax.random.fold_in(arg_keys[10], 71), 0),
        "output_gain": jnp.clip(1.0 + 0.15 * jax.random.normal(arg_keys[7], (2, DI), jnp.float32), 0.25, 1.75).astype(jnp.bfloat16),
        "out_proj": noise(arg_keys[8], (2, DI, MODEL_WIDTH), DI ** -0.5, 0.125, ((0, 2), (1, 2))),
        "cotangent": noise(arg_keys[9], (MICRO_BATCHES, BATCH_ROWS, ROW_TOKENS, MODEL_WIDTH), 1.0, 6.0, ((1, 8), (2, 2))),
    }


@jax.custom_vjp
def low(v):
    return lax.optimization_barrier(v.astype(jnp.bfloat16)).astype(jnp.float32)

@jax.custom_vjp
def low_back(v):
    return v

def low_keep(v):
    return (low(v), None)

def low_pass(kept, grad):
    return (grad,)

def back_keep(v):
    return (v, None)

def back_low(kept, grad):
    return (low(grad),)
low.defvjp(low_keep, low_pass)
low_back.defvjp(back_keep, back_low)

def rms_scale(values, gain):
    return values * lax.rsqrt(lax.optimization_barrier(jnp.mean(values * values, axis=-1, keepdims=True)) + 1e-05) * gain

def conv_silu(raw_mix, edge_rows, conv_weight, conv_bias, positions, boundary_pos):
    width = conv_weight.shape[1]
    padded = jnp.concatenate([edge_rows, raw_mix], axis=0)
    length = raw_mix.shape[0]
    total = jnp.zeros_like(raw_mix) + conv_bias[None, :]
    for offset in range(width):
        lag = width - 1 - offset
        source = padded[offset:offset + length]
        anchor = positions - lag
        dropped = (anchor < 0) | (anchor < boundary_pos) & (boundary_pos <= positions)
        total = total + jnp.where(dropped[:, None], 0.0, source * conv_weight[None, :, offset])
    return jax.nn.silu(total)

def ssd_blocks(values_x, read_b, read_c, step_size, rate, positions, boundary_pos):
    count = values_x.shape[0] // SPAN
    highest = lax.Precision.HIGHEST

    def block_step(state, block_item):
        block_x, block_b, block_c, block_dt, block_rate, block_pos = block_item
        decay_sum = jnp.cumsum(block_rate, axis=0)
        ordered = block_pos[:, None] >= block_pos[None, :]
        crossed = (block_pos[None, :] < boundary_pos) & (boundary_pos <= block_pos[:, None])
        inside = ordered & jnp.logical_not(crossed)
        spread = decay_sum.T[:, :, None] - decay_sum.T[:, None, :]
        decay_mat = jnp.exp(jnp.where(inside[None], spread, -jnp.inf))
        intersection = jnp.dot(block_c, block_b.T, precision=highest)
        mixing = decay_mat * intersection[None] * block_dt.T[:, None, :]
        direct = jnp.einsum('hij,jhp->ihp', mixing, block_x, precision=highest)
        fresh_start = (block_pos[0] <= boundary_pos) & (boundary_pos <= block_pos)
        carried = jnp.einsum('in,hpn->ihp', block_c, state, precision=highest)
        carry_scale = jnp.where(fresh_start[:, None], 0.0, jnp.exp(decay_sum))
        tail_cut = (block_pos < boundary_pos) & (boundary_pos <= block_pos[-1])
        tail_scale = jnp.where(tail_cut[:, None], 0.0, jnp.exp(decay_sum[-1][None, :] - decay_sum)) * block_dt
        fresh = jnp.einsum('jh,jhp,jn->hpn', tail_scale, block_x, block_b, precision=highest)
        whole_cut = (block_pos[0] <= boundary_pos) & (boundary_pos <= block_pos[-1])
        kept_scale = jnp.where(whole_cut, 0.0, jnp.exp(decay_sum[-1]))
        new_state = state * kept_scale[:, None, None] + fresh
        return (new_state, direct + carried * carry_scale[:, :, None])
    items = (values_x.reshape(count, SPAN, HEADS, HDIM), read_b.reshape(count, SPAN, NS), read_c.reshape(count, SPAN, NS), step_size.reshape(count, SPAN, HEADS), rate.reshape(count, SPAN, HEADS), positions.reshape(count, SPAN))
    start = jnp.zeros((HEADS, HDIM, NS), jnp.float32)
    final_state, outputs = lax.scan(jax.checkpoint(block_step), start, items)
    return (final_state, outputs.reshape(values_x.shape))

def layer_row(values, boundary_pos, weights):
    input_gain, in_proj, conv_weight, conv_bias, head_params, output_gain, out_proj = weights
    highest = lax.Precision.HIGHEST
    length = values.shape[0]
    positions = jnp.arange(length, dtype=jnp.int32)
    normed = low(rms_scale(values, input_gain))
    projected = low_back(jnp.dot(normed, in_proj, precision=highest))
    gate_cols = projected[:, :DI]
    raw_mix = projected[:, DI:DI + CONVC]
    step_raw = projected[:, DI + CONVC:]
    edge_rows = jnp.zeros((KW - 1, CONVC), jnp.float32)
    convolved = conv_silu(raw_mix, edge_rows, conv_weight, conv_bias, positions, boundary_pos)
    values_x = convolved[:, :DI].reshape(length, HEADS, HDIM)
    read_b = convolved[:, DI:DI + NS]
    read_c = convolved[:, DI + NS:]
    step_size = jax.nn.softplus(step_raw + head_params[:, 0])
    rate = -step_size * jnp.exp(head_params[:, 1])
    final_state, direct = ssd_blocks(values_x, read_b, read_c, step_size, rate, positions, boundary_pos)
    mixed_heads = direct + head_params[:, 2][None, :, None] * values_x
    mixed = mixed_heads.reshape(length, DI) * jax.nn.silu(gate_cols)
    gated = low(rms_scale(mixed, output_gain))
    return values + jnp.dot(gated, out_proj, precision=highest)

def reference(first_layer_input, boundary, input_gain, in_proj, conv_weight, conv_bias, head_params, output_gain, out_proj, cotangent):
    weights = tuple((w.astype(jnp.float32) for w in (input_gain, in_proj, conv_weight, conv_bias, head_params, output_gain, out_proj)))
    input_rows = first_layer_input.astype(jnp.float32).reshape(MICRO_BATCHES * BATCH_ROWS, ROW_TOKENS, MODEL_WIDTH)
    bounds = boundary.reshape(MICRO_BATCHES * BATCH_ROWS).astype(jnp.int32)
    tap_zero = jnp.zeros_like(input_rows)

    def both_segments(rows_first, tap_values, segment_weights):
        first = tuple((w[0] for w in segment_weights))
        second = tuple((w[1] for w in segment_weights))

        def segment_one(row_item):
            return layer_row(row_item[0], row_item[1], first)

        def segment_two(row_item):
            return layer_row(row_item[0], row_item[1], second)
        first_out = lax.map(jax.checkpoint(segment_one), (rows_first, bounds))
        middle = low(low_back(first_out)) + tap_values
        second_out = lax.map(jax.checkpoint(segment_two), (middle, bounds))
        return (first_out, second_out)
    (first_out, second_out), pull = jax.vjp(both_segments, input_rows, tap_zero, weights)
    grad_rows, grad_middle, grad_weights = pull((jnp.zeros_like(first_out), cotangent.astype(jnp.float32).reshape(input_rows.shape)))
    output_shape = (2, MICRO_BATCHES, BATCH_ROWS, ROW_TOKENS, MODEL_WIDTH)
    segment_output = jnp.stack([first_out, second_out]).reshape(output_shape).astype(jnp.bfloat16)
    input_grad = jnp.stack([grad_rows, grad_middle]).reshape(output_shape).astype(jnp.bfloat16)
    return (segment_output, input_grad, grad_weights[0], grad_weights[1], grad_weights[2], grad_weights[3], grad_weights[4], grad_weights[5], grad_weights[6])
```

```python
import functools

import jax
import jax.numpy as jnp
from jax import lax
from jax.experimental import pallas as pl
from jax.experimental.pallas import tpu as pltpu
from jax.sharding import PartitionSpec as P

DM = 1024
HEADS = 32
HDIM = 64
NS = 128
KW = 4
DI = 2048
CONVC = 2304
HL = HEADS // 2
DH = DI // 2
CH = DH + 2 * NS
CP = DH + CH + 128
LANE = 128
TILE = 256
RC = 32
HEAD_ROWS = 8
EPS = 1e-05
VMEM_BYTES = 63 * 1024 * 1024

f32 = jnp.float32
bf16 = jnp.bfloat16


def nn(left, right):
    return jnp.dot(left, right, preferred_element_type=f32)


def nt(left, right):
    return lax.dot_general(left, right, (((1,), (1,)), ((), ())), preferred_element_type=f32)


def tn(left, right):
    return lax.dot_general(left, right, (((0,), (0,)), ((), ())), preferred_element_type=f32)


def tile_at(index, size):
    return pl.ds(pl.multiple_of(index * size, size), size)


def loop(count, body):
    def step(index, carry):
        body(index)
        return carry

    lax.fori_loop(0, count, step, 0)


def iota(shape, dim):
    return lax.broadcasted_iota(jnp.int32, shape, dim)


def sigmoid(values):
    return 0.5 * jnp.tanh(0.5 * values) + 0.5


def softplus(values):
    small = jnp.exp(-jnp.abs(values))
    series = small * (1.0 - small * (0.5 - small * (1.0 / 3.0 - small * 0.25)))
    return jnp.maximum(values, 0.0) + jnp.where(small < 0.03, series, jnp.log(1.0 + small))


def split3(values):
    high = values.astype(bf16)
    rest = values - high.astype(f32)
    middle = rest.astype(bf16)
    low = (rest - middle.astype(f32)).astype(bf16)
    return high, middle, low


def pack3(values):
    high, middle, low = split3(values)
    packed = (
        high.astype(f32)
        + pltpu.roll(middle.astype(f32), HL, 1)
        + pltpu.roll(low.astype(f32), 2 * HL, 1)
    )
    return packed.astype(bf16)


def fill_spread(spread_s, width):
    shape = spread_s.shape
    row = iota(shape, 0)
    col = iota(shape, 1)
    hit = (row < 3 * HL) & ((row & (HL - 1)) == col // width)
    spread_s[...] = jnp.where(hit, 1.0, 0.0).astype(bf16)


def fill_gather(gather_s):
    shape = gather_s.shape
    hit = iota(shape, 0) // HDIM == iota(shape, 1)
    gather_s[...] = jnp.where(hit, 1.0, 0.0).astype(bf16)


def head_sums(values, gather_s):
    high = values.astype(bf16)
    low = (values - high.astype(f32)).astype(bf16)
    rows = values.shape[0]
    both = nn(jnp.concatenate([high, low], axis=0), gather_s[...])
    return both[:rows] + both[rows:]


def fill_masks(mask_s, bound, count):
    rows = mask_s.shape[1]
    pos = iota((rows, LANE), 0)
    for lag in range(1, KW):
        anchor = pos - lag
        dropped = (anchor < 0) | ((anchor < bound) & (bound <= pos)) | (pos >= count)
        mask_s[lag - 1] = jnp.where(dropped, 0.0, 1.0)


def conv_phase(proj_s, par, mask_s, conv_s, pre_s, count):
    def body(index):
        src = pl.ds(pl.multiple_of(DH + index * LANE, LANE), LANE)
        dst = tile_at(index, LANE)
        taps = par[0:8, dst]
        for at in range(0, count, 64):
            pre = taps[4:5] + taps[3:4] * proj_s[HEAD_ROWS + at : HEAD_ROWS + at + 64, src]
            for lag in range(1, KW):
                begin = HEAD_ROWS + at - lag
                part = proj_s[begin : begin + 64, src] * mask_s[lag - 1, at : at + 64]
                pre = pre + taps[3 - lag : 4 - lag] * part
            if pre_s is not None:
                pre_s[at : at + 64, dst] = pre
            conv_s[at : at + 64, dst] = pre * sigmoid(pre)

    loop(CH // LANE, body)


def step_phase(proj_s, hp, dt_s, rate_s, cs_s, cst_s, count):
    span = count // 2
    lanes = iota((count, LANE), 1)
    raw = proj_s[HEAD_ROWS : HEAD_ROWS + count, DH + CH : CP] + hp[0:1, :]
    step = jnp.where(lanes < HL, softplus(raw), 0.0)
    rate = -step * hp[1:2, :]
    dt_s[...] = step
    rate_s[...] = rate
    lower = jnp.where(iota((span, span), 0) >= iota((span, span), 1), 1.0, 0.0).astype(bf16)
    for block in range(2):
        rows = slice(block * span, (block + 1) * span)
        triple = jnp.concatenate(split3(rate[rows]), axis=1)
        sums = nn(lower, triple)
        total = sums[:, :LANE] + sums[:, LANE : 2 * LANE] + sums[:, 2 * LANE :]
        cs_s[rows] = total
        cst_s[block] = jnp.transpose(total)


def scaled_inputs(conv_s, dt_s, spread_s, xdt_s, xlo_s, count):
    def body(index):
        rows = tile_at(index, RC * 4)
        scale = nn(pack3(dt_s[rows]), spread_s[...])
        v = conv_s[rows, :DH] * scale
        xdt_s[rows] = v.astype(bf16)
        xlo_s[rows] = (v - v.astype(bf16).astype(f32)).astype(bf16)

    loop(count // (RC * 4), body)


def tail_weight(cs_s, bound, span):
    total = cs_s[0:span]
    pos = iota((span, LANE), 0)
    cut = (pos < bound) & (bound <= span - 1)
    lanes = iota((span, LANE), 1)
    keep = jnp.logical_not(cut) & (lanes < HL)
    return jnp.where(keep, jnp.exp(total[span - 1 : span] - total), 0.0)


def carry_weight(cs_s, bound, span):
    total = cs_s[span : 2 * span]
    pos = iota((span, LANE), 0) + span
    fresh = (span <= bound) & (bound <= pos)
    lanes = iota((span, LANE), 1)
    keep = jnp.logical_not(fresh) & (lanes < HL)
    return jnp.where(keep, jnp.exp(total), 0.0)


def inside_mask(block, bound, span, flipped):
    shape = (span, span)
    later = iota(shape, 1 if flipped else 0) + block * span
    early = iota(shape, 0 if flipped else 1) + block * span
    keep = (later >= early) & jnp.logical_not((early < bound) & (bound <= later))
    return jnp.where(keep, 1.0, 0.0)


def split2(values):
    high = values.astype(bf16)
    return high, (values - high.astype(f32)).astype(bf16)


def nt3(left, right):
    left_high, left_low = split2(left)
    right_high, right_low = split2(right)
    return nt(
        jnp.concatenate([left_high, left_low, left_high], axis=1),
        jnp.concatenate([right_high, right_high, right_low], axis=1),
    )


def nn3(left, right):
    left_high, left_low = split2(left)
    right_high, right_low = split2(right)
    return nn(
        jnp.concatenate([left_high, left_low, left_high], axis=1),
        jnp.concatenate([right_high, right_high, right_low], axis=0),
    )


def mix_tokens(first, second, high, low):
    rows = first.shape[0]
    first_high, first_low = split2(first)
    second_high, second_low = split2(second)
    stacked = jnp.concatenate([first_high, second_high, first_low, second_low], axis=0)
    both = nn(stacked, jnp.concatenate([high, low], axis=1))
    left, right = both[:, :LANE], both[:, LANE:]
    total = left[: 2 * rows] + right[: 2 * rows] + left[2 * rows :]
    keep = iota((rows, LANE), 1) < HDIM
    return jnp.where(keep, total[:rows], total[rows:])


def copies(pairs, sems, base):
    return [
        pltpu.make_async_copy(src, dst, sems.at[base + at]) for at, (src, dst) in enumerate(pairs)
    ]


def load_outer(layer, sec, wo_a, wo_b, wo_s, sem):
    held = pltpu.make_async_copy(wo_a, wo_s, sem)
    given = pltpu.make_async_copy(wo_b, wo_s, sem)

    @pl.when(sec == layer)
    def _():
        held.start()

    @pl.when(sec != layer)
    def _():
        given.start()

    return held


def load_weights(layer, sec, grp, w_a, w_b, w_x, w_y, w_s, sems):
    width = w_a.shape[1]
    part = w_x.shape[0]
    mine = pl.ds(pl.multiple_of(grp * width, width), width)
    other = pl.ds(pl.multiple_of((1 - grp) * width, width), width)
    first = pl.multiple_of(grp * DH, DH)
    steps = pl.multiple_of(DI + CONVC + grp * HL, HL)
    places = [
        (pl.ds(first, DH), pl.ds(0, DH)),
        (pl.ds(DI + first, DH), pl.ds(DH, DH)),
        (pl.ds(2 * DI, 2 * NS), pl.ds(2 * DH, 2 * NS)),
        (pl.ds(steps, HL), pl.ds(DH + CH, HL)),
    ]
    w_s[DH + CH + HL : CP, mine] = jnp.zeros((LANE - HL, width), bf16)

    def pieces(block):
        return copies([(block.at[src], w_s.at[dst, mine]) for src, dst in places], sems, 0)

    held, given = pieces(w_a), pieces(w_b)

    @pl.when(sec == layer)
    def _():
        for copy in held:
            copy.start()

    @pl.when(sec != layer)
    def _():
        for copy in given:
            copy.start()

    at_x = pl.ds(pl.multiple_of(sec * part, part), part)
    at_y = pl.ds(pl.multiple_of((1 - sec) * part, part), part)
    far = copies([(w_x, w_s.at[at_x, other]), (w_y, w_s.at[at_y, other])], sems, 5)
    for copy in far:
        copy.start()
    return held + far


def column_of(stat_ref, hold_s):
    hold_s[...] = jnp.zeros_like(hold_s)
    hold_s[0:8] = stat_ref[...]
    return jnp.transpose(hold_s[...])


def forward_kernel(layer, *refs):
    (scal, par, hp, w_a, w_b, w_x, w_y, wo_a, wo_b) = refs[:9]
    if layer == 0:
        in_own, in_far = refs[9:11]
        rest = refs[11:]
    else:
        u_prev, p_own, p_far, in_own, in_far = refs[9:14]
        rest = refs[14:]
    (u_out, proj_out, ys_out, st_out, mix_out, sum_out, stat_out) = rest[:7]
    (w_s, wo_s, u_s, n_s, proj_s, conv_s, mask_s, dt_s, rate_s, cs_s, cst_s, xdt_s,
     y_s, mix_s, st_s, pp_s, g_s, spread_s, stat_s, hold_s, in_s, xlo_s, sems) = rest[7:]
    sec, grp, bound = scal[0], scal[1], scal[2]
    count = u_s.shape[0]
    span = count // 2
    piece = count // 2
    place_own = pl.ds(pl.multiple_of(grp * piece, piece), piece)
    place_far = pl.ds(pl.multiple_of((1 - grp) * piece, piece), piece)
    token_target = u_s if layer == 0 else in_s
    token_in = copies(
        [(in_own, token_target.at[place_own]), (in_far, token_target.at[place_far])], sems, 8
    )
    if layer == 0:
        for copy in token_in:
            copy.start()
    else:
        more = copies([(u_prev, u_s), (p_own, pp_s.at[0]), (p_far, pp_s.at[1])], sems, 10)
        for copy in more:
            copy.start()
    w_in = load_weights(layer, sec, grp, w_a, w_b, w_x, w_y, w_s, sems)
    if layer == 1:
        for copy in token_in:
            copy.start()
        wo_in = load_outer(layer, sec, wo_a, wo_b, wo_s, sems.at[4])
    fill_masks(mask_s, bound, count)
    fill_spread(spread_s, HDIM)
    proj_s[0:HEAD_ROWS] = jnp.zeros((HEAD_ROWS, CP), f32)
    gain_in = par[6:7, :DM]
    if layer == 0:
        for copy in token_in:
            copy.wait()
    else:
        for copy in more:
            copy.wait()

    def norm_rows(index):
        rows = tile_at(index, RC)
        values = u_s[rows].astype(f32)
        if layer == 1:
            total = pp_s[0, rows] + pp_s[1, rows]
            pp_s[0, rows] = total
            low = (values + total).astype(bf16)
            u_s[rows] = low
            values = low.astype(f32)
        scale = lax.rsqrt(jnp.mean(values * values, axis=-1, keepdims=True) + EPS)
        n_s[rows] = (values * scale * gain_in).astype(bf16)

    loop(count // RC, norm_rows)
    out_sum = None
    if layer == 1:
        out_sum = pltpu.make_async_copy(pp_s.at[0], sum_out, sems.at[18])
        out_sum.start()
    out_u = pltpu.make_async_copy(u_s, u_out, sems.at[13])
    out_u.start()
    for copy in w_in:
        copy.wait()

    body_rows = slice(HEAD_ROWS, HEAD_ROWS + count)

    def project(index):
        lane = tile_at(index, TILE)
        proj_s[body_rows, lane] = nt(n_s[...], w_s[lane, :])

    loop(CP // TILE, project)
    proj_s[body_rows, CP - LANE : CP] = nt(n_s[...], w_s[CP - LANE : CP, :])
    out_proj = pltpu.make_async_copy(proj_s, proj_out, sems.at[14])
    out_proj.start()

    conv_phase(proj_s, par, mask_s, conv_s, None, count)
    step_phase(proj_s, hp, dt_s, rate_s, cs_s, cst_s, count)
    scaled_inputs(conv_s, dt_s, spread_s, xdt_s, xlo_s, count)

    skip = par[7:8, :DH]
    gain_out = par[5:6, :DH]
    lanes = iota((RC, LANE), 1)

    def mix_rows(index):
        rows = tile_at(index, RC)
        shifted_rows = pl.ds(pl.multiple_of(HEAD_ROWS + index * RC, HEAD_ROWS), RC)
        gate = proj_s[shifted_rows, :DH]
        value = y_s[rows] + skip * conv_s[rows, :DH]
        y_s[rows] = value
        mixed = value * (gate * sigmoid(gate))
        conv_s[rows, :DH] = mixed
        if layer == 1:
            mix_s[rows] = (mixed * gain_out).astype(bf16)
        square = jnp.sum(mixed * mixed, axis=-1, keepdims=True)
        stat_s[rows] = jnp.where(lanes == 0, square, 0.0)

    flushed = []
    for block in range(2):
        rows = slice(block * span, (block + 1) * span)
        low_b = conv_s[rows, DH : DH + NS].astype(bf16)
        low_c = conv_s[rows, DH + NS : CH].astype(bf16)
        g_s[...] = nt3(conv_s[rows, DH + NS : CH], conv_s[rows, DH : DH + NS]) * inside_mask(block, bound, span, False)

        def pair(index):
            lane = tile_at(index, LANE)
            near = xdt_s[rows, lane]
            near_low = xlo_s[rows, lane]
            turned_cs = pltpu.roll(cs_s[rows], lax.rem(LANE - 2 * index, LANE), 1)
            for at in range(0, span, LANE):
                size = at + LANE
                here = slice(block * span + at, block * span + at + LANE)
                mixings = []
                for side in range(2):
                    head = 2 * index + side
                    col = jnp.broadcast_to(turned_cs[at : at + LANE, side : side + 1], (LANE, LANE))
                    line = cst_s[block, pl.ds(head, 1), :][:, :size]
                    wide = jnp.concatenate([col] * (size // LANE), axis=1)
                    decay = jnp.exp(jnp.minimum(wide - line, 0.0))
                    mixings.append(decay * g_s[at : at + LANE, :size])
                y_s[here, lane] = mix_tokens(*mixings, near[:size], near_low[:size])

        loop(HL // 2, pair)
        if block == 0:
            weight = pack3(tail_weight(cs_s, bound, span))
            turned = jnp.transpose(conv_s[rows, DH : DH + NS])

            def state_tile(index):
                lane = tile_at(index, TILE)
                scaled = (xdt_s[rows, lane].astype(f32) + xlo_s[rows, lane].astype(f32)) * nn(weight, spread_s[:, lane])
                st_s[:, lane] = nn3(turned, scaled)

            loop(DH // TILE, state_tile)
        else:
            weight = pack3(carry_weight(cs_s, bound, span))

            def carry_tile(index):
                lane = tile_at(index, TILE)
                carried = nn3(conv_s[rows, DH + NS : CH], st_s[:, lane])
                y_s[rows, lane] += carried * nn(weight, spread_s[:, lane])

            loop(DH // TILE, carry_tile)
        first_tile = block * (span // RC)
        loop(span // RC, lambda index: mix_rows(first_tile + index))
        flushed += copies(
            [
                (y_s.at[rows], ys_out.at[rows]),
                (conv_s.at[rows, pl.ds(0, DH)], mix_out.at[rows]),
            ],
            sems,
            16 if block == 0 else 20,
        )
        for copy in flushed[-2:]:
            copy.start()
    out_st = pltpu.make_async_copy(st_s, st_out, sems.at[15])
    out_st.start()

    if layer == 1:
        wo_in.wait()
        for copy in token_in:
            copy.wait()

        def out_tile(index):
            lane = tile_at(index, TILE)
            partial = nn(mix_s[...], wo_s[:, lane])
            dots = jnp.sum(partial * in_s[:, lane].astype(f32), axis=-1, keepdims=True)
            stat_s[...] += jnp.where(iota((count, LANE), 1) == 1, dots, 0.0)

        loop(DM // TILE, out_tile)
    stat_out[...] = jnp.transpose(stat_s[...])[0:8]
    for copy in (out_u, out_proj, out_st, *flushed):
        copy.wait()
    if layer == 1:
        out_sum.wait()


def backward_kernel(layer, *refs):
    (scal, par, hp, w_a, w_b, w_x, w_y, wo_a, wo_b) = refs[:9]
    (u_in, proj_in, ys_in, st_in, stat_own, stat_far, in_own, in_far) = refs[9:17]
    if layer == 1:
        rest = refs[17:]
    else:
        p_sum, up_in, dn_own, dn_far, par_up = refs[17:22]
        rest = refs[22:]
    (n_out, dp_out, gated_out, g_out, dn_out, small_out) = rest[:6]
    (w_s, wo_s, u_s, n_s, proj_s, conv_s, pre_s, mask_s, dt_s, rate_s, cs_s, cst_s, grad_cs_s, xdt_s,
     y_s, st_s, ad_s, pp_s, dn_s, g_s, up_s, gg_s, dys_s, dx_s, dpre_s, dp_s, gm_s, dg_s,
     spread_s, gather_s, stat_s, hold_s, xlo_s, dlo_s, sems) = rest[6:]
    sec, grp, bound = scal[0], scal[1], scal[2]
    count = u_s.shape[0]
    span = count // 2
    piece = count // 2
    place_own = pl.ds(pl.multiple_of(grp * piece, piece), piece)
    place_far = pl.ds(pl.multiple_of((1 - grp) * piece, piece), piece)
    token_in = copies([(in_own, g_s.at[place_own]), (in_far, g_s.at[place_far])], sems, 8)
    saved_in = copies([(u_in, u_s), (proj_in, proj_s), (ys_in, y_s), (st_in, st_s)], sems, 10)
    for copy in token_in:
        copy.start()
    if layer == 0:
        more = copies(
            [
                (dn_own, dn_s.at[0]),
                (dn_far, dn_s.at[1]),
                (up_in, up_s),
                (p_sum, pp_s),
            ],
            sems,
            14,
        )
        for copy in more:
            copy.start()
    wo_in = load_outer(layer, sec, wo_a, wo_b, wo_s, sems.at[4])
    for copy in saved_in[1:]:
        copy.start()
    fill_masks(mask_s, bound, count)
    fill_spread(spread_s, HDIM)
    fill_gather(gather_s)
    stats = column_of(stat_own, hold_s) + column_of(stat_far, hold_s)
    stat_s[...] = stats
    for copy in token_in:
        copy.wait()
    lane_rc = iota((RC, LANE), 1)
    if layer == 0:
        for copy in more:
            copy.wait()
        gain_up = par_up[6:7, :DM]

        def upstream_rows(index):
            rows = tile_at(index, RC)
            values = up_s[rows].astype(f32)
            scale = lax.rsqrt(jnp.mean(values * values, axis=-1, keepdims=True) + EPS)
            arrived = (dn_s[0, rows].astype(f32) + dn_s[1, rows].astype(f32)) * gain_up
            inner = jnp.mean(arrived * values, axis=-1, keepdims=True)
            total = g_s[rows].astype(f32) + scale * arrived - values * (scale * scale * scale * inner)
            low = total.astype(bf16)
            g_s[rows] = low
            dots = jnp.sum(low.astype(f32) * pp_s[rows], axis=-1, keepdims=True)
            stat_s[rows] = jnp.where(lane_rc == 1, dots, stat_s[rows])

        loop(count // RC, upstream_rows)
    out_g = pltpu.make_async_copy(g_s, g_out, sems.at[19])
    out_g.start()
    wo_in.wait()

    def gated_tile(index):
        lane = tile_at(index, TILE)
        gg_s[:, lane] = nt(g_s[...], wo_s[lane, :])

    loop(DH // TILE, gated_tile)
    for copy in saved_in[1:]:
        copy.wait()
    w_in = load_weights(layer, sec, grp, w_a, w_b, w_x, w_y, w_s, sems)
    saved_in[0].start()

    conv_phase(proj_s, par, mask_s, conv_s, pre_s, count)
    step_phase(proj_s, hp, dt_s, rate_s, cs_s, cst_s, count)
    scaled_inputs(conv_s, dt_s, spread_s, xdt_s, xlo_s, count)

    skip = par[7:8, :DH]
    gain_out = par[5:6, :DH]
    gain_in = par[6:7, :DM]

    def fold(values):
        return jnp.sum(values.reshape(-1, 8, values.shape[-1]), axis=0)

    def mix_rows(index, carry):
        gain_sum, skip_sum = carry
        rows = tile_at(index, RC)
        shifted_rows = pl.ds(pl.multiple_of(HEAD_ROWS + index * RC, HEAD_ROWS), RC)
        scale = lax.rsqrt(stat_s[rows, 0:1] * (1.0 / DI) + EPS)
        inner = stat_s[rows, 1:2] * (scale * scale * (1.0 / DI))
        if layer == 1:
            inner = inner * scale
        gate = proj_s[shifted_rows, :DH]
        gate_sig = sigmoid(gate)
        gate_act = gate * gate_sig
        value = y_s[rows]
        grad = gg_s[rows]
        mixed = value * gate_act
        scaled = mixed * scale
        dmixed = grad * gain_out * scale - mixed * inner
        mixed_low = (scaled * gain_out).astype(bf16)
        gated_s[rows] = mixed_low
        dys = dmixed * gate_act
        dgate = dmixed * value * (gate_sig + gate_act * (1.0 - gate_sig))
        dp_s[rows, :DH] = dgate.astype(bf16)
        inputs = conv_s[rows, :DH]
        gg_s[rows] = dys
        low = dys.astype(bf16)
        dys_s[rows] = low
        dlo_s[rows] = (dys - low.astype(f32)).astype(bf16)
        y_s[rows] = dys * (value - skip * inputs)
        return (gain_sum + fold(grad * scaled), skip_sum + fold(dys * inputs))

    gated_s = n_s
    zero = jnp.zeros((8, DH), f32)
    gain_sum, skip_sum = lax.fori_loop(0, count // RC, mix_rows, (zero, zero))
    small_out[...] = jnp.zeros_like(small_out)
    small_out[5:6, :DH] = jnp.sum(gain_sum, axis=0, keepdims=True)
    small_out[7:8, :DH] = jnp.sum(skip_sum, axis=0, keepdims=True)
    out_gated = pltpu.make_async_copy(n_s, gated_out, sems.at[20])
    out_gated.start()

    lane_left = iota((span, LANE), 1) < HDIM
    for block in (1, 0):
        rows = slice(block * span, (block + 1) * span)
        low_b = conv_s[rows, DH : DH + NS].astype(bf16)
        low_c = conv_s[rows, DH + NS : CH].astype(bf16)
        keep = inside_mask(block, bound, span, True)
        gm_s[...] = nt3(conv_s[rows, DH : DH + NS], conv_s[rows, DH + NS : CH]) * keep
        dg_s[...] = jnp.zeros_like(dg_s)

        def pair(index):
            lane = tile_at(index, LANE)
            near = xdt_s[rows, lane]
            far = dys_s[rows, lane]
            far_low = dlo_s[rows, lane]
            turned_cs = pltpu.roll(cs_s[rows], lax.rem(LANE - 2 * index, LANE), 1)
            for at in range(0, span, LANE):
                size = span - at
                here = slice(block * span + at, block * span + at + LANE)
                part = near[at : at + LANE]
                mixings, decays, parts = [], [], []
                for side in range(2):
                    head = 2 * index + side
                    col = jnp.broadcast_to(turned_cs[at : at + LANE, side : side + 1], (LANE, LANE))
                    line = cst_s[block, pl.ds(head, 1), :][:, at:]
                    wide = jnp.concatenate([col] * (size // LANE), axis=1)
                    decay = jnp.exp(jnp.minimum(line - wide, 0.0))
                    decays.append(decay)
                    mixings.append(decay * gm_s[at : at + LANE, at:])
                    mine = lane_left[:LANE] if side == 0 else jnp.logical_not(lane_left[:LANE])
                    parts.append(jnp.where(mine, part.astype(f32), 0.0).astype(bf16))
                dx_s[here, lane] = mix_tokens(*mixings, far[at:], far_low[at:])
                pairs = nt(jnp.concatenate(parts, axis=0), far[at:])
                dg_s[at : at + LANE, at:] += pairs[:LANE] * decays[0] + pairs[LANE:] * decays[1]

        loop(HL // 2, pair)
        grad_g = dg_s[...] * keep
        dpre_s[rows, DH : DH + NS] = nn(grad_g.astype(bf16), low_c)
        dpre_s[rows, DH + NS : CH] = nn(jnp.transpose(grad_g).astype(bf16), low_b)
        if block == 1:
            weight = pack3(carry_weight(cs_s, bound, span))
            turned_c = jnp.transpose(conv_s[rows, DH + NS : CH])

            def carry_tile(index):
                lane = tile_at(index, TILE)
                scaled = (dys_s[rows, lane].astype(f32) + dlo_s[rows, lane].astype(f32)) * nn(weight, spread_s[:, lane])
                ad_s[:, lane] = nn3(turned_c, scaled)
                dpre_s[rows, DH + NS : CH] += nt3(scaled, st_s[:, lane])

            loop(DH // TILE, carry_tile)
        else:
            weight = pack3(tail_weight(cs_s, bound, span))

            def state_tile(index):
                lane = tile_at(index, TILE)
                scale = nn(weight, spread_s[:, lane])
                low_a = ad_s[:, lane]
                inputs = xdt_s[rows, lane].astype(f32) + xlo_s[rows, lane].astype(f32)
                extra = nn3(conv_s[rows, DH : DH + NS], low_a) * scale
                dx_s[rows, lane] += extra
                both = inputs * scale
                pre_tail = jnp.sum(fold(inputs * extra), axis=0, keepdims=True)
                dpre_s[count : count + 1, lane] = pre_tail
                dpre_s[rows, DH : DH + NS] += nt3(both, low_a)

            loop(DH // TILE, state_tile)

    def head_rows(index):
        chunk = RC * 4
        rows = tile_at(index, chunk)
        steps = dt_s[rows]
        scale = nn(pack3(steps), spread_s[...])
        grad = dx_s[rows]
        sums = head_sums(jnp.concatenate([conv_s[rows, :DH] * grad, y_s[rows]], axis=0), gather_s)
        per_step = sums[:chunk]
        stat_s[rows] = per_step
        grad_cs_s[rows] = sums[chunk:] - steps * per_step
        dpre_s[rows, :DH] = gg_s[rows] * skip + grad * scale

    loop(count // (RC * 4), head_rows)
    tail = jnp.broadcast_to(dpre_s[count : count + 1, :DH], (8, DH))
    tail_heads = head_sums(tail, gather_s)[0:1]
    last = iota((span, LANE), 0) == span - 1
    upper = jnp.where(iota((span, span), 0) <= iota((span, span), 1), 1.0, 0.0).astype(bf16)
    bias_sum = jnp.zeros((1, LANE), f32)
    decay_sum = jnp.zeros((1, LANE), f32)
    for block in range(2):
        rows = slice(block * span, (block + 1) * span)
        raw = proj_s[HEAD_ROWS + block * span : HEAD_ROWS + (block + 1) * span, DH + CH : CP]
        grad_cs = grad_cs_s[rows]
        if block == 0:
            grad_cs = grad_cs + jnp.where(last, tail_heads, 0.0)
        sums = nn(upper, jnp.concatenate(split3(grad_cs), axis=1))
        grad_rate = sums[:, :LANE] + sums[:, LANE : 2 * LANE] + sums[:, 2 * LANE :]
        grad_step = stat_s[rows] - grad_rate * hp[1:2, :]
        lanes = iota((span, LANE), 1)
        grad_raw = jnp.where(lanes < HL, grad_step * sigmoid(raw + hp[0:1, :]), 0.0)
        dp_s[rows, DH + CH : CP] = grad_raw.astype(bf16)
        bias_sum = bias_sum + jnp.sum(grad_raw, axis=0, keepdims=True)
        decay_sum = decay_sum + jnp.sum(grad_rate * rate_s[rows], axis=0, keepdims=True)
    small_out[8:9, :LANE] = bias_sum
    small_out[9:10, :LANE] = decay_sum

    dpre_s[count : count + 8] = jnp.zeros((8, CH), f32)

    def conv_back(index):
        src = pl.ds(pl.multiple_of(DH + index * LANE, LANE), LANE)
        dst = tile_at(index, LANE)
        taps = par[0:8, dst]
        sums = [jnp.zeros((8, LANE), f32) for _ in range(KW + 1)]
        for at in range(0, count, 64):
            pre = pre_s[at : at + 64, dst]
            sig = sigmoid(pre)
            grad = dpre_s[at : at + 64, dst] * (sig + pre * sig * (1.0 - sig))
            dpre_s[at : at + 64, dst] = grad
            sums[4] = sums[4] + fold(grad)
            for lag in range(KW):
                begin = HEAD_ROWS + at - lag
                part = proj_s[begin : begin + 64, src]
                if lag:
                    part = part * mask_s[lag - 1, at : at + 64]
                sums[3 - lag] = sums[3 - lag] + fold(grad * part)
        for at in range(0, count, 64):
            total = taps[3:4] * dpre_s[at : at + 64, dst]
            for lag in range(1, KW):
                begin = at + lag
                part = dpre_s[begin : begin + 64, dst] * mask_s[lag - 1, begin : begin + 64]
                total = total + taps[3 - lag : 4 - lag] * part
            dp_s[at : at + 64, src] = total.astype(bf16)
        for at in range(KW + 1):
            small_out[at : at + 1, dst] = jnp.sum(sums[at], axis=0, keepdims=True)

    loop(CH // LANE, conv_back)
    out_dp = pltpu.make_async_copy(dp_s, dp_out, sems.at[21])
    out_dp.start()
    for copy in w_in:
        copy.wait()
    saved_in[0].wait()

    def normed_tile(index):
        lane = tile_at(index, TILE)
        gg_s[:, lane] = nn(dp_s[...], w_s[:, lane])

    loop(DM // TILE, normed_tile)
    out_gated.wait()

    def norm_rows(index, gain_sum):
        rows = tile_at(index, RC)
        values = u_s[rows].astype(f32)
        scale = lax.rsqrt(jnp.mean(values * values, axis=-1, keepdims=True) + EPS)
        unit = values * scale
        n_s[rows] = (unit * gain_in).astype(bf16)
        grad = gg_s[rows]
        dys_s[rows] = grad.astype(bf16)
        return gain_sum + fold(grad * unit)

    gain_total = lax.fori_loop(0, count // RC, norm_rows, jnp.zeros((8, DM), f32))
    small_out[6:7, :DM] = jnp.sum(gain_total, axis=0, keepdims=True)
    out_n = pltpu.make_async_copy(n_s, n_out, sems.at[22])
    out_dn = pltpu.make_async_copy(dys_s, dn_out, sems.at[23])
    out_n.start()
    out_dn.start()
    for copy in (out_g, out_dp, out_n, out_dn):
        copy.wait()


def project_kernel(layer, scal, par, wo_a, wo_b, stat_own, stat_far, mix_in, p_out, wo_s, low_s, stat_s, hold_s, sems):
    sec = scal[0]
    count = mix_in.shape[0]
    from_a = pltpu.make_async_copy(wo_a, wo_s, sems.at[0])
    from_b = pltpu.make_async_copy(wo_b, wo_s, sems.at[0])

    @pl.when(sec == layer)
    def _():
        from_a.start()

    @pl.when(sec != layer)
    def _():
        from_b.start()

    stats = column_of(stat_own, hold_s) + column_of(stat_far, hold_s)
    stat_s[...] = lax.rsqrt(stats * (1.0 / DI) + EPS)
    gain_out = par[5:6, :DH]

    def rows_of(index):
        rows = tile_at(index, RC)
        low_s[rows] = (mix_in[rows] * stat_s[rows, 0:1] * gain_out).astype(bf16)

    loop(count // RC, rows_of)
    from_a.wait()

    def out_tile(index):
        lane = tile_at(index, TILE)
        p_out[:, lane] = nn(low_s[...], wo_s[:, lane]).astype(p_out.dtype)

    loop(DM // TILE, out_tile)


ANY = pl.BlockSpec(memory_space=pl.ANY)
VM = pl.BlockSpec(memory_space=pltpu.VMEM)
SM = pl.BlockSpec(memory_space=pltpu.SMEM)


def call(kernel, args, specs, outs, out_specs, scratch, name, flops):
    return pl.pallas_call(
        kernel,
        in_specs=specs,
        out_specs=out_specs,
        out_shape=[jax.ShapeDtypeStruct(shape, dtype) for shape, dtype in outs],
        scratch_shapes=scratch,
        compiler_params=pltpu.CompilerParams(vmem_limit_bytes=VMEM_BYTES),
        cost_estimate=pl.CostEstimate(
            flops=flops, bytes_accessed=20_000_000, transcendentals=4_000_000
        ),
        name=name,
    )(*args)


def vm(shape, dtype):
    return pltpu.VMEM(shape, dtype)


def run_forward(layer, scal, par, hp, weights, tokens, saved):
    count = 2 * tokens[0].shape[0]
    span = count // 2
    args = [scal, par, hp, *weights]
    specs = [SM, VM, VM] + [ANY] * 6
    if layer == 1:
        args += saved
        specs += [ANY, ANY, ANY]
    args += tokens
    specs += [ANY, ANY]
    outs = [
        ((count, DM), bf16),
        ((count + HEAD_ROWS, CP), f32),
        ((count, DH), f32),
        ((NS, DH), f32),
        ((count, DH), f32),
        ((count, DM) if layer == 1 else (8, LANE), f32),
        ((8, count), f32),
    ]
    out_specs = [ANY] * 6 + [VM]
    scratch = [
        vm((CP, DM), bf16),
        vm((DH, DM), bf16),
        vm((count, DM), bf16),
        vm((count, DM), bf16),
        vm((count + HEAD_ROWS, CP), f32),
        vm((count, CH), f32),
        vm((KW - 1, count + 8, LANE), f32),
        vm((count, LANE), f32),
        vm((count, LANE), f32),
        vm((count, LANE), f32),
        vm((2, LANE, span), f32),
        vm((count, DH), bf16),
        vm((count, DH), f32),
        vm((count, DH), bf16),
        vm((NS, DH), f32),
        vm((2, count, DM), f32),
        vm((span, span), f32),
        vm((LANE, DH), bf16),
        vm((count, LANE), f32),
        vm((LANE, count), f32),
        vm((count, DM), bf16),
        vm((count, DH), bf16),
        pltpu.SemaphoreType.DMA((22,)),
    ]
    return call(
        functools.partial(forward_kernel, layer),
        args,
        specs,
        outs,
        out_specs,
        scratch,
        "forward_%d" % layer,
        35_000_000_000,
    )


def assemble_kernel(scal, *refs):
    got, own = refs[:3], refs[3:6]
    a1, a1_got, came, came_got, b1, b1_got = refs[6:12]
    in_out, out_out, whole_s, outer_s, in_s, out_s, sems = refs[12:]
    sec, grp = scal[0], scal[1]
    half = whole_s.shape[1] // 2
    quart = whole_s.shape[2] // 2
    outer = outer_s.shape[0] // 2
    share = b1.shape[0]

    def first_pairs(blocks, core):
        near, far, wide = blocks
        pairs = []
        for at, block in ((scal[2], near), (1 - scal[2], far)):
            rows = pl.ds(pl.multiple_of(at * half, 16), half)
            pairs.append((block, whole_s.at[core, rows]))
        return pairs + [(wide.at[pl.ds(0, outer)], outer_s.at[pl.ds(core * outer, outer)])]

    def outer_pairs(early, wide, core):
        return [
            (early, outer_s.at[pl.ds(core * outer, share)]),
            (wide.at[pl.ds(outer, share)], outer_s.at[pl.ds(core * outer + share, share)]),
        ]

    def second_pairs(block, moved, core):
        near = pl.ds(pl.multiple_of(grp * quart, quart), quart)
        far = pl.ds(pl.multiple_of((1 - grp) * quart, quart), quart)
        return [
            (block.at[:, near], whole_s.at[core, :, near]),
            (moved, whole_s.at[core, :, far]),
        ]

    def fetch(pairs):
        started = copies(pairs, sems, 0)
        for copy in started:
            copy.start()
        for copy in started:
            copy.wait()

    @pl.when(sec == 0)
    def _():
        fetch(first_pairs(own, 0) + first_pairs(got, 1))

    @pl.when(sec != 0)
    def _():
        fetch(
            second_pairs(a1, came, 1)
            + second_pairs(a1_got, came_got, 0)
            + outer_pairs(b1, own[2], 1)
            + outer_pairs(b1_got, got[2], 0)
        )

    width = in_s.shape[1]
    quarter = width // 2
    step = 64
    started = []

    def send(piece, sem):
        copy = pltpu.make_async_copy(in_s.at[piece], in_out.at[piece], sems.at[sem])
        copy.start()
        started.append(copy)

    def emit(target, source, count, side):
        def body(index):
            at = pl.multiple_of(index * step, step)
            for core in range(2):
                value = whole_s[core, pl.ds(source + at, step), side * quarter : (side + 1) * quarter]
                lane = slice(core * quarter, (core + 1) * quarter)
                in_s[pl.ds(target + at, step), lane] = value.astype(f32)

        loop(count // step, body)

    for at, (target, source, side) in enumerate(
        ((0, 0, 0), (DH, 0, 1), (DI, DH, 0), (DI + DH, DH, 1))
    ):
        emit(target, source, DH, side)
        send(pl.ds(target, DH), 8 + at)
    for core in range(2):
        lane = slice(core * quarter, (core + 1) * quarter)
        left, right = slice(0, quarter), slice(quarter, width)
        shared = slice(2 * DH, 2 * DH + 2 * NS)
        in_s[2 * DI : 2 * DI + 2 * NS, lane] = whole_s[core, shared, left].astype(f32) + whole_s[
            core, shared, right
        ].astype(f32)
        steps = slice(DH + CH, DH + CH + HL)
        in_s[DI + CONVC : DI + CONVC + HL, lane] = whole_s[core, steps, left].astype(f32)
        in_s[DI + CONVC + HL :, lane] = whole_s[core, steps, right].astype(f32)
    send(pl.ds(2 * DI, 2 * NS + HEADS), 12)

    def body(index):
        rows = tile_at(index, step)
        out_s[rows] = outer_s[rows].astype(f32)

    loop(out_s.shape[0] // step, body)
    copy = pltpu.make_async_copy(out_s, out_out, sems.at[13])
    copy.start()
    started.append(copy)
    for copy in started:
        copy.wait()


def run_assemble(scal, got, own, second, columns):
    rows, width = second[0].shape
    outer = (4 * second[-1].shape[0], second[-1].shape[1])
    return call(
        assemble_kernel,
        [scal, *got, *own, *second],
        [SM] + [ANY] * 12,
        [((columns, width), f32), (outer, f32)],
        [ANY, ANY],
        [
            vm((2, rows, width), bf16),
            vm(outer, bf16),
            vm((columns, width), f32),
            vm(outer, f32),
            pltpu.SemaphoreType.DMA((14,)),
        ],
        "assemble",
        6_000_000_000,
    )


def run_project(layer, scal, par, wo_a, wo_b, stat_own, stat_far, mixed):
    count = mixed.shape[0]
    return call(
        functools.partial(project_kernel, layer),
        [scal, par, wo_a, wo_b, stat_own, stat_far, mixed],
        [SM, VM, ANY, ANY, VM, VM, VM],
        [((count, DM), f32)],
        [VM],
        [
            vm((DH, DM), bf16),
            vm((count, DH), bf16),
            vm((count, LANE), f32),
            vm((LANE, count), f32),
            pltpu.SemaphoreType.DMA((1,)),
        ],
        "project_%d" % layer,
        6_000_000_000,
    )[0]


def run_backward(layer, scal, par, hp, weights, saved, tokens, late):
    count = 2 * tokens[0].shape[0]
    span = count // 2
    args = [scal, par, hp, *weights, *saved, *tokens]
    specs = [SM, VM, VM] + [ANY] * 6 + [ANY] * 4 + [VM, VM] + [ANY] * 2
    if layer == 0:
        args += late
        specs += [ANY] * 4 + [VM]
    outs = [
        ((count, DM), bf16),
        ((count, CP), bf16),
        ((count, DH), bf16),
        ((count, DM), bf16),
        ((count, DM), bf16),
        ((16, CH), f32),
    ]
    out_specs = [ANY] * 5 + [VM]
    scratch = [
        vm((CP, DM), bf16),
        vm((DH, DM), bf16),
        vm((count, DM), bf16),
        vm((count, DM), bf16),
        vm((count + HEAD_ROWS, CP), f32),
        vm((count, CH), f32),
        vm((count, CH), f32),
        vm((KW - 1, count + 8, LANE), f32),
        vm((count, LANE), f32),
        vm((count, LANE), f32),
        vm((count, LANE), f32),
        vm((2, LANE, span), f32),
        vm((count, LANE), f32),
        vm((count, DH), bf16),
        vm((count, DH), f32),
        vm((NS, DH), f32),
        vm((NS, DH), f32),
        vm((count, DM), f32),
        vm((2, count, DM), bf16),
        vm((count, DM), bf16),
        vm((count, DM), bf16),
        vm((count, DM), f32),
        vm((count, DM), bf16),
        vm((count, DH), f32),
        vm((count + 8, CH), f32),
        vm((count, CP), bf16),
        vm((span, span), f32),
        vm((span, span), f32),
        vm((LANE, DH), bf16),
        vm((DH, LANE), bf16),
        vm((count, LANE), f32),
        vm((LANE, count), f32),
        vm((count, DH), bf16),
        vm((count, DH), bf16),
        pltpu.SemaphoreType.DMA((24,)),
    ]
    return call(
        functools.partial(backward_kernel, layer),
        args,
        specs,
        outs,
        out_specs,
        scratch,
        "backward_%d" % layer,
        55_000_000_000,
    )


def swap(block, axis):
    return lax.ppermute(block, axis, [(0, 1), (1, 0)])


def flip(block, mask):
    size = lax.axis_size("replica")
    return lax.ppermute(block, "replica", [(at, at ^ mask) for at in range(size)])


def add_low(left, right):
    return (left.astype(f32) + right.astype(f32)).astype(bf16)


def halves(block, which):
    size = block.shape[0] // 2
    keep = lax.dynamic_slice_in_dim(block, which * size, size, 0)
    send = lax.dynamic_slice_in_dim(block, (1 - which) * size, size, 0)
    return keep, send


def stages_of(bits):
    return [(at,) for at in range(bits)]


def scatter_sum(pieces, stages, rep):
    for (bit,) in stages:
        cut = [halves(piece, (rep >> bit) & 1) for piece in pieces]
        sent = flip(sum_low([send for keep, send in cut]), 1 << bit)
        pieces = [sum_low([keep for keep, send in cut]), sent]
    return sum_low(pieces)


def sum_low(pieces):
    total = pieces[0].astype(f32)
    for piece in pieces[1:]:
        total = total + piece.astype(f32)
    return total.astype(bf16)


def collect(block, stage, rep):
    pieces = [block] + [flip(block, away << stage[0]) for away in range(1, 1 << len(stage))]
    for level in range(len(stage)):
        which = (rep >> stage[level]) & 1
        pieces = [
            in_order(pieces[at], pieces[at + 1], which, 0) for at in range(0, len(pieces), 2)
        ]
    return pieces[0]


def in_order(mine, other, which, dim):
    return jnp.where(
        which == 0,
        jnp.concatenate([mine, other], axis=dim),
        jnp.concatenate([other, mine], axis=dim),
    )


def gather_back(block, order, rep):
    for bit in reversed(order):
        block = in_order(block, flip(block, bit), (rep >> bit) & 1, 0)
    return block


def on_device(
    first_layer_input,
    boundary,
    input_gain,
    in_proj,
    conv_weight,
    conv_bias,
    head_params,
    output_gain,
    out_proj,
    cotangent,
):
    sec = lax.axis_index("section")
    grp = lax.axis_index("group")
    rep = lax.axis_index("replica")
    replicas = lax.axis_size("replica")
    bits = replicas.bit_length() - 1
    order_a = stages_of(bits)
    order_b = order_a[1::-1] + order_a[2:]

    bound = lax.dynamic_index_in_dim(boundary[:, 0], sec, 0, keepdims=False)
    scal = jnp.stack([sec, grp, bound]).astype(jnp.int32)
    u_own = lax.dynamic_index_in_dim(first_layer_input[:, 0], sec, 0, keepdims=False)
    u_far = swap(u_own, "group")
    cot_own = lax.dynamic_index_in_dim(cotangent[:, 0], sec, 0, keepdims=False)

    block = jnp.swapaxes(in_proj, 1, 2)[0]
    far_grp = 1 - grp
    other = jnp.concatenate(
        [
            lax.dynamic_slice_in_dim(block, far_grp * DH, DH, 0),
            lax.dynamic_slice_in_dim(block, DI + far_grp * DH, DH, 0),
            block[2 * DI : 2 * DI + 2 * NS],
            lax.dynamic_slice_in_dim(block, DI + CONVC + far_grp * HL, HL, 0),
            jnp.zeros((LANE - HL, block.shape[1]), bf16),
        ],
        axis=0,
    )
    keep, give = halves(other, sec)
    got = swap(give, "section")
    first_x = swap(jnp.where(sec == 0, keep, got), "group")
    keep, got, cot_own, first_x = lax.optimization_barrier((keep, got, cot_own, first_x))
    second_x = swap(jnp.where(sec == 1, keep, got), "group")
    cot_far = swap(cot_own, "group")
    w_a, w_b = block, swap(block, "section")
    wo_a = out_proj[0]
    wo_b = swap(wo_a, "section")
    weights = [
        (w_a, w_b, w_x, swap(w_x, "section"), wo_a, wo_b) for w_x in (first_x, second_x)
    ]

    width = conv_bias.shape[1]
    half_in = input_gain.shape[1]

    def row_of(*pieces):
        line = jnp.concatenate(pieces)
        return jnp.pad(line, (0, width - line.shape[0]))[None]

    smalls = jnp.concatenate(
        [
            conv_weight[0].T,
            conv_bias,
            row_of(output_gain[0]),
            row_of(input_gain[0], head_params[0].T.reshape(-1)),
            jnp.zeros((1, width), bf16),
        ],
        axis=0,
    )
    both = in_order(smalls[None], swap(smalls, "section")[None], sec, 0)
    far_both = swap(both, "group")
    both = both.astype(f32)
    full = in_order(both, far_both.astype(f32), grp, 2)
    pars, hps = [], []
    for layer in range(2):
        taps = jnp.concatenate(
            [
                lax.dynamic_slice_in_dim(full[layer, 0:5], grp * DH, DH, 1),
                full[layer, 0:5, DI:],
            ],
            axis=1,
        )
        line = both[layer, 6]
        heads = line[half_in : half_in + 3 * HL].reshape(3, HL)
        gain_in = jnp.concatenate(
            [full[layer, 6, :half_in], full[layer, 6, width : width + half_in]]
        )
        rest = jnp.stack([both[layer, 5, :DH], gain_in, jnp.repeat(heads[2], HDIM)])
        pars.append(jnp.concatenate([taps, jnp.pad(rest, ((0, 0), (0, CH - DH)))], axis=0))
        lines = jnp.stack([heads[0], jnp.exp(heads[1]), heads[2]])
        hps.append(jnp.pad(lines, ((0, 5), (0, LANE - HL))))

    tokens = [u_own, u_far]
    cots = [cot_own, cot_far]
    quarter = half_in // 2

    def own_quarter(normed):
        return jnp.concatenate(
            [
                lax.dynamic_slice_in_dim(normed, at * half_in + sec * quarter, quarter, 1)
                for at in range(2)
            ],
            axis=1,
        )

    def own_channels(gated):
        return lax.dynamic_slice_in_dim(gated, sec * (DH // 2), DH // 2, 1)

    def join_in(normed, dproj):
        far_n, far_p = swap(normed, "section"), swap(dproj, "section")
        return (tn(dproj, own_quarter(normed)) + tn(far_p, own_quarter(far_n))).astype(bf16)

    def join_out(gated, upstream):
        far_g, far_u = swap(gated, "section"), swap(upstream, "section")
        return (tn(own_channels(gated), upstream) + tn(own_channels(far_g), far_u)).astype(bf16)

    def guarded(branch, operand):
        shapes = jax.eval_shape(branch, operand)

        def nothing(operand):
            return jax.tree.map(lambda leaf: jnp.zeros(leaf.shape, leaf.dtype), shapes)

        return lax.cond(bound >= 0, branch, nothing, operand)

    u0, proj0, ys0, st0, mix0, unused_sum, stat0 = guarded(
        lambda tokens: run_forward(0, scal, pars[0], hps[0], weights[0], tokens, None), tokens
    )
    stat0, cot_far = lax.optimization_barrier((stat0, cots[1]))
    cots = [cot_own, cot_far]
    stat0_far = swap(stat0, "group")
    p0 = run_project(0, scal, pars[0], wo_a, wo_b, stat0, stat0_far, mix0)
    p0_far = swap(p0.astype(jnp.float16), "group").astype(f32)
    u1, proj1, ys1, st1, mix1, p_total, stat1 = run_forward(
        1, scal, pars[1], hps[1], weights[1], cots, [u0, p0, p0_far]
    )
    stat1_far = swap(stat1, "group")
    piece = u_own.shape[0]

    def own_rows(block):
        return lax.dynamic_slice_in_dim(block, grp * piece, piece, 0)

    def far_rows(block):
        return lax.dynamic_slice_in_dim(block, (1 - grp) * piece, piece, 0)

    scale1 = lax.rsqrt((stat1 + stat1_far)[0] * (1.0 / DI) + EPS)[:, None]
    gated1 = (mix1 * scale1 * pars[1][5:6, :DH]).astype(bf16)
    b1 = join_out(gated1, in_order(cot_own, cot_far, grp, 0))
    stat1_far, b1 = lax.optimization_barrier((stat1_far, b1))
    share = b1.shape[0] // 2
    b1_late = b1[share:]
    b1 = lax.psum(b1[:share], "replica")

    def second_layer(stat1_far):
        n1, dp1, unused_gated, unused_g, dn1, small1 = run_backward(
            1, scal, pars[1], hps[1], weights[1],
            [u1, proj1, ys1, st1, stat1, stat1_far], cots, None,
        )
        dn1_far = swap(dn1, "group")
        dn1_far, a1 = lax.optimization_barrier((dn1_far, join_in(n1, dp1)))
        return dn1, dn1_far, a1, small1

    dn1, dn1_far, a1, small1 = guarded(second_layer, stat1_far)
    a1, b1 = lax.optimization_barrier((a1, b1))
    a1 = lax.psum(a1, "replica")

    def to_sections(first, second):
        held = jnp.where(sec == 0, first, second)
        given = swap(jnp.where(sec == 0, second, first), "section")
        return in_order(held[None], given[None], sec, 0)

    def swap_rows(part_a):
        stay = lax.dynamic_slice_in_dim(part_a, grp * quarter, quarter, 1)
        leave = lax.dynamic_slice_in_dim(part_a, far_grp * quarter, quarter, 1)
        return in_order(stay, swap(leave, "group"), grp, 1)

    def to_owner(block, layer):
        return lax.ppermute(block, "section", [(1 - layer, layer)])

    def gather_back(block, stages):
        for stage in reversed(stages):
            block = collect(block, stage, rep)
        return block

    def first_layer(dn1_far):
        n0, dp0, gated0, g0, dn0, small0 = run_backward(
            0, scal, pars[0], hps[0], weights[0],
            [u0, proj0, ys0, st0, stat0, stat0_far], cots,
            [p_total, u1, dn1, dn1_far, pars[1]],
        )
        a0 = join_in(n0, dp0)
        b0 = jnp.concatenate([join_out(gated0, g0), b1_late], axis=0)
        cut = [halves(block, (rep >> stages[0][0]) & 1) for block, stages in ((a0, order_a), (b0, order_b))]
        cut, dn0, g0, small0, late_gated, late_small = lax.optimization_barrier(
            (cut, dn0, g0, small0, gated1, small1)
        )
        sent = [
            flip(send, 1 << stages[0][0])
            for (keep, send), stages in zip(cut, (order_a, order_b))
        ]
        dn0_far = swap(far_rows(dn0), "group")

        p1 = nn(late_gated, jnp.where(sec == 1, wo_a, wo_b))
        p1_far = swap(far_rows(p1).astype(bf16), "group")
        small = jnp.stack([small0, late_small])
        small = small + swap(small, "section")
        far = swap(small, "group")
        shared = small + far
        own_x = jnp.concatenate([small[:, 0:5, :DH], far[:, 0:5, :LANE]], axis=2)
        own_y = jnp.concatenate([small[:, 0:5, LANE:DH], shared[:, 0:5, DH:]], axis=2)
        conv_part = jnp.where(grp == 0, own_x, own_y)
        gain_in = lax.dynamic_slice_in_dim(shared[:, 6, :DM], grp * half_in, half_in, 1)
        skip = small[:, 7, :DH].reshape(2, HL, HDIM).sum(axis=2)
        line = jnp.concatenate([gain_in, small[:, 8, :HL], small[:, 9, :HL], skip], axis=1)
        packed = jnp.concatenate(
            [
                conv_part,
                jnp.pad(small[:, 5:6, :DH], ((0, 0), (0, 0), (0, width - DH))),
                jnp.pad(line, ((0, 0), (0, width - line.shape[1])))[:, None],
                jnp.zeros((2, 1, width), f32),
            ],
            axis=1,
        )
        sent, dn0_far, p1_far, packed = lax.optimization_barrier((sent, dn0_far, p1_far, packed))
        state = [[keep, came] for (keep, send), came in zip(cut, sent)]
        values = u_own.astype(f32)
        scale = lax.rsqrt(jnp.mean(values * values, axis=-1, keepdims=True) + EPS)
        arrived = (own_rows(dn0).astype(f32) + dn0_far.astype(f32)) * pars[0][6:7, :DM]
        inner = jnp.mean(arrived * values, axis=-1, keepdims=True)
        grad1 = own_rows(g0)
        grad0 = (
            grad1.astype(f32) + scale * arrived - values * (scale * scale * scale * inner)
        ).astype(bf16)

        input_grad = to_sections(grad0, grad1)
        out0 = own_rows(u1)
        out1 = (out0.astype(f32) + own_rows(p1) + p1_far.astype(f32)).astype(bf16)
        segment_output = to_sections(out0, out1)
        for at in range(1, bits):
            cut = [
                [halves(piece, (rep >> stages[at][0]) & 1) for piece in pieces]
                for pieces, stages in zip(state, (order_a, order_b))
            ]
            sent = [
                flip(sum_low([send for keep, send in pair]), 1 << stages[at][0])
                for pair, stages in zip(cut, (order_a, order_b))
            ]
            far_packed = flip(packed, 1 << at)
            state = [
                [sum_low([keep for keep, send in pair]), came] for pair, came in zip(cut, sent)
            ]
            state, far_packed = lax.optimization_barrier((state, far_packed))
            packed = packed + far_packed
        a0, b0 = sum_low(state[0]), sum_low(state[1])
        far_packed = flip(packed, 1)
        a0 = swap_rows(a0)
        a0, far_packed = lax.optimization_barrier((a0, far_packed))
        packed = packed + far_packed
        a0, b0 = gather_back(a0, order_a[1:]), gather_back(b0, order_b[1:])
        packed = jnp.where(sec == 0, packed[0], packed[1])
        heads = packed[6, half_in : half_in + 3 * HL].reshape(3, HL)
        smalls = (packed[6:7, :half_in], packed[0:4], packed[4:5], heads, packed[5:6, :DH])
        return segment_output, input_grad, smalls, a0, b0

    segment_output, input_grad, smalls, a0, b0 = guarded(first_layer, dn1_far)
    a0_far = flip(a0, 1 << order_a[0][0])
    b0 = collect(b0, order_b[0], rep)
    came = swap(lax.dynamic_slice_in_dim(a1, far_grp * quarter, quarter, 1), "group")
    side = (rep >> order_a[0][0]) & 1
    grad_in_proj, grad_out_proj = run_assemble(
        jnp.stack([sec, grp, side]).astype(jnp.int32),
        [to_owner(a0, 0), to_owner(a0_far, 0), swap(b0, "section")],
        [a0, a0_far, b0],
        [a1, to_owner(a1, 1), came, to_owner(came, 1), b1, to_owner(b1, 1)],
        in_proj.shape[2],
    )
    grad_in_proj = jnp.swapaxes(grad_in_proj, 0, 1)
    return (
        segment_output[None, :, None],
        input_grad[None, :, None],
        smalls[0],
        grad_in_proj[None],
        smalls[1].T[None],
        smalls[2],
        smalls[3].T[None],
        smalls[4],
        grad_out_proj[None],
    )


def solution(mesh):
    placed = (
        P(None, "replica", "group", None),
        P(None, "replica"),
        P("section", "group"),
        P("section", "group", None),
        P("section", "group", None),
        P("section", "group"),
        P("section", "group", None),
        P("section", "group"),
        P("section", "group", None),
        P(None, "replica", "group", None),
    )
    return jax.shard_map(
        on_device,
        mesh=mesh,
        in_specs=placed,
        out_specs=(
            P("section", None, "replica", "group", None),
            P("section", None, "replica", "group", None),
            P("section", "group"),
            P("section", "group", None),
            P("section", "group", None),
            P("section", "group"),
            P("section", "group", None),
            P("section", "group"),
            P("section", "group", None),
        ),
        check_vma=False,
    )
```

```python
import functools

import jax
import jax.numpy as jnp
from jax import lax
from jax.experimental import pallas as pl
from jax.experimental.pallas import tpu as pltpu
from jax.sharding import PartitionSpec as P

DM = 1024
HEADS = 32
HDIM = 64
NS = 128
KW = 4
DI = 2048
CONVC = 2304
HL = HEADS // 2
DH = DI // 2
CH = DH + 2 * NS
CP = DH + CH + 128
LANE = 128
TILE = 256
RC = 32
HEAD_ROWS = 8
EPS = 1e-05
VMEM_BYTES = 63 * 1024 * 1024

f32 = jnp.float32
bf16 = jnp.bfloat16


def nn(left, right):
    return jnp.dot(left, right, preferred_element_type=f32)


def nt(left, right):
    return lax.dot_general(left, right, (((1,), (1,)), ((), ())), preferred_element_type=f32)


def tn(left, right):
    return lax.dot_general(left, right, (((0,), (0,)), ((), ())), preferred_element_type=f32)


def tile_at(index, size):
    return pl.ds(pl.multiple_of(index * size, size), size)


def loop(count, body):
    def step(index, carry):
        body(index)
        return carry

    lax.fori_loop(0, count, step, 0)


def iota(shape, dim):
    return lax.broadcasted_iota(jnp.int32, shape, dim)


def sigmoid(values):
    return 0.5 * jnp.tanh(0.5 * values) + 0.5


def softplus(values):
    small = jnp.exp(-jnp.abs(values))
    series = small * (1.0 - small * (0.5 - small * (1.0 / 3.0 - small * 0.25)))
    return jnp.maximum(values, 0.0) + jnp.where(small < 0.03, series, jnp.log(1.0 + small))


def split3(values):
    high = values.astype(bf16)
    rest = values - high.astype(f32)
    middle = rest.astype(bf16)
    low = (rest - middle.astype(f32)).astype(bf16)
    return high, middle, low


def pack3(values):
    high, middle, low = split3(values)
    packed = (
        high.astype(f32)
        + pltpu.roll(middle.astype(f32), HL, 1)
        + pltpu.roll(low.astype(f32), 2 * HL, 1)
    )
    return packed.astype(bf16)


def fill_spread(spread_s, width):
    shape = spread_s.shape
    row = iota(shape, 0)
    col = iota(shape, 1)
    hit = (row < 3 * HL) & ((row & (HL - 1)) == col // width)
    spread_s[...] = jnp.where(hit, 1.0, 0.0).astype(bf16)


def fill_gather(gather_s):
    shape = gather_s.shape
    hit = iota(shape, 0) // HDIM == iota(shape, 1)
    gather_s[...] = jnp.where(hit, 1.0, 0.0).astype(bf16)


def head_sums(values, gather_s):
    high = values.astype(bf16)
    low = (values - high.astype(f32)).astype(bf16)
    rows = values.shape[0]
    both = nn(jnp.concatenate([high, low], axis=0), gather_s[...])
    return both[:rows] + both[rows:]


def fill_masks(mask_s, bound, count):
    rows = mask_s.shape[1]
    pos = iota((rows, LANE), 0)
    for lag in range(1, KW):
        anchor = pos - lag
        dropped = (anchor < 0) | ((anchor < bound) & (bound <= pos)) | (pos >= count)
        mask_s[lag - 1] = jnp.where(dropped, 0.0, 1.0)


def conv_phase(proj_s, par, mask_s, conv_s, pre_s, count):
    def body(index):
        src = pl.ds(pl.multiple_of(DH + index * LANE, LANE), LANE)
        dst = tile_at(index, LANE)
        taps = par[0:8, dst]
        for at in range(0, count, 64):
            pre = taps[4:5] + taps[3:4] * proj_s[HEAD_ROWS + at : HEAD_ROWS + at + 64, src]
            for lag in range(1, KW):
                begin = HEAD_ROWS + at - lag
                part = proj_s[begin : begin + 64, src] * mask_s[lag - 1, at : at + 64]
                pre = pre + taps[3 - lag : 4 - lag] * part
            if pre_s is not None:
                pre_s[at : at + 64, dst] = pre
            conv_s[at : at + 64, dst] = pre * sigmoid(pre)

    loop(CH // LANE, body)


def step_phase(proj_s, hp, dt_s, rate_s, cs_s, cst_s, count):
    span = count // 2
    lanes = iota((count, LANE), 1)
    raw = proj_s[HEAD_ROWS : HEAD_ROWS + count, DH + CH : CP] + hp[0:1, :]
    step = jnp.where(lanes < HL, softplus(raw), 0.0)
    rate = -step * hp[1:2, :]
    dt_s[...] = step
    rate_s[...] = rate
    lower = jnp.where(iota((span, span), 0) >= iota((span, span), 1), 1.0, 0.0).astype(bf16)
    for block in range(2):
        rows = slice(block * span, (block + 1) * span)
        triple = jnp.concatenate(split3(rate[rows]), axis=1)
        sums = nn(lower, triple)
        total = sums[:, :LANE] + sums[:, LANE : 2 * LANE] + sums[:, 2 * LANE :]
        cs_s[rows] = total
        cst_s[block] = jnp.transpose(total)


def scaled_inputs(conv_s, dt_s, spread_s, xdt_s, xlo_s, count):
    def body(index):
        rows = tile_at(index, RC * 4)
        scale = nn(pack3(dt_s[rows]), spread_s[...])
        v = conv_s[rows, :DH] * scale
        xdt_s[rows] = v.astype(bf16)
        xlo_s[rows] = (v - v.astype(bf16).astype(f32)).astype(bf16)

    loop(count // (RC * 4), body)


def tail_weight(cs_s, bound, span):
    total = cs_s[0:span]
    pos = iota((span, LANE), 0)
    cut = (pos < bound) & (bound <= span - 1)
    lanes = iota((span, LANE), 1)
    keep = jnp.logical_not(cut) & (lanes < HL)
    return jnp.where(keep, jnp.exp(total[span - 1 : span] - total), 0.0)


def carry_weight(cs_s, bound, span):
    total = cs_s[span : 2 * span]
    pos = iota((span, LANE), 0) + span
    fresh = (span <= bound) & (bound <= pos)
    lanes = iota((span, LANE), 1)
    keep = jnp.logical_not(fresh) & (lanes < HL)
    return jnp.where(keep, jnp.exp(total), 0.0)


def inside_mask(block, bound, span, flipped):
    shape = (span, span)
    later = iota(shape, 1 if flipped else 0) + block * span
    early = iota(shape, 0 if flipped else 1) + block * span
    keep = (later >= early) & jnp.logical_not((early < bound) & (bound <= later))
    return jnp.where(keep, 1.0, 0.0)


def split2(values):
    high = values.astype(bf16)
    return high, (values - high.astype(f32)).astype(bf16)


def nt3(left, right):
    left_high, left_low = split2(left)
    right_high, right_low = split2(right)
    return nt(
        jnp.concatenate([left_high, left_low, left_high], axis=1),
        jnp.concatenate([right_high, right_high, right_low], axis=1),
    )


def nn3(left, right):
    left_high, left_low = split2(left)
    right_high, right_low = split2(right)
    return nn(
        jnp.concatenate([left_high, left_low, left_high], axis=1),
        jnp.concatenate([right_high, right_high, right_low], axis=0),
    )


def mix_tokens(first, second, high, low):
    rows = first.shape[0]
    first_high, first_low = split2(first)
    second_high, second_low = split2(second)
    stacked = jnp.concatenate([first_high, second_high, first_low, second_low], axis=0)
    both = nn(stacked, jnp.concatenate([high, low], axis=1))
    left, right = both[:, :LANE], both[:, LANE:]
    total = left[: 2 * rows] + right[: 2 * rows] + left[2 * rows :]
    keep = iota((rows, LANE), 1) < HDIM
    return jnp.where(keep, total[:rows], total[rows:])


def copies(pairs, sems, base):
    return [
        pltpu.make_async_copy(src, dst, sems.at[base + at]) for at, (src, dst) in enumerate(pairs)
    ]


def load_outer(layer, sec, wo_a, wo_b, wo_s, sem):
    held = pltpu.make_async_copy(wo_a, wo_s, sem)
    given = pltpu.make_async_copy(wo_b, wo_s, sem)

    @pl.when(sec == layer)
    def _():
        held.start()

    @pl.when(sec != layer)
    def _():
        given.start()

    return held


def load_weights(layer, sec, grp, w_a, w_b, w_x, w_y, w_s, sems):
    width = w_a.shape[1]
    mine = pl.ds(pl.multiple_of(grp * width, width), width)
    other = pl.ds(pl.multiple_of((1 - grp) * width, width), width)
    first = pl.multiple_of(grp * DH, DH)
    steps = pl.multiple_of(DI + CONVC + grp * HL, HL)
    places = [
        (pl.ds(first, DH), pl.ds(0, DH)),
        (pl.ds(DI + first, DH), pl.ds(DH, DH)),
        (pl.ds(2 * DI, 2 * NS), pl.ds(2 * DH, 2 * NS)),
        (pl.ds(steps, HL), pl.ds(DH + CH, HL)),
    ]
    w_s[DH + CH + HL : CP] = jnp.zeros((LANE - HL, 2 * width), bf16)

    def pieces(block):
        return copies([(block.at[src], w_s.at[dst, mine]) for src, dst in places], sems, 0)

    held, given = pieces(w_a), pieces(w_b)

    @pl.when(sec == layer)
    def _():
        for copy in held:
            copy.start()

    @pl.when(sec != layer)
    def _():
        for copy in given:
            copy.start()

    pairs = []
    for part, which in ((w_x, sec), (w_y, 1 - sec)):
        wide = pl.ds(pl.multiple_of(which * DH, DH), DH)
        thin = pl.ds(pl.multiple_of(2 * DH + which * NS, NS), NS)
        pairs.append((part.at[pl.ds(0, DH)], w_s.at[wide, other]))
        pairs.append((part.at[pl.ds(DH, NS)], w_s.at[thin, other]))
    pairs.append((w_x.at[pl.ds(DH + NS, HL)], w_s.at[pl.ds(DH + CH, HL), other]))
    far = copies(pairs, sems, 24)
    for copy in far:
        copy.start()
    return held + far


def column_of(stat_ref, hold_s):
    hold_s[...] = jnp.zeros_like(hold_s)
    hold_s[0:8] = stat_ref[...]
    return jnp.transpose(hold_s[...])


def forward_kernel(layer, *refs):
    (scal, par, hp, w_a, w_b, w_x, w_y, wo_a, wo_b) = refs[:9]
    if layer == 0:
        in_own, in_far = refs[9:11]
        rest = refs[11:]
    else:
        u_prev, p_own, p_far, in_own, in_far = refs[9:14]
        rest = refs[14:]
    (u_out, proj_out, ys_out, st_out, mix_out, sum_out, stat_out) = rest[:7]
    (w_s, wo_s, u_s, n_s, proj_s, conv_s, mask_s, dt_s, rate_s, cs_s, cst_s, xdt_s,
     y_s, mix_s, st_s, pp_s, g_s, spread_s, stat_s, hold_s, in_s, xlo_s, sems) = rest[7:]
    sec, grp, bound = scal[0], scal[1], scal[2]
    count = u_s.shape[0]
    span = count // 2
    piece = count // 2
    place_own = pl.ds(pl.multiple_of(grp * piece, piece), piece)
    place_far = pl.ds(pl.multiple_of((1 - grp) * piece, piece), piece)
    token_target = u_s if layer == 0 else in_s
    token_in = copies(
        [(in_own, token_target.at[place_own]), (in_far, token_target.at[place_far])], sems, 8
    )
    if layer == 0:
        for copy in token_in:
            copy.start()
    else:
        more = copies([(u_prev, u_s), (p_own, pp_s.at[0]), (p_far, pp_s.at[1])], sems, 10)
        for copy in more:
            copy.start()
    w_in = load_weights(layer, sec, grp, w_a, w_b, w_x, w_y, w_s, sems)
    if layer == 1:
        for copy in token_in:
            copy.start()
        wo_in = load_outer(layer, sec, wo_a, wo_b, wo_s, sems.at[4])
    fill_masks(mask_s, bound, count)
    fill_spread(spread_s, HDIM)
    proj_s[0:HEAD_ROWS] = jnp.zeros((HEAD_ROWS, CP), f32)
    gain_in = par[6:7, :DM]
    if layer == 0:
        for copy in token_in:
            copy.wait()
    else:
        for copy in more:
            copy.wait()

    def norm_rows(index):
        rows = tile_at(index, RC)
        values = u_s[rows].astype(f32)
        if layer == 1:
            total = pp_s[0, rows] + pp_s[1, rows]
            pp_s[0, rows] = total
            low = (values + total).astype(bf16)
            u_s[rows] = low
            values = low.astype(f32)
        scale = lax.rsqrt(jnp.mean(values * values, axis=-1, keepdims=True) + EPS)
        n_s[rows] = (values * scale * gain_in).astype(bf16)

    loop(count // RC, norm_rows)
    out_sum = None
    if layer == 1:
        out_sum = pltpu.make_async_copy(pp_s.at[0], sum_out, sems.at[18])
        out_sum.start()
    out_u = pltpu.make_async_copy(u_s, u_out, sems.at[13])
    out_u.start()
    for copy in w_in:
        copy.wait()

    body_rows = slice(HEAD_ROWS, HEAD_ROWS + count)

    def project(index):
        lane = tile_at(index, TILE)
        proj_s[body_rows, lane] = nt(n_s[...], w_s[lane, :])

    loop(CP // TILE, project)
    proj_s[body_rows, CP - LANE : CP] = nt(n_s[...], w_s[CP - LANE : CP, :])
    out_proj = pltpu.make_async_copy(proj_s, proj_out, sems.at[14])
    out_proj.start()

    conv_phase(proj_s, par, mask_s, conv_s, None, count)
    step_phase(proj_s, hp, dt_s, rate_s, cs_s, cst_s, count)
    scaled_inputs(conv_s, dt_s, spread_s, xdt_s, xlo_s, count)

    skip = par[7:8, :DH]
    gain_out = par[5:6, :DH]
    lanes = iota((RC, LANE), 1)

    def mix_rows(index):
        rows = tile_at(index, RC)
        shifted_rows = pl.ds(pl.multiple_of(HEAD_ROWS + index * RC, HEAD_ROWS), RC)
        gate = proj_s[shifted_rows, :DH]
        value = y_s[rows] + skip * conv_s[rows, :DH]
        y_s[rows] = value
        mixed = value * (gate * sigmoid(gate))
        conv_s[rows, :DH] = mixed
        if layer == 1:
            mix_s[rows] = (mixed * gain_out).astype(bf16)
        square = jnp.sum(mixed * mixed, axis=-1, keepdims=True)
        stat_s[rows] = jnp.where(lanes == 0, square, 0.0)

    flushed = []
    for block in range(2):
        rows = slice(block * span, (block + 1) * span)
        low_b = conv_s[rows, DH : DH + NS].astype(bf16)
        low_c = conv_s[rows, DH + NS : CH].astype(bf16)
        g_s[...] = nt3(conv_s[rows, DH + NS : CH], conv_s[rows, DH : DH + NS]) * inside_mask(block, bound, span, False)

        def pair(index):
            lane = tile_at(index, LANE)
            near = xdt_s[rows, lane]
            near_low = xlo_s[rows, lane]
            turned_cs = pltpu.roll(cs_s[rows], lax.rem(LANE - 2 * index, LANE), 1)
            for at in range(0, span, LANE):
                size = at + LANE
                here = slice(block * span + at, block * span + at + LANE)
                mixings = []
                for side in range(2):
                    head = 2 * index + side
                    col = jnp.broadcast_to(turned_cs[at : at + LANE, side : side + 1], (LANE, LANE))
                    line = cst_s[block, pl.ds(head, 1), :][:, :size]
                    wide = jnp.concatenate([col] * (size // LANE), axis=1)
                    decay = jnp.exp(jnp.minimum(wide - line, 0.0))
                    mixings.append(decay * g_s[at : at + LANE, :size])
                y_s[here, lane] = mix_tokens(*mixings, near[:size], near_low[:size])

        loop(HL // 2, pair)
        if block == 0:
            weight = pack3(tail_weight(cs_s, bound, span))
            turned = jnp.transpose(conv_s[rows, DH : DH + NS])

            def state_tile(index):
                lane = tile_at(index, TILE)
                scaled = (xdt_s[rows, lane].astype(f32) + xlo_s[rows, lane].astype(f32)) * nn(weight, spread_s[:, lane])
                st_s[:, lane] = nn3(turned, scaled)

            loop(DH // TILE, state_tile)
        else:
            weight = pack3(carry_weight(cs_s, bound, span))

            def carry_tile(index):
                lane = tile_at(index, TILE)
                carried = nn3(conv_s[rows, DH + NS : CH], st_s[:, lane])
                y_s[rows, lane] += carried * nn(weight, spread_s[:, lane])

            loop(DH // TILE, carry_tile)
        first_tile = block * (span // RC)
        loop(span // RC, lambda index: mix_rows(first_tile + index))
        flushed += copies(
            [
                (y_s.at[rows], ys_out.at[rows]),
                (conv_s.at[rows, pl.ds(0, DH)], mix_out.at[rows]),
            ],
            sems,
            16 if block == 0 else 20,
        )
        for copy in flushed[-2:]:
            copy.start()
    out_st = pltpu.make_async_copy(st_s, st_out, sems.at[15])
    out_st.start()

    if layer == 1:
        wo_in.wait()
        for copy in token_in:
            copy.wait()

        def out_tile(index):
            lane = tile_at(index, TILE)
            partial = nn(mix_s[...], wo_s[:, lane])
            dots = jnp.sum(partial * in_s[:, lane].astype(f32), axis=-1, keepdims=True)
            stat_s[...] += jnp.where(iota((count, LANE), 1) == 1, dots, 0.0)

        loop(DM // TILE, out_tile)
    stat_out[...] = jnp.transpose(stat_s[...])[0:8]
    for copy in (out_u, out_proj, out_st, *flushed):
        copy.wait()
    if layer == 1:
        out_sum.wait()


def backward_kernel(layer, *refs):
    (scal, par, hp, w_a, w_b, w_x, w_y, wo_a, wo_b) = refs[:9]
    (u_in, proj_in, ys_in, st_in, stat_own, stat_far, in_own, in_far) = refs[9:17]
    if layer == 1:
        rest = refs[17:]
    else:
        p_sum, up_in, dn_own, dn_far, par_up = refs[17:22]
        rest = refs[22:]
    (n_out, dp_out, gated_out, g_out, dn_out, small_out) = rest[:6]
    (w_s, wo_s, u_s, n_s, proj_s, conv_s, pre_s, mask_s, dt_s, rate_s, cs_s, cst_s, grad_cs_s, xdt_s,
     y_s, st_s, ad_s, pp_s, dn_s, g_s, up_s, gg_s, dys_s, dx_s, dpre_s, dp_s, gm_s, dg_s,
     spread_s, gather_s, stat_s, hold_s, xlo_s, dlo_s, sems) = rest[6:]
    sec, grp, bound = scal[0], scal[1], scal[2]
    count = u_s.shape[0]
    span = count // 2
    piece = count // 2
    place_own = pl.ds(pl.multiple_of(grp * piece, piece), piece)
    place_far = pl.ds(pl.multiple_of((1 - grp) * piece, piece), piece)
    token_in = copies([(in_own, g_s.at[place_own]), (in_far, g_s.at[place_far])], sems, 8)
    saved_in = copies([(u_in, u_s), (proj_in, proj_s), (ys_in, y_s), (st_in, st_s)], sems, 10)
    for copy in token_in:
        copy.start()
    if layer == 0:
        more = copies(
            [
                (dn_own, dn_s.at[0]),
                (dn_far, dn_s.at[1]),
                (up_in, up_s),
                (p_sum, pp_s),
            ],
            sems,
            14,
        )
        for copy in more:
            copy.start()
    wo_in = load_outer(layer, sec, wo_a, wo_b, wo_s, sems.at[4])
    for copy in saved_in[1:]:
        copy.start()
    fill_masks(mask_s, bound, count)
    fill_spread(spread_s, HDIM)
    fill_gather(gather_s)
    stats = column_of(stat_own, hold_s) + column_of(stat_far, hold_s)
    stat_s[...] = stats
    for copy in token_in:
        copy.wait()
    lane_rc = iota((RC, LANE), 1)
    if layer == 0:
        for copy in more:
            copy.wait()
        gain_up = par_up[6:7, :DM]

        def upstream_rows(index):
            rows = tile_at(index, RC)
            values = up_s[rows].astype(f32)
            scale = lax.rsqrt(jnp.mean(values * values, axis=-1, keepdims=True) + EPS)
            arrived = (dn_s[0, rows].astype(f32) + dn_s[1, rows].astype(f32)) * gain_up
            inner = jnp.mean(arrived * values, axis=-1, keepdims=True)
            total = g_s[rows].astype(f32) + scale * arrived - values * (scale * scale * scale * inner)
            low = total.astype(bf16)
            g_s[rows] = low
            dots = jnp.sum(low.astype(f32) * pp_s[rows], axis=-1, keepdims=True)
            stat_s[rows] = jnp.where(lane_rc == 1, dots, stat_s[rows])

        loop(count // RC, upstream_rows)
    out_g = pltpu.make_async_copy(g_s, g_out, sems.at[19])
    out_g.start()
    wo_in.wait()

    def gated_tile(index):
        lane = tile_at(index, TILE)
        gg_s[:, lane] = nt(g_s[...], wo_s[lane, :])

    loop(DH // TILE, gated_tile)
    for copy in saved_in[1:]:
        copy.wait()
    w_in = load_weights(layer, sec, grp, w_a, w_b, w_x, w_y, w_s, sems)
    saved_in[0].start()

    conv_phase(proj_s, par, mask_s, conv_s, pre_s, count)
    step_phase(proj_s, hp, dt_s, rate_s, cs_s, cst_s, count)
    scaled_inputs(conv_s, dt_s, spread_s, xdt_s, xlo_s, count)

    skip = par[7:8, :DH]
    gain_out = par[5:6, :DH]
    gain_in = par[6:7, :DM]

    def fold(values):
        return jnp.sum(values.reshape(-1, 8, values.shape[-1]), axis=0)

    def mix_rows(index, carry):
        gain_sum, skip_sum = carry
        rows = tile_at(index, RC)
        shifted_rows = pl.ds(pl.multiple_of(HEAD_ROWS + index * RC, HEAD_ROWS), RC)
        scale = lax.rsqrt(stat_s[rows, 0:1] * (1.0 / DI) + EPS)
        inner = stat_s[rows, 1:2] * (scale * scale * (1.0 / DI))
        if layer == 1:
            inner = inner * scale
        gate = proj_s[shifted_rows, :DH]
        gate_sig = sigmoid(gate)
        gate_act = gate * gate_sig
        value = y_s[rows]
        grad = gg_s[rows]
        mixed = value * gate_act
        scaled = mixed * scale
        dmixed = grad * gain_out * scale - mixed * inner
        mixed_low = (scaled * gain_out).astype(bf16)
        gated_s[rows] = mixed_low
        dys = dmixed * gate_act
        dgate = dmixed * value * (gate_sig + gate_act * (1.0 - gate_sig))
        dp_s[rows, :DH] = dgate.astype(bf16)
        inputs = conv_s[rows, :DH]
        gg_s[rows] = dys
        low = dys.astype(bf16)
        dys_s[rows] = low
        dlo_s[rows] = (dys - low.astype(f32)).astype(bf16)
        y_s[rows] = dys * (value - skip * inputs)
        return (gain_sum + fold(grad * scaled), skip_sum + fold(dys * inputs))

    gated_s = n_s
    zero = jnp.zeros((8, DH), f32)
    gain_sum, skip_sum = lax.fori_loop(0, count // RC, mix_rows, (zero, zero))
    small_out[...] = jnp.zeros_like(small_out)
    small_out[5:6, :DH] = jnp.sum(gain_sum, axis=0, keepdims=True)
    small_out[7:8, :DH] = jnp.sum(skip_sum, axis=0, keepdims=True)
    out_gated = pltpu.make_async_copy(n_s, gated_out, sems.at[20])
    out_gated.start()

    lane_left = iota((span, LANE), 1) < HDIM
    for block in (1, 0):
        rows = slice(block * span, (block + 1) * span)
        low_b = conv_s[rows, DH : DH + NS].astype(bf16)
        low_c = conv_s[rows, DH + NS : CH].astype(bf16)
        keep = inside_mask(block, bound, span, True)
        gm_s[...] = nt3(conv_s[rows, DH : DH + NS], conv_s[rows, DH + NS : CH]) * keep
        dg_s[...] = jnp.zeros_like(dg_s)

        def pair(index):
            lane = tile_at(index, LANE)
            near = xdt_s[rows, lane]
            far = dys_s[rows, lane]
            far_low = dlo_s[rows, lane]
            turned_cs = pltpu.roll(cs_s[rows], lax.rem(LANE - 2 * index, LANE), 1)
            for at in range(0, span, LANE):
                size = span - at
                here = slice(block * span + at, block * span + at + LANE)
                part = near[at : at + LANE]
                mixings, decays, parts = [], [], []
                for side in range(2):
                    head = 2 * index + side
                    col = jnp.broadcast_to(turned_cs[at : at + LANE, side : side + 1], (LANE, LANE))
                    line = cst_s[block, pl.ds(head, 1), :][:, at:]
                    wide = jnp.concatenate([col] * (size // LANE), axis=1)
                    decay = jnp.exp(jnp.minimum(line - wide, 0.0))
                    decays.append(decay)
                    mixings.append(decay * gm_s[at : at + LANE, at:])
                    mine = lane_left[:LANE] if side == 0 else jnp.logical_not(lane_left[:LANE])
                    parts.append(jnp.where(mine, part.astype(f32), 0.0).astype(bf16))
                dx_s[here, lane] = mix_tokens(*mixings, far[at:], far_low[at:])
                pairs = nt(jnp.concatenate(parts, axis=0), far[at:])
                dg_s[at : at + LANE, at:] += pairs[:LANE] * decays[0] + pairs[LANE:] * decays[1]

        loop(HL // 2, pair)
        grad_g = dg_s[...] * keep
        dpre_s[rows, DH : DH + NS] = nn(grad_g.astype(bf16), low_c)
        dpre_s[rows, DH + NS : CH] = nn(jnp.transpose(grad_g).astype(bf16), low_b)
        if block == 1:
            weight = pack3(carry_weight(cs_s, bound, span))
            turned_c = jnp.transpose(conv_s[rows, DH + NS : CH])

            def carry_tile(index):
                lane = tile_at(index, TILE)
                scaled = (dys_s[rows, lane].astype(f32) + dlo_s[rows, lane].astype(f32)) * nn(weight, spread_s[:, lane])
                ad_s[:, lane] = nn3(turned_c, scaled)
                dpre_s[rows, DH + NS : CH] += nt3(scaled, st_s[:, lane])

            loop(DH // TILE, carry_tile)
        else:
            weight = pack3(tail_weight(cs_s, bound, span))

            def state_tile(index):
                lane = tile_at(index, TILE)
                scale = nn(weight, spread_s[:, lane])
                low_a = ad_s[:, lane]
                inputs = xdt_s[rows, lane].astype(f32) + xlo_s[rows, lane].astype(f32)
                extra = nn3(conv_s[rows, DH : DH + NS], low_a) * scale
                dx_s[rows, lane] += extra
                both = inputs * scale
                pre_tail = jnp.sum(fold(inputs * extra), axis=0, keepdims=True)
                dpre_s[count : count + 1, lane] = pre_tail
                dpre_s[rows, DH : DH + NS] += nt3(both, low_a)

            loop(DH // TILE, state_tile)

    def head_rows(index):
        chunk = RC * 4
        rows = tile_at(index, chunk)
        steps = dt_s[rows]
        scale = nn(pack3(steps), spread_s[...])
        grad = dx_s[rows]
        sums = head_sums(jnp.concatenate([conv_s[rows, :DH] * grad, y_s[rows]], axis=0), gather_s)
        per_step = sums[:chunk]
        stat_s[rows] = per_step
        grad_cs_s[rows] = sums[chunk:] - steps * per_step
        dpre_s[rows, :DH] = gg_s[rows] * skip + grad * scale

    loop(count // (RC * 4), head_rows)
    tail = jnp.broadcast_to(dpre_s[count : count + 1, :DH], (8, DH))
    tail_heads = head_sums(tail, gather_s)[0:1]
    last = iota((span, LANE), 0) == span - 1
    upper = jnp.where(iota((span, span), 0) <= iota((span, span), 1), 1.0, 0.0).astype(bf16)
    bias_sum = jnp.zeros((1, LANE), f32)
    decay_sum = jnp.zeros((1, LANE), f32)
    for block in range(2):
        rows = slice(block * span, (block + 1) * span)
        raw = proj_s[HEAD_ROWS + block * span : HEAD_ROWS + (block + 1) * span, DH + CH : CP]
        grad_cs = grad_cs_s[rows]
        if block == 0:
            grad_cs = grad_cs + jnp.where(last, tail_heads, 0.0)
        sums = nn(upper, jnp.concatenate(split3(grad_cs), axis=1))
        grad_rate = sums[:, :LANE] + sums[:, LANE : 2 * LANE] + sums[:, 2 * LANE :]
        grad_step = stat_s[rows] - grad_rate * hp[1:2, :]
        lanes = iota((span, LANE), 1)
        grad_raw = jnp.where(lanes < HL, grad_step * sigmoid(raw + hp[0:1, :]), 0.0)
        dp_s[rows, DH + CH : CP] = grad_raw.astype(bf16)
        bias_sum = bias_sum + jnp.sum(grad_raw, axis=0, keepdims=True)
        decay_sum = decay_sum + jnp.sum(grad_rate * rate_s[rows], axis=0, keepdims=True)
    small_out[8:9, :LANE] = bias_sum
    small_out[9:10, :LANE] = decay_sum

    dpre_s[count : count + 8] = jnp.zeros((8, CH), f32)

    def conv_back(index):
        src = pl.ds(pl.multiple_of(DH + index * LANE, LANE), LANE)
        dst = tile_at(index, LANE)
        taps = par[0:8, dst]
        sums = [jnp.zeros((8, LANE), f32) for _ in range(KW + 1)]
        for at in range(0, count, 64):
            pre = pre_s[at : at + 64, dst]
            sig = sigmoid(pre)
            grad = dpre_s[at : at + 64, dst] * (sig + pre * sig * (1.0 - sig))
            dpre_s[at : at + 64, dst] = grad
            sums[4] = sums[4] + fold(grad)
            for lag in range(KW):
                begin = HEAD_ROWS + at - lag
                part = proj_s[begin : begin + 64, src]
                if lag:
                    part = part * mask_s[lag - 1, at : at + 64]
                sums[3 - lag] = sums[3 - lag] + fold(grad * part)
        for at in range(0, count, 64):
            total = taps[3:4] * dpre_s[at : at + 64, dst]
            for lag in range(1, KW):
                begin = at + lag
                part = dpre_s[begin : begin + 64, dst] * mask_s[lag - 1, begin : begin + 64]
                total = total + taps[3 - lag : 4 - lag] * part
            dp_s[at : at + 64, src] = total.astype(bf16)
        for at in range(KW + 1):
            small_out[at : at + 1, dst] = jnp.sum(sums[at], axis=0, keepdims=True)

    loop(CH // LANE, conv_back)
    out_dp = pltpu.make_async_copy(dp_s, dp_out, sems.at[21])
    out_dp.start()
    for copy in w_in:
        copy.wait()
    saved_in[0].wait()

    def normed_tile(index):
        lane = tile_at(index, TILE)
        gg_s[:, lane] = nn(dp_s[...], w_s[:, lane])

    loop(DM // TILE, normed_tile)
    out_gated.wait()

    def norm_rows(index, gain_sum):
        rows = tile_at(index, RC)
        values = u_s[rows].astype(f32)
        scale = lax.rsqrt(jnp.mean(values * values, axis=-1, keepdims=True) + EPS)
        unit = values * scale
        n_s[rows] = (unit * gain_in).astype(bf16)
        grad = gg_s[rows]
        dys_s[rows] = grad.astype(bf16)
        return gain_sum + fold(grad * unit)

    gain_total = lax.fori_loop(0, count // RC, norm_rows, jnp.zeros((8, DM), f32))
    small_out[6:7, :DM] = jnp.sum(gain_total, axis=0, keepdims=True)
    out_n = pltpu.make_async_copy(n_s, n_out, sems.at[22])
    out_dn = pltpu.make_async_copy(dys_s, dn_out, sems.at[23])
    out_n.start()
    out_dn.start()
    for copy in (out_g, out_dp, out_n, out_dn):
        copy.wait()


def project_kernel(layer, scal, par, wo_a, wo_b, stat_own, stat_far, mix_in, p_out, wo_s, low_s, stat_s, hold_s, sems):
    sec = scal[0]
    count = mix_in.shape[0]
    from_a = pltpu.make_async_copy(wo_a, wo_s, sems.at[0])
    from_b = pltpu.make_async_copy(wo_b, wo_s, sems.at[0])

    @pl.when(sec == layer)
    def _():
        from_a.start()

    @pl.when(sec != layer)
    def _():
        from_b.start()

    stats = column_of(stat_own, hold_s) + column_of(stat_far, hold_s)
    stat_s[...] = lax.rsqrt(stats * (1.0 / DI) + EPS)
    gain_out = par[5:6, :DH]

    def rows_of(index):
        rows = tile_at(index, RC)
        low_s[rows] = (mix_in[rows] * stat_s[rows, 0:1] * gain_out).astype(bf16)

    loop(count // RC, rows_of)
    from_a.wait()

    def out_tile(index):
        lane = tile_at(index, TILE)
        p_out[:, lane] = nn(low_s[...], wo_s[:, lane]).astype(p_out.dtype)

    loop(DM // TILE, out_tile)


ANY = pl.BlockSpec(memory_space=pl.ANY)
VM = pl.BlockSpec(memory_space=pltpu.VMEM)
SM = pl.BlockSpec(memory_space=pltpu.SMEM)


def call(kernel, args, specs, outs, out_specs, scratch, name, flops):
    return pl.pallas_call(
        kernel,
        in_specs=specs,
        out_specs=out_specs,
        out_shape=[jax.ShapeDtypeStruct(shape, dtype) for shape, dtype in outs],
        scratch_shapes=scratch,
        compiler_params=pltpu.CompilerParams(vmem_limit_bytes=VMEM_BYTES),
        cost_estimate=pl.CostEstimate(
            flops=flops, bytes_accessed=20_000_000, transcendentals=4_000_000
        ),
        name=name,
    )(*args)


def vm(shape, dtype):
    return pltpu.VMEM(shape, dtype)


def run_forward(layer, scal, par, hp, weights, tokens, saved):
    count = 2 * tokens[0].shape[0]
    span = count // 2
    args = [scal, par, hp, *weights]
    specs = [SM, VM, VM] + [ANY] * 6
    if layer == 1:
        args += saved
        specs += [ANY, ANY, ANY]
    args += tokens
    specs += [ANY, ANY]
    outs = [
        ((count, DM), bf16),
        ((count + HEAD_ROWS, CP), f32),
        ((count, DH), f32),
        ((NS, DH), f32),
        ((count, DH), f32),
        ((count, DM) if layer == 1 else (8, LANE), f32),
        ((8, count), f32),
    ]
    out_specs = [ANY] * 6 + [VM]
    scratch = [
        vm((CP, DM), bf16),
        vm((DH, DM), bf16),
        vm((count, DM), bf16),
        vm((count, DM), bf16),
        vm((count + HEAD_ROWS, CP), f32),
        vm((count, CH), f32),
        vm((KW - 1, count + 8, LANE), f32),
        vm((count, LANE), f32),
        vm((count, LANE), f32),
        vm((count, LANE), f32),
        vm((2, LANE, span), f32),
        vm((count, DH), bf16),
        vm((count, DH), f32),
        vm((count, DH), bf16),
        vm((NS, DH), f32),
        vm((2, count, DM), f32),
        vm((span, span), f32),
        vm((LANE, DH), bf16),
        vm((count, LANE), f32),
        vm((LANE, count), f32),
        vm((count, DM), bf16),
        vm((count, DH), bf16),
        pltpu.SemaphoreType.DMA((29,)),
    ]
    return call(
        functools.partial(forward_kernel, layer),
        args,
        specs,
        outs,
        out_specs,
        scratch,
        "forward_%d" % layer,
        35_000_000_000,
    )


def assemble_kernel(scal, *refs):
    got, own = refs[:3], refs[3:6]
    a1, a1_got, came, came_got, b1, b1_got = refs[6:12]
    in_out, out_out, whole_s, outer_s, in_s, out_s, sems = refs[12:]
    sec, grp = scal[0], scal[1]
    half = whole_s.shape[1] // 2
    quart = whole_s.shape[2] // 2
    outer = outer_s.shape[0] // 2
    share = b1.shape[0]

    def first_pairs(blocks, core):
        near, far, wide = blocks
        pairs = []
        for at, block in ((scal[2], near), (1 - scal[2], far)):
            rows = pl.ds(pl.multiple_of(at * half, 16), half)
            pairs.append((block, whole_s.at[core, rows]))
        return pairs + [(wide.at[pl.ds(0, outer)], outer_s.at[pl.ds(core * outer, outer)])]

    def outer_pairs(early, wide, core):
        return [
            (early, outer_s.at[pl.ds(core * outer, share)]),
            (wide.at[pl.ds(outer, share)], outer_s.at[pl.ds(core * outer + share, share)]),
        ]

    def second_pairs(block, moved, core):
        near = pl.ds(pl.multiple_of(grp * quart, quart), quart)
        far = pl.ds(pl.multiple_of((1 - grp) * quart, quart), quart)
        return [
            (block.at[:, near], whole_s.at[core, :, near]),
            (moved, whole_s.at[core, :, far]),
        ]

    def fetch(pairs):
        started = copies(pairs, sems, 0)
        for copy in started:
            copy.start()
        for copy in started:
            copy.wait()

    @pl.when(sec == 0)
    def _():
        fetch(first_pairs(own, 0) + first_pairs(got, 1))

    @pl.when(sec != 0)
    def _():
        fetch(
            second_pairs(a1, came, 1)
            + second_pairs(a1_got, came_got, 0)
            + outer_pairs(b1, own[2], 1)
            + outer_pairs(b1_got, got[2], 0)
        )

    width = in_s.shape[1]
    quarter = width // 2
    step = 64
    started = []

    def send(piece, sem):
        copy = pltpu.make_async_copy(in_s.at[piece], in_out.at[piece], sems.at[sem])
        copy.start()
        started.append(copy)

    def emit(target, source, count, side):
        def body(index):
            at = pl.multiple_of(index * step, step)
            for core in range(2):
                value = whole_s[core, pl.ds(source + at, step), side * quarter : (side + 1) * quarter]
                lane = slice(core * quarter, (core + 1) * quarter)
                in_s[pl.ds(target + at, step), lane] = value.astype(f32)

        loop(count // step, body)

    for at, (target, source, side) in enumerate(
        ((0, 0, 0), (DH, 0, 1), (DI, DH, 0), (DI + DH, DH, 1))
    ):
        emit(target, source, DH, side)
        send(pl.ds(target, DH), 8 + at)
    for core in range(2):
        lane = slice(core * quarter, (core + 1) * quarter)
        left, right = slice(0, quarter), slice(quarter, width)
        shared = slice(2 * DH, 2 * DH + 2 * NS)
        in_s[2 * DI : 2 * DI + 2 * NS, lane] = whole_s[core, shared, left].astype(f32) + whole_s[
            core, shared, right
        ].astype(f32)
        steps = slice(DH + CH, DH + CH + HL)
        in_s[DI + CONVC : DI + CONVC + HL, lane] = whole_s[core, steps, left].astype(f32)
        in_s[DI + CONVC + HL :, lane] = whole_s[core, steps, right].astype(f32)
    send(pl.ds(2 * DI, 2 * NS + HEADS), 12)

    def body(index):
        rows = tile_at(index, step)
        out_s[rows] = outer_s[rows].astype(f32)

    loop(out_s.shape[0] // step, body)
    copy = pltpu.make_async_copy(out_s, out_out, sems.at[13])
    copy.start()
    started.append(copy)
    for copy in started:
        copy.wait()


def run_assemble(scal, got, own, second, columns):
    rows, width = second[0].shape
    outer = (4 * second[-1].shape[0], second[-1].shape[1])
    return call(
        assemble_kernel,
        [scal, *got, *own, *second],
        [SM] + [ANY] * 12,
        [((columns, width), f32), (outer, f32)],
        [ANY, ANY],
        [
            vm((2, rows, width), bf16),
            vm(outer, bf16),
            vm((columns, width), f32),
            vm(outer, f32),
            pltpu.SemaphoreType.DMA((14,)),
        ],
        "assemble",
        6_000_000_000,
    )


def run_project(layer, scal, par, wo_a, wo_b, stat_own, stat_far, mixed):
    count = mixed.shape[0]
    return call(
        functools.partial(project_kernel, layer),
        [scal, par, wo_a, wo_b, stat_own, stat_far, mixed],
        [SM, VM, ANY, ANY, VM, VM, VM],
        [((count, DM), f32)],
        [VM],
        [
            vm((DH, DM), bf16),
            vm((count, DH), bf16),
            vm((count, LANE), f32),
            vm((LANE, count), f32),
            pltpu.SemaphoreType.DMA((1,)),
        ],
        "project_%d" % layer,
        6_000_000_000,
    )[0]


def run_backward(layer, scal, par, hp, weights, saved, tokens, late):
    count = 2 * tokens[0].shape[0]
    span = count // 2
    args = [scal, par, hp, *weights, *saved, *tokens]
    specs = [SM, VM, VM] + [ANY] * 6 + [ANY] * 4 + [VM, VM] + [ANY] * 2
    if layer == 0:
        args += late
        specs += [ANY] * 4 + [VM]
    outs = [
        ((count, DM), bf16),
        ((count, CP), bf16),
        ((count, DH), bf16),
        ((count, DM), bf16),
        ((count, DM), bf16),
        ((16, CH), f32),
    ]
    out_specs = [ANY] * 5 + [VM]
    scratch = [
        vm((CP, DM), bf16),
        vm((DH, DM), bf16),
        vm((count, DM), bf16),
        vm((count, DM), bf16),
        vm((count + HEAD_ROWS, CP), f32),
        vm((count, CH), f32),
        vm((count, CH), f32),
        vm((KW - 1, count + 8, LANE), f32),
        vm((count, LANE), f32),
        vm((count, LANE), f32),
        vm((count, LANE), f32),
        vm((2, LANE, span), f32),
        vm((count, LANE), f32),
        vm((count, DH), bf16),
        vm((count, DH), f32),
        vm((NS, DH), f32),
        vm((NS, DH), f32),
        vm((count, DM), f32),
        vm((2, count, DM), bf16),
        vm((count, DM), bf16),
        vm((count, DM), bf16),
        vm((count, DM), f32),
        vm((count, DM), bf16),
        vm((count, DH), f32),
        vm((count + 8, CH), f32),
        vm((count, CP), bf16),
        vm((span, span), f32),
        vm((span, span), f32),
        vm((LANE, DH), bf16),
        vm((DH, LANE), bf16),
        vm((count, LANE), f32),
        vm((LANE, count), f32),
        vm((count, DH), bf16),
        vm((count, DH), bf16),
        pltpu.SemaphoreType.DMA((29,)),
    ]
    return call(
        functools.partial(backward_kernel, layer),
        args,
        specs,
        outs,
        out_specs,
        scratch,
        "backward_%d" % layer,
        55_000_000_000,
    )


def swap(block, axis):
    return lax.ppermute(block, axis, [(0, 1), (1, 0)])


def flip(block, mask):
    size = lax.axis_size("replica")
    return lax.ppermute(block, "replica", [(at, at ^ mask) for at in range(size)])


def add_low(left, right):
    return (left.astype(f32) + right.astype(f32)).astype(bf16)


def halves(block, which):
    size = block.shape[0] // 2
    keep = lax.dynamic_slice_in_dim(block, which * size, size, 0)
    send = lax.dynamic_slice_in_dim(block, (1 - which) * size, size, 0)
    return keep, send


def stages_of(bits):
    return [(at,) for at in range(bits)]


def scatter_sum(pieces, stages, rep):
    for (bit,) in stages:
        cut = [halves(piece, (rep >> bit) & 1) for piece in pieces]
        sent = flip(sum_low([send for keep, send in cut]), 1 << bit)
        pieces = [sum_low([keep for keep, send in cut]), sent]
    return sum_low(pieces)


def sum_low(pieces):
    total = pieces[0].astype(f32)
    for piece in pieces[1:]:
        total = total + piece.astype(f32)
    return total.astype(bf16)


def collect(block, stage, rep):
    pieces = [block] + [flip(block, away << stage[0]) for away in range(1, 1 << len(stage))]
    for level in range(len(stage)):
        which = (rep >> stage[level]) & 1
        pieces = [
            in_order(pieces[at], pieces[at + 1], which, 0) for at in range(0, len(pieces), 2)
        ]
    return pieces[0]


def in_order(mine, other, which, dim):
    return jnp.where(
        which == 0,
        jnp.concatenate([mine, other], axis=dim),
        jnp.concatenate([other, mine], axis=dim),
    )


def gather_back(block, order, rep):
    for bit in reversed(order):
        block = in_order(block, flip(block, bit), (rep >> bit) & 1, 0)
    return block


def on_device(
    first_layer_input,
    boundary,
    input_gain,
    in_proj,
    conv_weight,
    conv_bias,
    head_params,
    output_gain,
    out_proj,
    cotangent,
):
    sec = lax.axis_index("section")
    grp = lax.axis_index("group")
    rep = lax.axis_index("replica")
    replicas = lax.axis_size("replica")
    bits = replicas.bit_length() - 1
    order_a = stages_of(bits)
    order_b = order_a[1::-1] + order_a[2:]

    bound = lax.dynamic_index_in_dim(boundary[:, 0], sec, 0, keepdims=False)
    scal = jnp.stack([sec, grp, bound]).astype(jnp.int32)
    u_own = lax.dynamic_index_in_dim(first_layer_input[:, 0], sec, 0, keepdims=False)
    u_far = swap(u_own, "group")
    cot_own = lax.dynamic_index_in_dim(cotangent[:, 0], sec, 0, keepdims=False)

    block = jnp.swapaxes(in_proj, 1, 2)[0]
    far_grp = 1 - grp

    def far_part(which):
        return jnp.concatenate(
            [
                lax.dynamic_slice_in_dim(block, which * DI + far_grp * DH, DH, 0),
                lax.dynamic_slice_in_dim(block, 2 * DI + which * NS, NS, 0),
                lax.dynamic_slice_in_dim(block, DI + CONVC + far_grp * HL, HL, 0),
            ],
            axis=0,
        )

    keep, give = far_part(sec), far_part(1 - sec)
    got = swap(give, "section")
    first_x = swap(jnp.where(sec == 0, keep, got), "group")
    keep, got, cot_own, first_x = lax.optimization_barrier((keep, got, cot_own, first_x))
    second_x = swap(jnp.where(sec == 1, keep, got), "group")
    cot_far = swap(cot_own, "group")
    w_a, w_b = block, swap(block, "section")
    wo_a = out_proj[0]
    wo_b = swap(wo_a, "section")
    weights = [
        (w_a, w_b, w_x, swap(w_x, "section"), wo_a, wo_b) for w_x in (first_x, second_x)
    ]

    width = conv_bias.shape[1]
    half_in = input_gain.shape[1]

    def row_of(*pieces):
        line = jnp.concatenate(pieces)
        return jnp.pad(line, (0, width - line.shape[0]))[None]

    smalls = jnp.concatenate(
        [
            conv_weight[0].T,
            conv_bias,
            row_of(output_gain[0]),
            row_of(input_gain[0], head_params[0].T.reshape(-1)),
            jnp.zeros((1, width), bf16),
        ],
        axis=0,
    )
    both = in_order(smalls[None], swap(smalls, "section")[None], sec, 0)
    far_both = swap(both, "group")
    both = both.astype(f32)
    full = in_order(both, far_both.astype(f32), grp, 2)
    pars, hps = [], []
    for layer in range(2):
        taps = jnp.concatenate(
            [
                lax.dynamic_slice_in_dim(full[layer, 0:5], grp * DH, DH, 1),
                full[layer, 0:5, DI:],
            ],
            axis=1,
        )
        line = both[layer, 6]
        heads = line[half_in : half_in + 3 * HL].reshape(3, HL)
        gain_in = jnp.concatenate(
            [full[layer, 6, :half_in], full[layer, 6, width : width + half_in]]
        )
        rest = jnp.stack([both[layer, 5, :DH], gain_in, jnp.repeat(heads[2], HDIM)])
        pars.append(jnp.concatenate([taps, jnp.pad(rest, ((0, 0), (0, CH - DH)))], axis=0))
        lines = jnp.stack([heads[0], jnp.exp(heads[1]), heads[2]])
        hps.append(jnp.pad(lines, ((0, 5), (0, LANE - HL))))

    tokens = [u_own, u_far]
    cots = [cot_own, cot_far]
    quarter = half_in // 2

    def own_quarter(normed):
        return jnp.concatenate(
            [
                lax.dynamic_slice_in_dim(normed, at * half_in + sec * quarter, quarter, 1)
                for at in range(2)
            ],
            axis=1,
        )

    def own_channels(gated):
        return lax.dynamic_slice_in_dim(gated, sec * (DH // 2), DH // 2, 1)

    def join_in(normed, dproj):
        far_n, far_p = swap(normed, "section"), swap(dproj, "section")
        return (tn(dproj, own_quarter(normed)) + tn(far_p, own_quarter(far_n))).astype(bf16)

    def join_out(gated, upstream):
        far_g, far_u = swap(gated, "section"), swap(upstream, "section")
        return (tn(own_channels(gated), upstream) + tn(own_channels(far_g), far_u)).astype(bf16)

    def guarded(branch, operand):
        shapes = jax.eval_shape(branch, operand)

        def nothing(operand):
            return jax.tree.map(lambda leaf: jnp.zeros(leaf.shape, leaf.dtype), shapes)

        return lax.cond(bound >= 0, branch, nothing, operand)

    u0, proj0, ys0, st0, mix0, unused_sum, stat0 = guarded(
        lambda tokens: run_forward(0, scal, pars[0], hps[0], weights[0], tokens, None), tokens
    )
    stat0_far = swap(stat0, "group")
    p0 = run_project(0, scal, pars[0], wo_a, wo_b, stat0, stat0_far, mix0)
    p0, cot_far = lax.optimization_barrier((p0, cot_far))
    cots = [cot_own, cot_far]
    p0_far = swap(p0.astype(jnp.float16), "group").astype(f32)
    u1, proj1, ys1, st1, mix1, p_total, stat1 = run_forward(
        1, scal, pars[1], hps[1], weights[1], cots, [u0, p0, p0_far]
    )
    stat1_far = swap(stat1, "group")
    piece = u_own.shape[0]

    def own_rows(block):
        return lax.dynamic_slice_in_dim(block, grp * piece, piece, 0)

    def far_rows(block):
        return lax.dynamic_slice_in_dim(block, (1 - grp) * piece, piece, 0)

    scale1 = lax.rsqrt((stat1 + stat1_far)[0] * (1.0 / DI) + EPS)[:, None]
    gated1 = (mix1 * scale1 * pars[1][5:6, :DH]).astype(bf16)
    b1 = join_out(gated1, in_order(cot_own, cot_far, grp, 0))
    stat1_far, b1 = lax.optimization_barrier((stat1_far, b1))
    share = b1.shape[0] // 2
    b1_late = b1[share:]
    b1 = lax.psum(b1[:share], "replica")

    def second_layer(stat1_far):
        n1, dp1, unused_gated, unused_g, dn1, small1 = run_backward(
            1, scal, pars[1], hps[1], weights[1],
            [u1, proj1, ys1, st1, stat1, stat1_far], cots, None,
        )
        dn1_far = swap(dn1, "group")
        dn1_far, a1 = lax.optimization_barrier((dn1_far, join_in(n1, dp1)))
        return dn1, dn1_far, a1, small1

    dn1, dn1_far, a1, small1 = guarded(second_layer, stat1_far)
    a1, b1 = lax.optimization_barrier((a1, b1))
    a1 = lax.psum(a1, "replica")

    def to_sections(first, second):
        held = jnp.where(sec == 0, first, second)
        given = swap(jnp.where(sec == 0, second, first), "section")
        return in_order(held[None], given[None], sec, 0)

    def swap_rows(part_a):
        stay = lax.dynamic_slice_in_dim(part_a, grp * quarter, quarter, 1)
        leave = lax.dynamic_slice_in_dim(part_a, far_grp * quarter, quarter, 1)
        return in_order(stay, swap(leave, "group"), grp, 1)

    def to_owner(block, layer):
        return lax.ppermute(block, "section", [(1 - layer, layer)])

    def gather_back(block, stages):
        for stage in reversed(stages):
            block = collect(block, stage, rep)
        return block

    def first_layer(dn1_far):
        n0, dp0, gated0, g0, dn0, small0 = run_backward(
            0, scal, pars[0], hps[0], weights[0],
            [u0, proj0, ys0, st0, stat0, stat0_far], cots,
            [p_total, u1, dn1, dn1_far, pars[1]],
        )
        a0 = join_in(n0, dp0)
        b0 = jnp.concatenate([join_out(gated0, g0), b1_late], axis=0)
        cut = [halves(block, (rep >> stages[0][0]) & 1) for block, stages in ((a0, order_a), (b0, order_b))]
        cut, dn0, g0, small0, late_gated, late_small = lax.optimization_barrier(
            (cut, dn0, g0, small0, gated1, small1)
        )
        sent = [
            flip(send, 1 << stages[0][0])
            for (keep, send), stages in zip(cut, (order_a, order_b))
        ]
        dn0_far = swap(far_rows(dn0), "group")

        p1 = nn(late_gated, jnp.where(sec == 1, wo_a, wo_b))
        p1_far = swap(far_rows(p1).astype(bf16), "group")
        small = jnp.stack([small0, late_small])
        small = small + swap(small, "section")
        far = swap(small, "group")
        shared = small + far
        own_x = jnp.concatenate([small[:, 0:5, :DH], far[:, 0:5, :LANE]], axis=2)
        own_y = jnp.concatenate([small[:, 0:5, LANE:DH], shared[:, 0:5, DH:]], axis=2)
        conv_part = jnp.where(grp == 0, own_x, own_y)
        gain_in = lax.dynamic_slice_in_dim(shared[:, 6, :DM], grp * half_in, half_in, 1)
        skip = small[:, 7, :DH].reshape(2, HL, HDIM).sum(axis=2)
        line = jnp.concatenate([gain_in, small[:, 8, :HL], small[:, 9, :HL], skip], axis=1)
        packed = jnp.concatenate(
            [
                conv_part,
                jnp.pad(small[:, 5:6, :DH], ((0, 0), (0, 0), (0, width - DH))),
                jnp.pad(line, ((0, 0), (0, width - line.shape[1])))[:, None],
                jnp.zeros((2, 1, width), f32),
            ],
            axis=1,
        )
        sent, dn0_far, p1_far, packed = lax.optimization_barrier((sent, dn0_far, p1_far, packed))
        state = [[keep, came] for (keep, send), came in zip(cut, sent)]
        values = u_own.astype(f32)
        scale = lax.rsqrt(jnp.mean(values * values, axis=-1, keepdims=True) + EPS)
        arrived = (own_rows(dn0).astype(f32) + dn0_far.astype(f32)) * pars[0][6:7, :DM]
        inner = jnp.mean(arrived * values, axis=-1, keepdims=True)
        grad1 = own_rows(g0)
        grad0 = (
            grad1.astype(f32) + scale * arrived - values * (scale * scale * scale * inner)
        ).astype(bf16)

        input_grad = to_sections(grad0, grad1)
        out0 = own_rows(u1)
        out1 = (out0.astype(f32) + own_rows(p1) + p1_far.astype(f32)).astype(bf16)
        segment_output = to_sections(out0, out1)
        for at in range(1, bits):
            cut = [
                [halves(piece, (rep >> stages[at][0]) & 1) for piece in pieces]
                for pieces, stages in zip(state, (order_a, order_b))
            ]
            sent = [
                flip(sum_low([send for keep, send in pair]), 1 << stages[at][0])
                for pair, stages in zip(cut, (order_a, order_b))
            ]
            far_packed = flip(packed, 1 << at)
            state = [
                [sum_low([keep for keep, send in pair]), came] for pair, came in zip(cut, sent)
            ]
            state, far_packed = lax.optimization_barrier((state, far_packed))
            packed = packed + far_packed
        a0, b0 = sum_low(state[0]), sum_low(state[1])
        far_packed = flip(packed, 1)
        a0 = swap_rows(a0)
        a0, far_packed = lax.optimization_barrier((a0, far_packed))
        packed = packed + far_packed
        a0, b0 = gather_back(a0, order_a[1:]), gather_back(b0, order_b[1:])
        packed = jnp.where(sec == 0, packed[0], packed[1])
        heads = packed[6, half_in : half_in + 3 * HL].reshape(3, HL)
        smalls = (packed[6:7, :half_in], packed[0:4], packed[4:5], heads, packed[5:6, :DH])
        return segment_output, input_grad, smalls, a0, b0

    segment_output, input_grad, smalls, a0, b0 = guarded(first_layer, dn1_far)
    a0_far = flip(a0, 1 << order_a[0][0])
    b0 = collect(b0, order_b[0], rep)
    came = swap(lax.dynamic_slice_in_dim(a1, far_grp * quarter, quarter, 1), "group")
    side = (rep >> order_a[0][0]) & 1
    grad_in_proj, grad_out_proj = run_assemble(
        jnp.stack([sec, grp, side]).astype(jnp.int32),
        [to_owner(a0, 0), to_owner(a0_far, 0), swap(b0, "section")],
        [a0, a0_far, b0],
        [a1, to_owner(a1, 1), came, to_owner(came, 1), b1, to_owner(b1, 1)],
        in_proj.shape[2],
    )
    grad_in_proj = jnp.swapaxes(grad_in_proj, 0, 1)
    return (
        segment_output[None, :, None],
        input_grad[None, :, None],
        smalls[0],
        grad_in_proj[None],
        smalls[1].T[None],
        smalls[2],
        smalls[3].T[None],
        smalls[4],
        grad_out_proj[None],
    )


def solution(mesh):
    placed = (
        P(None, "replica", "group", None),
        P(None, "replica"),
        P("section", "group"),
        P("section", "group", None),
        P("section", "group", None),
        P("section", "group"),
        P("section", "group", None),
        P("section", "group"),
        P("section", "group", None),
        P(None, "replica", "group", None),
    )
    return jax.shard_map(
        on_device,
        mesh=mesh,
        in_specs=placed,
        out_specs=(
            P("section", None, "replica", "group", None),
            P("section", None, "replica", "group", None),
            P("section", "group"),
            P("section", "group", None),
            P("section", "group", None),
            P("section", "group"),
            P("section", "group", None),
            P("section", "group"),
            P("section", "group", None),
        ),
        check_vma=False,
    )
```

```python
import functools

import jax
import jax.numpy as jnp
from jax import lax
from jax.experimental import pallas as pl
from jax.experimental.pallas import tpu as pltpu
from jax.sharding import PartitionSpec as P

DM = 1024
HEADS = 32
HDIM = 64
NS = 128
KW = 4
DI = 2048
CONVC = 2304
HL = HEADS // 2
DH = DI // 2
CH = DH + 2 * NS
CP = DH + CH + 128
LANE = 128
TILE = 256
RC = 32
HEAD_ROWS = 8
EPS = 1e-05
VMEM_BYTES = 63 * 1024 * 1024

f32 = jnp.float32
bf16 = jnp.bfloat16


def nn(left, right):
    return jnp.dot(left, right, preferred_element_type=f32)


def nt(left, right):
    return lax.dot_general(left, right, (((1,), (1,)), ((), ())), preferred_element_type=f32)


def tn(left, right):
    return lax.dot_general(left, right, (((0,), (0,)), ((), ())), preferred_element_type=f32)


def tile_at(index, size):
    return pl.ds(pl.multiple_of(index * size, size), size)


def loop(count, body):
    def step(index, carry):
        body(index)
        return carry

    lax.fori_loop(0, count, step, 0)


def iota(shape, dim):
    return lax.broadcasted_iota(jnp.int32, shape, dim)


def sigmoid(values):
    return 0.5 * jnp.tanh(0.5 * values) + 0.5


def softplus(values):
    small = jnp.exp(-jnp.abs(values))
    series = small * (1.0 - small * (0.5 - small * (1.0 / 3.0 - small * 0.25)))
    return jnp.maximum(values, 0.0) + jnp.where(small < 0.03, series, jnp.log(1.0 + small))


def split3(values):
    high = values.astype(bf16)
    rest = values - high.astype(f32)
    middle = rest.astype(bf16)
    low = (rest - middle.astype(f32)).astype(bf16)
    return high, middle, low


def pack3(values):
    high, middle, low = split3(values)
    packed = (
        high.astype(f32)
        + pltpu.roll(middle.astype(f32), HL, 1)
        + pltpu.roll(low.astype(f32), 2 * HL, 1)
    )
    return packed.astype(bf16)


def fill_spread(spread_s, width):
    shape = spread_s.shape
    row = iota(shape, 0)
    col = iota(shape, 1)
    hit = (row < 3 * HL) & ((row & (HL - 1)) == col // width)
    spread_s[...] = jnp.where(hit, 1.0, 0.0).astype(bf16)


def fill_gather(gather_s):
    shape = gather_s.shape
    hit = iota(shape, 0) // HDIM == iota(shape, 1)
    gather_s[...] = jnp.where(hit, 1.0, 0.0).astype(bf16)


def head_sums(values, gather_s):
    high = values.astype(bf16)
    low = (values - high.astype(f32)).astype(bf16)
    rows = values.shape[0]
    both = nn(jnp.concatenate([high, low], axis=0), gather_s[...])
    return both[:rows] + both[rows:]


def seam(bound, back, rows, align, count):
    first = jnp.clip(bound - back, 0, count - rows)
    return pl.multiple_of(first - lax.rem(first, align), align)


def seam_masks(first, rows, bound):
    pos = iota((rows, LANE), 0) + first
    masks = []
    for lag in range(1, KW):
        anchor = pos - lag
        dropped = (anchor < 0) | ((anchor < bound) & (bound <= pos))
        masks.append(jnp.where(dropped, 0.0, 1.0))
    return masks


def conv_phase(proj_s, par, bound, conv_s, pre_s, count):
    first = seam(bound, 0, 16, 8, count)
    masks = seam_masks(first, 16, bound)
    seam_rows = pl.ds(first, 16)

    def body(index):
        src = pl.ds(pl.multiple_of(DH + index * LANE, LANE), LANE)
        dst = tile_at(index, LANE)
        taps = par[0:8, dst]
        for at in range(0, count, 64):
            pre = taps[4:5] + taps[3:4] * proj_s[HEAD_ROWS + at : HEAD_ROWS + at + 64, src]
            for lag in range(1, KW):
                begin = HEAD_ROWS + at - lag
                pre = pre + taps[3 - lag : 4 - lag] * proj_s[begin : begin + 64, src]
            if pre_s is not None:
                pre_s[at : at + 64, dst] = pre
            conv_s[at : at + 64, dst] = pre * sigmoid(pre)
        window = proj_s[pl.ds(first, 16 + HEAD_ROWS), src]
        pre = taps[4:5] + taps[3:4] * window[HEAD_ROWS:]
        for lag in range(1, KW):
            part = window[HEAD_ROWS - lag : HEAD_ROWS - lag + 16] * masks[lag - 1]
            pre = pre + taps[3 - lag : 4 - lag] * part
        if pre_s is not None:
            pre_s[seam_rows, dst] = pre
        conv_s[seam_rows, dst] = pre * sigmoid(pre)

    loop(CH // LANE, body)


def step_phase(proj_s, hp, dt_s, rate_s, cs_s, cst_s, count):
    span = count // 2
    lanes = iota((count, LANE), 1)
    raw = proj_s[HEAD_ROWS : HEAD_ROWS + count, DH + CH : CP] + hp[0:1, :]
    step = jnp.where(lanes < HL, softplus(raw), 0.0)
    rate = -step * hp[1:2, :]
    dt_s[...] = step
    rate_s[...] = rate
    lower = jnp.where(iota((span, span), 0) >= iota((span, span), 1), 1.0, 0.0).astype(bf16)
    for block in range(2):
        rows = slice(block * span, (block + 1) * span)
        triple = jnp.concatenate(split3(rate[rows]), axis=1)
        sums = nn(lower, triple)
        total = sums[:, :LANE] + sums[:, LANE : 2 * LANE] + sums[:, 2 * LANE :]
        cs_s[rows] = total
        cst_s[block] = jnp.transpose(total)


def scaled_inputs(conv_s, dt_s, spread_s, xdt_s, xlo_s, count):
    def body(index):
        rows = tile_at(index, RC * 4)
        scale = nn(pack3(dt_s[rows]), spread_s[...])
        v = conv_s[rows, :DH] * scale
        xdt_s[rows] = v.astype(bf16)
        xlo_s[rows] = (v - v.astype(bf16).astype(f32)).astype(bf16)

    loop(count // (RC * 4), body)


def tail_weight(cs_s, bound, span):
    total = cs_s[0:span]
    pos = iota((span, LANE), 0)
    cut = (pos < bound) & (bound <= span - 1)
    lanes = iota((span, LANE), 1)
    keep = jnp.logical_not(cut) & (lanes < HL)
    return jnp.where(keep, jnp.exp(total[span - 1 : span] - total), 0.0)


def carry_weight(cs_s, bound, span):
    total = cs_s[span : 2 * span]
    pos = iota((span, LANE), 0) + span
    fresh = (span <= bound) & (bound <= pos)
    lanes = iota((span, LANE), 1)
    keep = jnp.logical_not(fresh) & (lanes < HL)
    return jnp.where(keep, jnp.exp(total), 0.0)


def inside_mask(block, bound, span, flipped):
    shape = (span, span)
    later = iota(shape, 1 if flipped else 0) + block * span
    early = iota(shape, 0 if flipped else 1) + block * span
    keep = (later >= early) & jnp.logical_not((early < bound) & (bound <= later))
    return jnp.where(keep, 1.0, 0.0)


def split2(values):
    high = values.astype(bf16)
    return high, (values - high.astype(f32)).astype(bf16)


def nt3(left, right):
    left_high, left_low = split2(left)
    right_high, right_low = split2(right)
    return nt(
        jnp.concatenate([left_high, left_low, left_high], axis=1),
        jnp.concatenate([right_high, right_high, right_low], axis=1),
    )


def nn3(left, right):
    left_high, left_low = split2(left)
    right_high, right_low = split2(right)
    return nn(
        jnp.concatenate([left_high, left_low, left_high], axis=1),
        jnp.concatenate([right_high, right_high, right_low], axis=0),
    )


def mix_tokens(first, second, high, low):
    rows = first.shape[0]
    first_high, first_low = split2(first)
    second_high, second_low = split2(second)
    stacked = jnp.concatenate([first_high, second_high, first_low, second_low], axis=0)
    both = nn(stacked, jnp.concatenate([high, low], axis=1))
    left, right = both[:, :LANE], both[:, LANE:]
    total = left[: 2 * rows] + right[: 2 * rows] + left[2 * rows :]
    keep = iota((rows, LANE), 1) < HDIM
    return jnp.where(keep, total[:rows], total[rows:])


def copies(pairs, sems, base):
    return [
        pltpu.make_async_copy(src, dst, sems.at[base + at]) for at, (src, dst) in enumerate(pairs)
    ]


def load_outer(layer, sec, wo_a, wo_b, wo_s, sem):
    held = pltpu.make_async_copy(wo_a, wo_s, sem)
    given = pltpu.make_async_copy(wo_b, wo_s, sem)

    @pl.when(sec == layer)
    def _():
        held.start()

    @pl.when(sec != layer)
    def _():
        given.start()

    return held


def load_weights(layer, sec, grp, w_a, w_b, w_x, w_y, w_s, sems):
    width = w_a.shape[1]
    mine = pl.ds(pl.multiple_of(grp * width, width), width)
    other = pl.ds(pl.multiple_of((1 - grp) * width, width), width)
    first = pl.multiple_of(grp * DH, DH)
    steps = pl.multiple_of(DI + CONVC + grp * HL, HL)
    places = [
        (pl.ds(first, DH), pl.ds(0, DH)),
        (pl.ds(DI + first, DH), pl.ds(DH, DH)),
        (pl.ds(2 * DI, 2 * NS), pl.ds(2 * DH, 2 * NS)),
        (pl.ds(steps, HL), pl.ds(DH + CH, HL)),
    ]
    w_s[DH + CH + HL : CP] = jnp.zeros((LANE - HL, 2 * width), bf16)

    def pieces(block):
        return copies([(block.at[src], w_s.at[dst, mine]) for src, dst in places], sems, 0)

    held, given = pieces(w_a), pieces(w_b)

    @pl.when(sec == layer)
    def _():
        for copy in held:
            copy.start()

    @pl.when(sec != layer)
    def _():
        for copy in given:
            copy.start()

    pairs = []
    for part, which in ((w_x, sec), (w_y, 1 - sec)):
        wide = pl.ds(pl.multiple_of(which * DH, DH), DH)
        thin = pl.ds(pl.multiple_of(2 * DH + which * NS, NS), NS)
        pairs.append((part.at[pl.ds(0, DH)], w_s.at[wide, other]))
        pairs.append((part.at[pl.ds(DH, NS)], w_s.at[thin, other]))
    pairs.append((w_x.at[pl.ds(DH + NS, HL)], w_s.at[pl.ds(DH + CH, HL), other]))
    far = copies(pairs, sems, 24)
    for copy in far:
        copy.start()
    return held + far


def column_of(stat_ref, hold_s):
    hold_s[...] = jnp.zeros_like(hold_s)
    hold_s[0:8] = stat_ref[...]
    return jnp.transpose(hold_s[...])


def forward_kernel(layer, *refs):
    (scal, par, hp, w_a, w_b, w_x, w_y, wo_a, wo_b) = refs[:9]
    if layer == 0:
        in_own, in_far = refs[9:11]
        rest = refs[11:]
    else:
        u_prev, p_own, p_far, in_own, in_far = refs[9:14]
        rest = refs[14:]
    (u_out, proj_out, ys_out, st_out, mix_out, sum_out, stat_out) = rest[:7]
    (w_s, wo_s, u_s, n_s, proj_s, conv_s, dt_s, rate_s, cs_s, cst_s, xdt_s,
     y_s, mix_s, st_s, pp_s, g_s, spread_s, stat_s, hold_s, in_s, xlo_s, sems) = rest[7:]
    sec, grp, bound = scal[0], scal[1], scal[2]
    count = u_s.shape[0]
    span = count // 2
    piece = count // 2
    place_own = pl.ds(pl.multiple_of(grp * piece, piece), piece)
    place_far = pl.ds(pl.multiple_of((1 - grp) * piece, piece), piece)
    token_target = u_s if layer == 0 else in_s
    token_in = copies(
        [(in_own, token_target.at[place_own]), (in_far, token_target.at[place_far])], sems, 8
    )
    if layer == 0:
        for copy in token_in:
            copy.start()
    else:
        more = copies([(u_prev, u_s), (p_own, pp_s.at[0]), (p_far, pp_s.at[1])], sems, 10)
        for copy in more:
            copy.start()
    w_in = load_weights(layer, sec, grp, w_a, w_b, w_x, w_y, w_s, sems)
    if layer == 1:
        for copy in token_in:
            copy.start()
        wo_in = load_outer(layer, sec, wo_a, wo_b, wo_s, sems.at[4])
    fill_spread(spread_s, HDIM)
    proj_s[0:HEAD_ROWS] = jnp.zeros((HEAD_ROWS, CP), f32)
    gain_in = par[6:7, :DM]
    if layer == 0:
        for copy in token_in:
            copy.wait()
    else:
        for copy in more:
            copy.wait()

    def norm_rows(index):
        rows = tile_at(index, RC)
        values = u_s[rows].astype(f32)
        if layer == 1:
            total = pp_s[0, rows] + pp_s[1, rows]
            pp_s[0, rows] = total
            low = (values + total).astype(bf16)
            u_s[rows] = low
            values = low.astype(f32)
        scale = lax.rsqrt(jnp.mean(values * values, axis=-1, keepdims=True) + EPS)
        n_s[rows] = (values * scale * gain_in).astype(bf16)

    loop(count // RC, norm_rows)
    out_sum = None
    if layer == 1:
        out_sum = pltpu.make_async_copy(pp_s.at[0], sum_out, sems.at[18])
        out_sum.start()
    out_u = pltpu.make_async_copy(u_s, u_out, sems.at[13])
    out_u.start()
    for copy in w_in:
        copy.wait()

    body_rows = slice(HEAD_ROWS, HEAD_ROWS + count)

    def project(index):
        lane = tile_at(index, TILE)
        proj_s[body_rows, lane] = nt(n_s[...], w_s[lane, :])

    loop(CP // TILE, project)
    proj_s[body_rows, CP - LANE : CP] = nt(n_s[...], w_s[CP - LANE : CP, :])
    out_proj = pltpu.make_async_copy(proj_s, proj_out, sems.at[14])
    out_proj.start()

    conv_phase(proj_s, par, bound, conv_s, None, count)
    step_phase(proj_s, hp, dt_s, rate_s, cs_s, cst_s, count)
    scaled_inputs(conv_s, dt_s, spread_s, xdt_s, xlo_s, count)

    skip = par[7:8, :DH]
    gain_out = par[5:6, :DH]
    lanes = iota((RC, LANE), 1)

    def mix_rows(index):
        rows = tile_at(index, RC)
        shifted_rows = pl.ds(pl.multiple_of(HEAD_ROWS + index * RC, HEAD_ROWS), RC)
        gate = proj_s[shifted_rows, :DH]
        value = y_s[rows] + skip * conv_s[rows, :DH]
        y_s[rows] = value
        mixed = value * (gate * sigmoid(gate))
        conv_s[rows, :DH] = mixed
        if layer == 1:
            mix_s[rows] = (mixed * gain_out).astype(bf16)
        square = jnp.sum(mixed * mixed, axis=-1, keepdims=True)
        stat_s[rows] = jnp.where(lanes == 0, square, 0.0)

    flushed = []
    for block in range(2):
        rows = slice(block * span, (block + 1) * span)
        low_b = conv_s[rows, DH : DH + NS].astype(bf16)
        low_c = conv_s[rows, DH + NS : CH].astype(bf16)
        g_s[...] = nt3(conv_s[rows, DH + NS : CH], conv_s[rows, DH : DH + NS]) * inside_mask(block, bound, span, False)

        def pair(index):
            lane = tile_at(index, LANE)
            near = xdt_s[rows, lane]
            near_low = xlo_s[rows, lane]
            turned_cs = pltpu.roll(cs_s[rows], lax.rem(LANE - 2 * index, LANE), 1)
            for at in range(0, span, LANE):
                size = at + LANE
                here = slice(block * span + at, block * span + at + LANE)
                mixings = []
                for side in range(2):
                    head = 2 * index + side
                    col = jnp.broadcast_to(turned_cs[at : at + LANE, side : side + 1], (LANE, LANE))
                    line = cst_s[block, pl.ds(head, 1), :][:, :size]
                    wide = jnp.concatenate([col] * (size // LANE), axis=1)
                    decay = jnp.exp(jnp.minimum(wide - line, 0.0))
                    mixings.append(decay * g_s[at : at + LANE, :size])
                y_s[here, lane] = mix_tokens(*mixings, near[:size], near_low[:size])

        loop(HL // 2, pair)
        if block == 0:
            weight = pack3(tail_weight(cs_s, bound, span))
            turned = jnp.transpose(conv_s[rows, DH : DH + NS])

            def state_tile(index):
                lane = tile_at(index, TILE)
                scaled = (xdt_s[rows, lane].astype(f32) + xlo_s[rows, lane].astype(f32)) * nn(weight, spread_s[:, lane])
                st_s[:, lane] = nn3(turned, scaled)

            loop(DH // TILE, state_tile)
        else:
            weight = pack3(carry_weight(cs_s, bound, span))

            def carry_tile(index):
                lane = tile_at(index, TILE)
                carried = nn3(conv_s[rows, DH + NS : CH], st_s[:, lane])
                y_s[rows, lane] += carried * nn(weight, spread_s[:, lane])

            loop(DH // TILE, carry_tile)
        first_tile = block * (span // RC)
        loop(span // RC, lambda index: mix_rows(first_tile + index))
        flushed += copies(
            [
                (y_s.at[rows], ys_out.at[rows]),
                (conv_s.at[rows, pl.ds(0, DH)], mix_out.at[rows]),
            ],
            sems,
            16 if block == 0 else 20,
        )
        for copy in flushed[-2:]:
            copy.start()
    out_st = pltpu.make_async_copy(st_s, st_out, sems.at[15])
    out_st.start()

    if layer == 1:
        wo_in.wait()
        for copy in token_in:
            copy.wait()

        def out_tile(index):
            lane = tile_at(index, TILE)
            partial = nn(mix_s[...], wo_s[:, lane])
            dots = jnp.sum(partial * in_s[:, lane].astype(f32), axis=-1, keepdims=True)
            stat_s[...] += jnp.where(iota((count, LANE), 1) == 1, dots, 0.0)

        loop(DM // TILE, out_tile)
    stat_out[...] = jnp.transpose(stat_s[...])[0:8]
    for copy in (out_u, out_proj, out_st, *flushed):
        copy.wait()
    if layer == 1:
        out_sum.wait()


def backward_kernel(layer, *refs):
    (scal, par, hp, w_a, w_b, w_x, w_y, wo_a, wo_b) = refs[:9]
    (u_in, proj_in, ys_in, st_in, stat_own, stat_far, in_own, in_far) = refs[9:17]
    if layer == 1:
        rest = refs[17:]
    else:
        p_sum, up_in, dn_own, dn_far, par_up = refs[17:22]
        rest = refs[22:]
    (n_out, dp_out, gated_out, g_out, dn_out, small_out) = rest[:6]
    (w_s, wo_s, u_s, n_s, proj_s, conv_s, pre_s, dt_s, rate_s, cs_s, cst_s, grad_cs_s, xdt_s,
     y_s, st_s, ad_s, pp_s, dn_s, g_s, up_s, gg_s, dys_s, dx_s, dpre_s, dp_s, gm_s, dg_s,
     spread_s, gather_s, stat_s, hold_s, xlo_s, dlo_s, sems) = rest[6:]
    sec, grp, bound = scal[0], scal[1], scal[2]
    count = u_s.shape[0]
    span = count // 2
    piece = count // 2
    place_own = pl.ds(pl.multiple_of(grp * piece, piece), piece)
    place_far = pl.ds(pl.multiple_of((1 - grp) * piece, piece), piece)
    token_in = copies([(in_own, g_s.at[place_own]), (in_far, g_s.at[place_far])], sems, 8)
    saved_in = copies([(u_in, u_s), (proj_in, proj_s), (ys_in, y_s), (st_in, st_s)], sems, 10)
    for copy in token_in:
        copy.start()
    if layer == 0:
        more = copies(
            [
                (dn_own, dn_s.at[0]),
                (dn_far, dn_s.at[1]),
                (up_in, up_s),
                (p_sum, pp_s),
            ],
            sems,
            14,
        )
        for copy in more:
            copy.start()
    wo_in = load_outer(layer, sec, wo_a, wo_b, wo_s, sems.at[4])
    for copy in saved_in[1:]:
        copy.start()
    fill_spread(spread_s, HDIM)
    fill_gather(gather_s)
    stats = column_of(stat_own, hold_s) + column_of(stat_far, hold_s)
    stat_s[...] = stats
    for copy in token_in:
        copy.wait()
    lane_rc = iota((RC, LANE), 1)
    if layer == 0:
        for copy in more:
            copy.wait()
        gain_up = par_up[6:7, :DM]

        def upstream_rows(index):
            rows = tile_at(index, RC)
            values = up_s[rows].astype(f32)
            scale = lax.rsqrt(jnp.mean(values * values, axis=-1, keepdims=True) + EPS)
            arrived = (dn_s[0, rows].astype(f32) + dn_s[1, rows].astype(f32)) * gain_up
            inner = jnp.mean(arrived * values, axis=-1, keepdims=True)
            total = g_s[rows].astype(f32) + scale * arrived - values * (scale * scale * scale * inner)
            low = total.astype(bf16)
            g_s[rows] = low
            dots = jnp.sum(low.astype(f32) * pp_s[rows], axis=-1, keepdims=True)
            stat_s[rows] = jnp.where(lane_rc == 1, dots, stat_s[rows])

        loop(count // RC, upstream_rows)
    out_g = pltpu.make_async_copy(g_s, g_out, sems.at[19])
    out_g.start()
    wo_in.wait()

    def gated_tile(index):
        lane = tile_at(index, TILE)
        gg_s[:, lane] = nt(g_s[...], wo_s[lane, :])

    loop(DH // TILE, gated_tile)
    for copy in saved_in[1:]:
        copy.wait()
    w_in = load_weights(layer, sec, grp, w_a, w_b, w_x, w_y, w_s, sems)
    saved_in[0].start()

    conv_phase(proj_s, par, bound, conv_s, pre_s, count)
    step_phase(proj_s, hp, dt_s, rate_s, cs_s, cst_s, count)
    scaled_inputs(conv_s, dt_s, spread_s, xdt_s, xlo_s, count)

    skip = par[7:8, :DH]
    gain_out = par[5:6, :DH]
    gain_in = par[6:7, :DM]

    def fold(values):
        return jnp.sum(values.reshape(-1, 8, values.shape[-1]), axis=0)

    def mix_rows(index, carry):
        gain_sum, skip_sum = carry
        rows = tile_at(index, RC)
        shifted_rows = pl.ds(pl.multiple_of(HEAD_ROWS + index * RC, HEAD_ROWS), RC)
        scale = lax.rsqrt(stat_s[rows, 0:1] * (1.0 / DI) + EPS)
        inner = stat_s[rows, 1:2] * (scale * scale * (1.0 / DI))
        if layer == 1:
            inner = inner * scale
        gate = proj_s[shifted_rows, :DH]
        gate_sig = sigmoid(gate)
        gate_act = gate * gate_sig
        value = y_s[rows]
        grad = gg_s[rows]
        mixed = value * gate_act
        scaled = mixed * scale
        dmixed = grad * gain_out * scale - mixed * inner
        mixed_low = (scaled * gain_out).astype(bf16)
        gated_s[rows] = mixed_low
        dys = dmixed * gate_act
        dgate = dmixed * value * (gate_sig + gate_act * (1.0 - gate_sig))
        dp_s[rows, :DH] = dgate.astype(bf16)
        inputs = conv_s[rows, :DH]
        gg_s[rows] = dys
        low = dys.astype(bf16)
        dys_s[rows] = low
        dlo_s[rows] = (dys - low.astype(f32)).astype(bf16)
        y_s[rows] = dys * (value - skip * inputs)
        return (gain_sum + fold(grad * scaled), skip_sum + fold(dys * inputs))

    gated_s = n_s
    zero = jnp.zeros((8, DH), f32)
    gain_sum, skip_sum = lax.fori_loop(0, count // RC, mix_rows, (zero, zero))
    small_out[...] = jnp.zeros_like(small_out)
    small_out[5:6, :DH] = jnp.sum(gain_sum, axis=0, keepdims=True)
    small_out[7:8, :DH] = jnp.sum(skip_sum, axis=0, keepdims=True)
    out_gated = pltpu.make_async_copy(n_s, gated_out, sems.at[20])
    out_gated.start()

    lane_left = iota((span, LANE), 1) < HDIM
    for block in (1, 0):
        rows = slice(block * span, (block + 1) * span)
        low_b = conv_s[rows, DH : DH + NS].astype(bf16)
        low_c = conv_s[rows, DH + NS : CH].astype(bf16)
        keep = inside_mask(block, bound, span, True)
        gm_s[...] = nt3(conv_s[rows, DH : DH + NS], conv_s[rows, DH + NS : CH]) * keep
        dg_s[...] = jnp.zeros_like(dg_s)

        def pair(index):
            lane = tile_at(index, LANE)
            near = xdt_s[rows, lane]
            far = dys_s[rows, lane]
            far_low = dlo_s[rows, lane]
            turned_cs = pltpu.roll(cs_s[rows], lax.rem(LANE - 2 * index, LANE), 1)
            for at in range(0, span, LANE):
                size = span - at
                here = slice(block * span + at, block * span + at + LANE)
                part = near[at : at + LANE]
                mixings, decays, parts = [], [], []
                for side in range(2):
                    head = 2 * index + side
                    col = jnp.broadcast_to(turned_cs[at : at + LANE, side : side + 1], (LANE, LANE))
                    line = cst_s[block, pl.ds(head, 1), :][:, at:]
                    wide = jnp.concatenate([col] * (size // LANE), axis=1)
                    decay = jnp.exp(jnp.minimum(line - wide, 0.0))
                    decays.append(decay)
                    mixings.append(decay * gm_s[at : at + LANE, at:])
                    mine = lane_left[:LANE] if side == 0 else jnp.logical_not(lane_left[:LANE])
                    parts.append(jnp.where(mine, part.astype(f32), 0.0).astype(bf16))
                dx_s[here, lane] = mix_tokens(*mixings, far[at:], far_low[at:])
                pairs = nt(jnp.concatenate(parts, axis=0), far[at:])
                dg_s[at : at + LANE, at:] += pairs[:LANE] * decays[0] + pairs[LANE:] * decays[1]

        loop(HL // 2, pair)
        grad_g = dg_s[...] * keep
        dpre_s[rows, DH : DH + NS] = nn(grad_g.astype(bf16), low_c)
        dpre_s[rows, DH + NS : CH] = nn(jnp.transpose(grad_g).astype(bf16), low_b)
        if block == 1:
            weight = pack3(carry_weight(cs_s, bound, span))
            turned_c = jnp.transpose(conv_s[rows, DH + NS : CH])

            def carry_tile(index):
                lane = tile_at(index, TILE)
                scaled = (dys_s[rows, lane].astype(f32) + dlo_s[rows, lane].astype(f32)) * nn(weight, spread_s[:, lane])
                ad_s[:, lane] = nn3(turned_c, scaled)
                dpre_s[rows, DH + NS : CH] += nt3(scaled, st_s[:, lane])

            loop(DH // TILE, carry_tile)
        else:
            weight = pack3(tail_weight(cs_s, bound, span))

            def state_tile(index):
                lane = tile_at(index, TILE)
                scale = nn(weight, spread_s[:, lane])
                low_a = ad_s[:, lane]
                inputs = xdt_s[rows, lane].astype(f32) + xlo_s[rows, lane].astype(f32)
                extra = nn3(conv_s[rows, DH : DH + NS], low_a) * scale
                dx_s[rows, lane] += extra
                both = inputs * scale
                pre_tail = jnp.sum(fold(inputs * extra), axis=0, keepdims=True)
                dpre_s[count : count + 1, lane] = pre_tail
                dpre_s[rows, DH : DH + NS] += nt3(both, low_a)

            loop(DH // TILE, state_tile)

    def head_rows(index):
        chunk = RC * 4
        rows = tile_at(index, chunk)
        steps = dt_s[rows]
        scale = nn(pack3(steps), spread_s[...])
        grad = dx_s[rows]
        sums = head_sums(jnp.concatenate([conv_s[rows, :DH] * grad, y_s[rows]], axis=0), gather_s)
        per_step = sums[:chunk]
        stat_s[rows] = per_step
        grad_cs_s[rows] = sums[chunk:] - steps * per_step
        dpre_s[rows, :DH] = gg_s[rows] * skip + grad * scale

    loop(count // (RC * 4), head_rows)
    tail = jnp.broadcast_to(dpre_s[count : count + 1, :DH], (8, DH))
    tail_heads = head_sums(tail, gather_s)[0:1]
    last = iota((span, LANE), 0) == span - 1
    upper = jnp.where(iota((span, span), 0) <= iota((span, span), 1), 1.0, 0.0).astype(bf16)
    bias_sum = jnp.zeros((1, LANE), f32)
    decay_sum = jnp.zeros((1, LANE), f32)
    for block in range(2):
        rows = slice(block * span, (block + 1) * span)
        raw = proj_s[HEAD_ROWS + block * span : HEAD_ROWS + (block + 1) * span, DH + CH : CP]
        grad_cs = grad_cs_s[rows]
        if block == 0:
            grad_cs = grad_cs + jnp.where(last, tail_heads, 0.0)
        sums = nn(upper, jnp.concatenate(split3(grad_cs), axis=1))
        grad_rate = sums[:, :LANE] + sums[:, LANE : 2 * LANE] + sums[:, 2 * LANE :]
        grad_step = stat_s[rows] - grad_rate * hp[1:2, :]
        lanes = iota((span, LANE), 1)
        grad_raw = jnp.where(lanes < HL, grad_step * sigmoid(raw + hp[0:1, :]), 0.0)
        dp_s[rows, DH + CH : CP] = grad_raw.astype(bf16)
        bias_sum = bias_sum + jnp.sum(grad_raw, axis=0, keepdims=True)
        decay_sum = decay_sum + jnp.sum(grad_rate * rate_s[rows], axis=0, keepdims=True)
    small_out[8:9, :LANE] = bias_sum
    small_out[9:10, :LANE] = decay_sum

    dpre_s[count : count + 8] = jnp.zeros((8, CH), f32)

    first = seam(bound, 0, 16, 8, count)
    masks = seam_masks(first, 16, bound)
    back = seam(bound, KW - 1, 32, 16, count)
    back_masks = seam_masks(back, 40, bound)

    def conv_back(index):
        src = pl.ds(pl.multiple_of(DH + index * LANE, LANE), LANE)
        dst = tile_at(index, LANE)
        taps = par[0:8, dst]
        sums = [jnp.zeros((8, LANE), f32) for _ in range(KW + 1)]
        for at in range(0, count, 64):
            pre = pre_s[at : at + 64, dst]
            sig = sigmoid(pre)
            grad = dpre_s[at : at + 64, dst] * (sig + pre * sig * (1.0 - sig))
            dpre_s[at : at + 64, dst] = grad
            sums[4] = sums[4] + fold(grad)
            for lag in range(KW):
                begin = HEAD_ROWS + at - lag
                sums[3 - lag] = sums[3 - lag] + fold(grad * proj_s[begin : begin + 64, src])
        window = proj_s[pl.ds(first, 16 + HEAD_ROWS), src]
        grad = dpre_s[pl.ds(first, 16), dst]
        for lag in range(1, KW):
            part = window[HEAD_ROWS - lag : HEAD_ROWS - lag + 16] * (1.0 - masks[lag - 1])
            sums[3 - lag] = sums[3 - lag] - fold(grad * part)
        for at in range(0, count, 64):
            total = taps[3:4] * dpre_s[at : at + 64, dst]
            for lag in range(1, KW):
                begin = at + lag
                total = total + taps[3 - lag : 4 - lag] * dpre_s[begin : begin + 64, dst]
            dp_s[at : at + 64, src] = total.astype(bf16)
        window = dpre_s[pl.ds(back, 40), dst]
        total = taps[3:4] * window[:32]
        for lag in range(1, KW):
            part = window[lag : lag + 32] * back_masks[lag - 1][lag : lag + 32]
            total = total + taps[3 - lag : 4 - lag] * part
        dp_s[pl.ds(back, 32), src] = total.astype(bf16)
        for at in range(KW + 1):
            small_out[at : at + 1, dst] = jnp.sum(sums[at], axis=0, keepdims=True)

    loop(CH // LANE, conv_back)
    out_dp = pltpu.make_async_copy(dp_s, dp_out, sems.at[21])
    out_dp.start()
    for copy in w_in:
        copy.wait()
    saved_in[0].wait()

    def normed_tile(index):
        lane = tile_at(index, TILE)
        gg_s[:, lane] = nn(dp_s[...], w_s[:, lane])

    loop(DM // TILE, normed_tile)
    out_gated.wait()

    def norm_rows(index, gain_sum):
        rows = tile_at(index, RC)
        values = u_s[rows].astype(f32)
        scale = lax.rsqrt(jnp.mean(values * values, axis=-1, keepdims=True) + EPS)
        unit = values * scale
        n_s[rows] = (unit * gain_in).astype(bf16)
        grad = gg_s[rows]
        dys_s[rows] = grad.astype(bf16)
        return gain_sum + fold(grad * unit)

    gain_total = lax.fori_loop(0, count // RC, norm_rows, jnp.zeros((8, DM), f32))
    small_out[6:7, :DM] = jnp.sum(gain_total, axis=0, keepdims=True)
    out_n = pltpu.make_async_copy(n_s, n_out, sems.at[22])
    out_dn = pltpu.make_async_copy(dys_s, dn_out, sems.at[23])
    out_n.start()
    out_dn.start()
    for copy in (out_g, out_dp, out_n, out_dn):
        copy.wait()


def project_kernel(layer, scal, par, wo_a, wo_b, stat_own, stat_far, mix_in, p_out, wo_s, low_s, stat_s, hold_s, sems):
    sec = scal[0]
    count = mix_in.shape[0]
    from_a = pltpu.make_async_copy(wo_a, wo_s, sems.at[0])
    from_b = pltpu.make_async_copy(wo_b, wo_s, sems.at[0])

    @pl.when(sec == layer)
    def _():
        from_a.start()

    @pl.when(sec != layer)
    def _():
        from_b.start()

    stats = column_of(stat_own, hold_s) + column_of(stat_far, hold_s)
    stat_s[...] = lax.rsqrt(stats * (1.0 / DI) + EPS)
    gain_out = par[5:6, :DH]

    def rows_of(index):
        rows = tile_at(index, RC)
        low_s[rows] = (mix_in[rows] * stat_s[rows, 0:1] * gain_out).astype(bf16)

    loop(count // RC, rows_of)
    from_a.wait()

    def out_tile(index):
        lane = tile_at(index, TILE)
        p_out[:, lane] = nn(low_s[...], wo_s[:, lane]).astype(p_out.dtype)

    loop(DM // TILE, out_tile)


ANY = pl.BlockSpec(memory_space=pl.ANY)
VM = pl.BlockSpec(memory_space=pltpu.VMEM)
SM = pl.BlockSpec(memory_space=pltpu.SMEM)


def call(kernel, args, specs, outs, out_specs, scratch, name, flops):
    return pl.pallas_call(
        kernel,
        in_specs=specs,
        out_specs=out_specs,
        out_shape=[jax.ShapeDtypeStruct(shape, dtype) for shape, dtype in outs],
        scratch_shapes=scratch,
        compiler_params=pltpu.CompilerParams(vmem_limit_bytes=VMEM_BYTES),
        cost_estimate=pl.CostEstimate(
            flops=flops, bytes_accessed=20_000_000, transcendentals=4_000_000
        ),
        name=name,
    )(*args)


def vm(shape, dtype):
    return pltpu.VMEM(shape, dtype)


def run_forward(layer, scal, par, hp, weights, tokens, saved):
    count = 2 * tokens[0].shape[0]
    span = count // 2
    args = [scal, par, hp, *weights]
    specs = [SM, VM, VM] + [ANY] * 6
    if layer == 1:
        args += saved
        specs += [ANY, ANY, ANY]
    args += tokens
    specs += [ANY, ANY]
    outs = [
        ((count, DM), bf16),
        ((count + HEAD_ROWS, CP), f32),
        ((count, DH), f32),
        ((NS, DH), f32),
        ((count, DH), f32),
        ((count, DM) if layer == 1 else (8, LANE), f32),
        ((8, count), f32),
    ]
    out_specs = [ANY] * 6 + [VM]
    scratch = [
        vm((CP, DM), bf16),
        vm((DH, DM), bf16),
        vm((count, DM), bf16),
        vm((count, DM), bf16),
        vm((count + HEAD_ROWS, CP), f32),
        vm((count, CH), f32),
        vm((count, LANE), f32),
        vm((count, LANE), f32),
        vm((count, LANE), f32),
        vm((2, LANE, span), f32),
        vm((count, DH), bf16),
        vm((count, DH), f32),
        vm((count, DH), bf16),
        vm((NS, DH), f32),
        vm((2, count, DM), f32),
        vm((span, span), f32),
        vm((LANE, DH), bf16),
        vm((count, LANE), f32),
        vm((LANE, count), f32),
        vm((count, DM), bf16),
        vm((count, DH), bf16),
        pltpu.SemaphoreType.DMA((29,)),
    ]
    return call(
        functools.partial(forward_kernel, layer),
        args,
        specs,
        outs,
        out_specs,
        scratch,
        "forward_%d" % layer,
        35_000_000_000,
    )


def assemble_kernel(scal, *refs):
    got, own = refs[:3], refs[3:6]
    a1, a1_got, came, came_got, b1, b1_got = refs[6:12]
    in_out, out_out, whole_s, outer_s, in_s, out_s, sems = refs[12:]
    sec, grp = scal[0], scal[1]
    half = whole_s.shape[1] // 2
    quart = whole_s.shape[2] // 2
    outer = outer_s.shape[0] // 2
    share = b1.shape[0]

    def first_pairs(blocks, core):
        near, far, wide = blocks
        pairs = []
        for at, block in ((scal[2], near), (1 - scal[2], far)):
            rows = pl.ds(pl.multiple_of(at * half, 16), half)
            pairs.append((block, whole_s.at[core, rows]))
        return pairs + [(wide.at[pl.ds(0, outer)], outer_s.at[pl.ds(core * outer, outer)])]

    def outer_pairs(early, wide, core):
        return [
            (early, outer_s.at[pl.ds(core * outer, share)]),
            (wide.at[pl.ds(outer, share)], outer_s.at[pl.ds(core * outer + share, share)]),
        ]

    def second_pairs(block, moved, core):
        near = pl.ds(pl.multiple_of(grp * quart, quart), quart)
        far = pl.ds(pl.multiple_of((1 - grp) * quart, quart), quart)
        return [
            (block.at[:, near], whole_s.at[core, :, near]),
            (moved, whole_s.at[core, :, far]),
        ]

    def fetch(pairs):
        started = copies(pairs, sems, 0)
        for copy in started:
            copy.start()
        for copy in started:
            copy.wait()

    @pl.when(sec == 0)
    def _():
        fetch(first_pairs(own, 0) + first_pairs(got, 1))

    @pl.when(sec != 0)
    def _():
        fetch(
            second_pairs(a1, came, 1)
            + second_pairs(a1_got, came_got, 0)
            + outer_pairs(b1, own[2], 1)
            + outer_pairs(b1_got, got[2], 0)
        )

    width = in_s.shape[1]
    quarter = width // 2
    step = 64
    started = []

    def send(piece, sem):
        copy = pltpu.make_async_copy(in_s.at[piece], in_out.at[piece], sems.at[sem])
        copy.start()
        started.append(copy)

    def emit(target, source, count, side):
        def body(index):
            at = pl.multiple_of(index * step, step)
            for core in range(2):
                value = whole_s[core, pl.ds(source + at, step), side * quarter : (side + 1) * quarter]
                lane = slice(core * quarter, (core + 1) * quarter)
                in_s[pl.ds(target + at, step), lane] = value.astype(f32)

        loop(count // step, body)

    for at, (target, source, side) in enumerate(
        ((0, 0, 0), (DH, 0, 1), (DI, DH, 0), (DI + DH, DH, 1))
    ):
        emit(target, source, DH, side)
        send(pl.ds(target, DH), 8 + at)
    for core in range(2):
        lane = slice(core * quarter, (core + 1) * quarter)
        left, right = slice(0, quarter), slice(quarter, width)
        shared = slice(2 * DH, 2 * DH + 2 * NS)
        in_s[2 * DI : 2 * DI + 2 * NS, lane] = whole_s[core, shared, left].astype(f32) + whole_s[
            core, shared, right
        ].astype(f32)
        steps = slice(DH + CH, DH + CH + HL)
        in_s[DI + CONVC : DI + CONVC + HL, lane] = whole_s[core, steps, left].astype(f32)
        in_s[DI + CONVC + HL :, lane] = whole_s[core, steps, right].astype(f32)
    send(pl.ds(2 * DI, 2 * NS + HEADS), 12)

    def body(index):
        rows = tile_at(index, step)
        out_s[rows] = outer_s[rows].astype(f32)

    loop(out_s.shape[0] // step, body)
    copy = pltpu.make_async_copy(out_s, out_out, sems.at[13])
    copy.start()
    started.append(copy)
    for copy in started:
        copy.wait()


def run_assemble(scal, got, own, second, columns):
    rows, width = second[0].shape
    outer = (4 * second[-1].shape[0], second[-1].shape[1])
    return call(
        assemble_kernel,
        [scal, *got, *own, *second],
        [SM] + [ANY] * 12,
        [((columns, width), f32), (outer, f32)],
        [ANY, ANY],
        [
            vm((2, rows, width), bf16),
            vm(outer, bf16),
            vm((columns, width), f32),
            vm(outer, f32),
            pltpu.SemaphoreType.DMA((14,)),
        ],
        "assemble",
        6_000_000_000,
    )


def run_project(layer, scal, par, wo_a, wo_b, stat_own, stat_far, mixed):
    count = mixed.shape[0]
    return call(
        functools.partial(project_kernel, layer),
        [scal, par, wo_a, wo_b, stat_own, stat_far, mixed],
        [SM, VM, ANY, ANY, VM, VM, VM],
        [((count, DM), f32)],
        [VM],
        [
            vm((DH, DM), bf16),
            vm((count, DH), bf16),
            vm((count, LANE), f32),
            vm((LANE, count), f32),
            pltpu.SemaphoreType.DMA((1,)),
        ],
        "project_%d" % layer,
        6_000_000_000,
    )[0]


def run_backward(layer, scal, par, hp, weights, saved, tokens, late):
    count = 2 * tokens[0].shape[0]
    span = count // 2
    args = [scal, par, hp, *weights, *saved, *tokens]
    specs = [SM, VM, VM] + [ANY] * 6 + [ANY] * 4 + [VM, VM] + [ANY] * 2
    if layer == 0:
        args += late
        specs += [ANY] * 4 + [VM]
    outs = [
        ((count, DM), bf16),
        ((count, CP), bf16),
        ((count, DH), bf16),
        ((count, DM), bf16),
        ((count, DM), bf16),
        ((16, CH), f32),
    ]
    out_specs = [ANY] * 5 + [VM]
    scratch = [
        vm((CP, DM), bf16),
        vm((DH, DM), bf16),
        vm((count, DM), bf16),
        vm((count, DM), bf16),
        vm((count + HEAD_ROWS, CP), f32),
        vm((count, CH), f32),
        vm((count, CH), f32),
        vm((count, LANE), f32),
        vm((count, LANE), f32),
        vm((count, LANE), f32),
        vm((2, LANE, span), f32),
        vm((count, LANE), f32),
        vm((count, DH), bf16),
        vm((count, DH), f32),
        vm((NS, DH), f32),
        vm((NS, DH), f32),
        vm((count, DM), f32),
        vm((2, count, DM), bf16),
        vm((count, DM), bf16),
        vm((count, DM), bf16),
        vm((count, DM), f32),
        vm((count, DM), bf16),
        vm((count, DH), f32),
        vm((count + 8, CH), f32),
        vm((count, CP), bf16),
        vm((span, span), f32),
        vm((span, span), f32),
        vm((LANE, DH), bf16),
        vm((DH, LANE), bf16),
        vm((count, LANE), f32),
        vm((LANE, count), f32),
        vm((count, DH), bf16),
        vm((count, DH), bf16),
        pltpu.SemaphoreType.DMA((29,)),
    ]
    return call(
        functools.partial(backward_kernel, layer),
        args,
        specs,
        outs,
        out_specs,
        scratch,
        "backward_%d" % layer,
        55_000_000_000,
    )


def swap(block, axis):
    return lax.ppermute(block, axis, [(0, 1), (1, 0)])


def flip(block, mask):
    size = lax.axis_size("replica")
    return lax.ppermute(block, "replica", [(at, at ^ mask) for at in range(size)])


def add_low(left, right):
    return (left.astype(f32) + right.astype(f32)).astype(bf16)


def halves(block, which):
    size = block.shape[0] // 2
    keep = lax.dynamic_slice_in_dim(block, which * size, size, 0)
    send = lax.dynamic_slice_in_dim(block, (1 - which) * size, size, 0)
    return keep, send


def stages_of(bits):
    return [(at,) for at in range(bits)]


def scatter_sum(pieces, stages, rep):
    for (bit,) in stages:
        cut = [halves(piece, (rep >> bit) & 1) for piece in pieces]
        sent = flip(sum_low([send for keep, send in cut]), 1 << bit)
        pieces = [sum_low([keep for keep, send in cut]), sent]
    return sum_low(pieces)


def sum_low(pieces):
    total = pieces[0].astype(f32)
    for piece in pieces[1:]:
        total = total + piece.astype(f32)
    return total.astype(bf16)


def collect(block, stage, rep):
    pieces = [block] + [flip(block, away << stage[0]) for away in range(1, 1 << len(stage))]
    for level in range(len(stage)):
        which = (rep >> stage[level]) & 1
        pieces = [
            in_order(pieces[at], pieces[at + 1], which, 0) for at in range(0, len(pieces), 2)
        ]
    return pieces[0]


def in_order(mine, other, which, dim):
    return jnp.where(
        which == 0,
        jnp.concatenate([mine, other], axis=dim),
        jnp.concatenate([other, mine], axis=dim),
    )


def gather_back(block, order, rep):
    for bit in reversed(order):
        block = in_order(block, flip(block, bit), (rep >> bit) & 1, 0)
    return block


def on_device(
    first_layer_input,
    boundary,
    input_gain,
    in_proj,
    conv_weight,
    conv_bias,
    head_params,
    output_gain,
    out_proj,
    cotangent,
):
    sec = lax.axis_index("section")
    grp = lax.axis_index("group")
    rep = lax.axis_index("replica")
    replicas = lax.axis_size("replica")
    bits = replicas.bit_length() - 1
    order_a = stages_of(bits)
    order_b = order_a[1::-1] + order_a[2:]

    bound = lax.dynamic_index_in_dim(boundary[:, 0], sec, 0, keepdims=False)
    scal = jnp.stack([sec, grp, bound]).astype(jnp.int32)
    u_own = lax.dynamic_index_in_dim(first_layer_input[:, 0], sec, 0, keepdims=False)
    u_far = swap(u_own, "group")
    cot_own = lax.dynamic_index_in_dim(cotangent[:, 0], sec, 0, keepdims=False)

    block = jnp.swapaxes(in_proj, 1, 2)[0]
    far_grp = 1 - grp

    def far_part(which):
        return jnp.concatenate(
            [
                lax.dynamic_slice_in_dim(block, which * DI + far_grp * DH, DH, 0),
                lax.dynamic_slice_in_dim(block, 2 * DI + which * NS, NS, 0),
                lax.dynamic_slice_in_dim(block, DI + CONVC + far_grp * HL, HL, 0),
            ],
            axis=0,
        )

    keep, give = far_part(sec), far_part(1 - sec)
    got = swap(give, "section")
    first_x = swap(jnp.where(sec == 0, keep, got), "group")
    keep, got, cot_own, first_x = lax.optimization_barrier((keep, got, cot_own, first_x))
    second_x = swap(jnp.where(sec == 1, keep, got), "group")
    cot_far = swap(cot_own, "group")
    w_a, w_b = block, swap(block, "section")
    wo_a = out_proj[0]
    wo_b = swap(wo_a, "section")
    weights = [
        (w_a, w_b, w_x, swap(w_x, "section"), wo_a, wo_b) for w_x in (first_x, second_x)
    ]

    width = conv_bias.shape[1]
    half_in = input_gain.shape[1]

    def row_of(*pieces):
        line = jnp.concatenate(pieces)
        return jnp.pad(line, (0, width - line.shape[0]))[None]

    smalls = jnp.concatenate(
        [
            conv_weight[0].T,
            conv_bias,
            row_of(output_gain[0]),
            row_of(input_gain[0], head_params[0].T.reshape(-1)),
            jnp.zeros((1, width), bf16),
        ],
        axis=0,
    )
    both = in_order(smalls[None], swap(smalls, "section")[None], sec, 0)
    far_both = swap(both, "group")
    both = both.astype(f32)
    full = in_order(both, far_both.astype(f32), grp, 2)
    pars, hps = [], []
    for layer in range(2):
        taps = jnp.concatenate(
            [
                lax.dynamic_slice_in_dim(full[layer, 0:5], grp * DH, DH, 1),
                full[layer, 0:5, DI:],
            ],
            axis=1,
        )
        line = both[layer, 6]
        heads = line[half_in : half_in + 3 * HL].reshape(3, HL)
        gain_in = jnp.concatenate(
            [full[layer, 6, :half_in], full[layer, 6, width : width + half_in]]
        )
        rest = jnp.stack([both[layer, 5, :DH], gain_in, jnp.repeat(heads[2], HDIM)])
        pars.append(jnp.concatenate([taps, jnp.pad(rest, ((0, 0), (0, CH - DH)))], axis=0))
        lines = jnp.stack([heads[0], jnp.exp(heads[1]), heads[2]])
        hps.append(jnp.pad(lines, ((0, 5), (0, LANE - HL))))

    tokens = [u_own, u_far]
    cots = [cot_own, cot_far]
    quarter = half_in // 2

    def own_quarter(normed):
        return jnp.concatenate(
            [
                lax.dynamic_slice_in_dim(normed, at * half_in + sec * quarter, quarter, 1)
                for at in range(2)
            ],
            axis=1,
        )

    def own_channels(gated):
        return lax.dynamic_slice_in_dim(gated, sec * (DH // 2), DH // 2, 1)

    def join_in(normed, dproj):
        far_n, far_p = swap(normed, "section"), swap(dproj, "section")
        return (tn(dproj, own_quarter(normed)) + tn(far_p, own_quarter(far_n))).astype(bf16)

    def join_out(gated, upstream):
        far_g, far_u = swap(gated, "section"), swap(upstream, "section")
        return (tn(own_channels(gated), upstream) + tn(own_channels(far_g), far_u)).astype(bf16)

    def guarded(branch, operand):
        shapes = jax.eval_shape(branch, operand)

        def nothing(operand):
            return jax.tree.map(lambda leaf: jnp.zeros(leaf.shape, leaf.dtype), shapes)

        return lax.cond(bound >= 0, branch, nothing, operand)

    u0, proj0, ys0, st0, mix0, unused_sum, stat0 = guarded(
        lambda tokens: run_forward(0, scal, pars[0], hps[0], weights[0], tokens, None), tokens
    )
    stat0_far = swap(stat0, "group")
    p0 = run_project(0, scal, pars[0], wo_a, wo_b, stat0, stat0_far, mix0)
    p0, cot_far = lax.optimization_barrier((p0, cot_far))
    cots = [cot_own, cot_far]
    p0_far = swap(p0.astype(jnp.float16), "group").astype(f32)
    u1, proj1, ys1, st1, mix1, p_total, stat1 = run_forward(
        1, scal, pars[1], hps[1], weights[1], cots, [u0, p0, p0_far]
    )
    stat1_far = swap(stat1, "group")
    piece = u_own.shape[0]

    def own_rows(block):
        return lax.dynamic_slice_in_dim(block, grp * piece, piece, 0)

    def far_rows(block):
        return lax.dynamic_slice_in_dim(block, (1 - grp) * piece, piece, 0)

    scale1 = lax.rsqrt((stat1 + stat1_far)[0] * (1.0 / DI) + EPS)[:, None]
    gated1 = (mix1 * scale1 * pars[1][5:6, :DH]).astype(bf16)
    b1 = join_out(gated1, in_order(cot_own, cot_far, grp, 0))
    stat1_far, b1 = lax.optimization_barrier((stat1_far, b1))
    share = b1.shape[0] // 2
    b1_late = b1[share:]
    b1 = lax.psum(b1[:share], "replica")

    def second_layer(stat1_far):
        n1, dp1, unused_gated, unused_g, dn1, small1 = run_backward(
            1, scal, pars[1], hps[1], weights[1],
            [u1, proj1, ys1, st1, stat1, stat1_far], cots, None,
        )
        dn1_far = swap(dn1, "group")
        dn1_far, a1 = lax.optimization_barrier((dn1_far, join_in(n1, dp1)))
        return dn1, dn1_far, a1, small1

    dn1, dn1_far, a1, small1 = guarded(second_layer, stat1_far)
    a1, b1 = lax.optimization_barrier((a1, b1))
    a1 = lax.psum(a1, "replica")

    def to_sections(first, second):
        held = jnp.where(sec == 0, first, second)
        given = swap(jnp.where(sec == 0, second, first), "section")
        return in_order(held[None], given[None], sec, 0)

    def swap_rows(part_a):
        stay = lax.dynamic_slice_in_dim(part_a, grp * quarter, quarter, 1)
        leave = lax.dynamic_slice_in_dim(part_a, far_grp * quarter, quarter, 1)
        return in_order(stay, swap(leave, "group"), grp, 1)

    def to_owner(block, layer):
        return lax.ppermute(block, "section", [(1 - layer, layer)])

    def gather_back(block, stages):
        for stage in reversed(stages):
            block = collect(block, stage, rep)
        return block

    def first_layer(dn1_far):
        n0, dp0, gated0, g0, dn0, small0 = run_backward(
            0, scal, pars[0], hps[0], weights[0],
            [u0, proj0, ys0, st0, stat0, stat0_far], cots,
            [p_total, u1, dn1, dn1_far, pars[1]],
        )
        a0 = join_in(n0, dp0)
        b0 = jnp.concatenate([join_out(gated0, g0), b1_late], axis=0)
        cut = [halves(block, (rep >> stages[0][0]) & 1) for block, stages in ((a0, order_a), (b0, order_b))]
        cut, dn0, g0, small0, late_gated, late_small = lax.optimization_barrier(
            (cut, dn0, g0, small0, gated1, small1)
        )
        sent = [
            flip(send, 1 << stages[0][0])
            for (keep, send), stages in zip(cut, (order_a, order_b))
        ]
        dn0_far = swap(far_rows(dn0), "group")

        p1 = nn(late_gated, jnp.where(sec == 1, wo_a, wo_b))
        p1_far = swap(far_rows(p1).astype(bf16), "group")
        small = jnp.stack([small0, late_small])
        small = small + swap(small, "section")
        far = swap(small, "group")
        shared = small + far
        own_x = jnp.concatenate([small[:, 0:5, :DH], far[:, 0:5, :LANE]], axis=2)
        own_y = jnp.concatenate([small[:, 0:5, LANE:DH], shared[:, 0:5, DH:]], axis=2)
        conv_part = jnp.where(grp == 0, own_x, own_y)
        gain_in = lax.dynamic_slice_in_dim(shared[:, 6, :DM], grp * half_in, half_in, 1)
        skip = small[:, 7, :DH].reshape(2, HL, HDIM).sum(axis=2)
        line = jnp.concatenate([gain_in, small[:, 8, :HL], small[:, 9, :HL], skip], axis=1)
        packed = jnp.concatenate(
            [
                conv_part,
                jnp.pad(small[:, 5:6, :DH], ((0, 0), (0, 0), (0, width - DH))),
                jnp.pad(line, ((0, 0), (0, width - line.shape[1])))[:, None],
                jnp.zeros((2, 1, width), f32),
            ],
            axis=1,
        )
        sent, dn0_far, p1_far, packed = lax.optimization_barrier((sent, dn0_far, p1_far, packed))
        state = [[keep, came] for (keep, send), came in zip(cut, sent)]
        values = u_own.astype(f32)
        scale = lax.rsqrt(jnp.mean(values * values, axis=-1, keepdims=True) + EPS)
        arrived = (own_rows(dn0).astype(f32) + dn0_far.astype(f32)) * pars[0][6:7, :DM]
        inner = jnp.mean(arrived * values, axis=-1, keepdims=True)
        grad1 = own_rows(g0)
        grad0 = (
            grad1.astype(f32) + scale * arrived - values * (scale * scale * scale * inner)
        ).astype(bf16)

        input_grad = to_sections(grad0, grad1)
        out0 = own_rows(u1)
        out1 = (out0.astype(f32) + own_rows(p1) + p1_far.astype(f32)).astype(bf16)
        segment_output = to_sections(out0, out1)
        for at in range(1, bits):
            cut = [
                [halves(piece, (rep >> stages[at][0]) & 1) for piece in pieces]
                for pieces, stages in zip(state, (order_a, order_b))
            ]
            sent = [
                flip(sum_low([send for keep, send in pair]), 1 << stages[at][0])
                for pair, stages in zip(cut, (order_a, order_b))
            ]
            far_packed = flip(packed, 1 << at)
            state = [
                [sum_low([keep for keep, send in pair]), came] for pair, came in zip(cut, sent)
            ]
            state, far_packed = lax.optimization_barrier((state, far_packed))
            packed = packed + far_packed
        a0, b0 = sum_low(state[0]), sum_low(state[1])
        far_packed = flip(packed, 1)
        a0 = swap_rows(a0)
        a0, far_packed = lax.optimization_barrier((a0, far_packed))
        packed = packed + far_packed
        a0, b0 = gather_back(a0, order_a[1:]), gather_back(b0, order_b[1:])
        packed = jnp.where(sec == 0, packed[0], packed[1])
        heads = packed[6, half_in : half_in + 3 * HL].reshape(3, HL)
        smalls = (packed[6:7, :half_in], packed[0:4], packed[4:5], heads, packed[5:6, :DH])
        return segment_output, input_grad, smalls, a0, b0

    segment_output, input_grad, smalls, a0, b0 = guarded(first_layer, dn1_far)
    a0_far = flip(a0, 1 << order_a[0][0])
    b0 = collect(b0, order_b[0], rep)
    came = swap(lax.dynamic_slice_in_dim(a1, far_grp * quarter, quarter, 1), "group")
    side = (rep >> order_a[0][0]) & 1
    grad_in_proj, grad_out_proj = run_assemble(
        jnp.stack([sec, grp, side]).astype(jnp.int32),
        [to_owner(a0, 0), to_owner(a0_far, 0), swap(b0, "section")],
        [a0, a0_far, b0],
        [a1, to_owner(a1, 1), came, to_owner(came, 1), b1, to_owner(b1, 1)],
        in_proj.shape[2],
    )
    grad_in_proj = jnp.swapaxes(grad_in_proj, 0, 1)
    return (
        segment_output[None, :, None],
        input_grad[None, :, None],
        smalls[0],
        grad_in_proj[None],
        smalls[1].T[None],
        smalls[2],
        smalls[3].T[None],
        smalls[4],
        grad_out_proj[None],
    )


def solution(mesh):
    placed = (
        P(None, "replica", "group", None),
        P(None, "replica"),
        P("section", "group"),
        P("section", "group", None),
        P("section", "group", None),
        P("section", "group"),
        P("section", "group", None),
        P("section", "group"),
        P("section", "group", None),
        P(None, "replica", "group", None),
    )
    return jax.shard_map(
        on_device,
        mesh=mesh,
        in_specs=placed,
        out_specs=(
            P("section", None, "replica", "group", None),
            P("section", None, "replica", "group", None),
            P("section", "group"),
            P("section", "group", None),
            P("section", "group", None),
            P("section", "group"),
            P("section", "group", None),
            P("section", "group"),
            P("section", "group", None),
        ),
        check_vma=False,
    )
```

```python
import functools

import jax
import jax.numpy as jnp
from jax import lax
from jax.experimental import pallas as pl
from jax.experimental.pallas import tpu as pltpu
from jax.sharding import PartitionSpec as P

DM = 1024
HEADS = 32
HDIM = 64
NS = 128
KW = 4
DI = 2048
CONVC = 2304
HL = HEADS // 2
DH = DI // 2
CH = DH + 2 * NS
CP = DH + CH + 128
LANE = 128
TILE = 256
RC = 64
HEAD_ROWS = 8
EPS = 1e-05
VMEM_BYTES = 63 * 1024 * 1024

f32 = jnp.float32
bf16 = jnp.bfloat16


def nn(left, right):
    return jnp.dot(left, right, preferred_element_type=f32)


def nt(left, right):
    return lax.dot_general(left, right, (((1,), (1,)), ((), ())), preferred_element_type=f32)


def tn(left, right):
    return lax.dot_general(left, right, (((0,), (0,)), ((), ())), preferred_element_type=f32)


def tile_at(index, size):
    return pl.ds(pl.multiple_of(index * size, size), size)


def loop(count, body):
    def step(index, carry):
        body(index)
        return carry

    lax.fori_loop(0, count, step, 0)


def iota(shape, dim):
    return lax.broadcasted_iota(jnp.int32, shape, dim)


def sigmoid(values):
    return 0.5 * jnp.tanh(0.5 * values) + 0.5


def softplus(values):
    small = jnp.exp(-jnp.abs(values))
    series = small * (1.0 - small * (0.5 - small * (1.0 / 3.0 - small * 0.25)))
    return jnp.maximum(values, 0.0) + jnp.where(small < 0.03, series, jnp.log(1.0 + small))


def split3(values):
    high = values.astype(bf16)
    rest = values - high.astype(f32)
    middle = rest.astype(bf16)
    low = (rest - middle.astype(f32)).astype(bf16)
    return high, middle, low


def pack3(values):
    high, middle, low = split3(values)
    packed = (
        high.astype(f32)
        + pltpu.roll(middle.astype(f32), HL, 1)
        + pltpu.roll(low.astype(f32), 2 * HL, 1)
    )
    return packed.astype(bf16)


def fill_spread(spread_s, width):
    shape = spread_s.shape
    row = iota(shape, 0)
    col = iota(shape, 1)
    hit = (row < 3 * HL) & ((row & (HL - 1)) == col // width)
    spread_s[...] = jnp.where(hit, 1.0, 0.0).astype(bf16)


def fill_gather(gather_s):
    shape = gather_s.shape
    hit = iota(shape, 0) // HDIM == iota(shape, 1)
    gather_s[...] = jnp.where(hit, 1.0, 0.0).astype(bf16)


def head_sums(values, gather_s):
    high = values.astype(bf16)
    low = (values - high.astype(f32)).astype(bf16)
    rows = values.shape[0]
    both = nn(jnp.concatenate([high, low], axis=0), gather_s[...])
    return both[:rows] + both[rows:]


def seam(bound, back, rows, align, count):
    first = jnp.clip(bound - back, 0, count - rows)
    return pl.multiple_of(first - lax.rem(first, align), align)


def seam_masks(first, rows, bound):
    pos = iota((rows, LANE), 0) + first
    masks = []
    for lag in range(1, KW):
        anchor = pos - lag
        dropped = (anchor < 0) | ((anchor < bound) & (bound <= pos))
        masks.append(jnp.where(dropped, 0.0, 1.0))
    return masks


def conv_phase(proj_s, par, bound, conv_s, pre_s, count):
    first = seam(bound, 0, 16, 8, count)
    masks = seam_masks(first, 16, bound)
    seam_rows = pl.ds(first, 16)

    def body(index):
        src = pl.ds(pl.multiple_of(DH + index * LANE, LANE), LANE)
        dst = tile_at(index, LANE)
        taps = par[0:8, dst]
        for at in range(0, count, 64):
            pre = taps[4:5] + taps[3:4] * proj_s[HEAD_ROWS + at : HEAD_ROWS + at + 64, src]
            for lag in range(1, KW):
                begin = HEAD_ROWS + at - lag
                pre = pre + taps[3 - lag : 4 - lag] * proj_s[begin : begin + 64, src]
            if pre_s is not None:
                pre_s[at : at + 64, dst] = pre
            conv_s[at : at + 64, dst] = pre * sigmoid(pre)
        window = proj_s[pl.ds(first, 16 + HEAD_ROWS), src]
        pre = taps[4:5] + taps[3:4] * window[HEAD_ROWS:]
        for lag in range(1, KW):
            part = window[HEAD_ROWS - lag : HEAD_ROWS - lag + 16] * masks[lag - 1]
            pre = pre + taps[3 - lag : 4 - lag] * part
        if pre_s is not None:
            pre_s[seam_rows, dst] = pre
        conv_s[seam_rows, dst] = pre * sigmoid(pre)

    loop(CH // LANE, body)


def step_phase(proj_s, hp, dt_s, rate_s, cs_s, cst_s, count):
    span = count // 2
    lanes = iota((count, LANE), 1)
    raw = proj_s[HEAD_ROWS : HEAD_ROWS + count, DH + CH : CP] + hp[0:1, :]
    step = jnp.where(lanes < HL, softplus(raw), 0.0)
    rate = -step * hp[1:2, :]
    dt_s[...] = step
    rate_s[...] = rate
    lower = jnp.where(iota((span, span), 0) >= iota((span, span), 1), 1.0, 0.0).astype(bf16)
    for block in range(2):
        rows = slice(block * span, (block + 1) * span)
        triple = jnp.concatenate(split3(rate[rows]), axis=1)
        sums = nn(lower, triple)
        total = sums[:, :LANE] + sums[:, LANE : 2 * LANE] + sums[:, 2 * LANE :]
        cs_s[rows] = total
        cst_s[block] = jnp.transpose(total)


def scaled_inputs(conv_s, dt_s, spread_s, xdt_s, xlo_s, count):
    def body(index):
        rows = tile_at(index, RC * 2)
        scale = nn(pack3(dt_s[rows]), spread_s[...])
        v = conv_s[rows, :DH] * scale
        xdt_s[rows] = v.astype(bf16)
        xlo_s[rows] = (v - v.astype(bf16).astype(f32)).astype(bf16)

    loop(count // (RC * 2), body)


def tail_weight(cs_s, bound, span):
    total = cs_s[0:span]
    pos = iota((span, LANE), 0)
    cut = (pos < bound) & (bound <= span - 1)
    lanes = iota((span, LANE), 1)
    keep = jnp.logical_not(cut) & (lanes < HL)
    return jnp.where(keep, jnp.exp(total[span - 1 : span] - total), 0.0)


def carry_weight(cs_s, bound, span):
    total = cs_s[span : 2 * span]
    pos = iota((span, LANE), 0) + span
    fresh = (span <= bound) & (bound <= pos)
    lanes = iota((span, LANE), 1)
    keep = jnp.logical_not(fresh) & (lanes < HL)
    return jnp.where(keep, jnp.exp(total), 0.0)


def inside_mask(block, bound, span, flipped):
    shape = (span, span)
    later = iota(shape, 1 if flipped else 0) + block * span
    early = iota(shape, 0 if flipped else 1) + block * span
    keep = (later >= early) & jnp.logical_not((early < bound) & (bound <= later))
    return jnp.where(keep, 1.0, 0.0)


def split2(values):
    high = values.astype(bf16)
    return high, (values - high.astype(f32)).astype(bf16)


def nt3(left, right):
    left_high, left_low = split2(left)
    right_high, right_low = split2(right)
    return nt(
        jnp.concatenate([left_high, left_low, left_high], axis=1),
        jnp.concatenate([right_high, right_high, right_low], axis=1),
    )


def nn3(left, right):
    left_high, left_low = split2(left)
    right_high, right_low = split2(right)
    return nn(
        jnp.concatenate([left_high, left_low, left_high], axis=1),
        jnp.concatenate([right_high, right_high, right_low], axis=0),
    )


def mix_tokens(first, second, high, low):
    rows = first.shape[0]
    first_high, first_low = split2(first)
    second_high, second_low = split2(second)
    stacked = jnp.concatenate([first_high, second_high, first_low, second_low], axis=0)
    both = nn(stacked, jnp.concatenate([high, low], axis=1))
    left, right = both[:, :LANE], both[:, LANE:]
    total = left[: 2 * rows] + right[: 2 * rows] + left[2 * rows :]
    keep = iota((rows, LANE), 1) < HDIM
    return jnp.where(keep, total[:rows], total[rows:])


def copies(pairs, sems, base):
    return [
        pltpu.make_async_copy(src, dst, sems.at[base + at]) for at, (src, dst) in enumerate(pairs)
    ]


def load_outer(layer, sec, wo_a, wo_b, wo_s, sem):
    held = pltpu.make_async_copy(wo_a, wo_s, sem)
    given = pltpu.make_async_copy(wo_b, wo_s, sem)

    @pl.when(sec == layer)
    def _():
        held.start()

    @pl.when(sec != layer)
    def _():
        given.start()

    return held


def load_weights(layer, sec, grp, w_a, w_b, w_x, w_y, w_s, sems):
    width = w_a.shape[1]
    mine = pl.ds(pl.multiple_of(grp * width, width), width)
    other = pl.ds(pl.multiple_of((1 - grp) * width, width), width)
    first = pl.multiple_of(grp * DH, DH)
    steps = pl.multiple_of(DI + CONVC + grp * HL, HL)
    places = [
        (pl.ds(first, DH), pl.ds(0, DH)),
        (pl.ds(DI + first, DH), pl.ds(DH, DH)),
        (pl.ds(2 * DI, 2 * NS), pl.ds(2 * DH, 2 * NS)),
        (pl.ds(steps, HL), pl.ds(DH + CH, HL)),
    ]
    w_s[DH + CH + HL : CP] = jnp.zeros((LANE - HL, 2 * width), bf16)

    def pieces(block):
        return copies([(block.at[src], w_s.at[dst, mine]) for src, dst in places], sems, 0)

    held, given = pieces(w_a), pieces(w_b)

    @pl.when(sec == layer)
    def _():
        for copy in held:
            copy.start()

    @pl.when(sec != layer)
    def _():
        for copy in given:
            copy.start()

    pairs = []
    for part, which in ((w_x, sec), (w_y, 1 - sec)):
        wide = pl.ds(pl.multiple_of(which * DH, DH), DH)
        thin = pl.ds(pl.multiple_of(2 * DH + which * NS, NS), NS)
        pairs.append((part.at[pl.ds(0, DH)], w_s.at[wide, other]))
        pairs.append((part.at[pl.ds(DH, NS)], w_s.at[thin, other]))
    pairs.append((w_x.at[pl.ds(DH + NS, HL)], w_s.at[pl.ds(DH + CH, HL), other]))
    far = copies(pairs, sems, 24)
    for copy in far:
        copy.start()
    return held + far


def column_of(stat_ref, hold_s):
    hold_s[...] = jnp.zeros_like(hold_s)
    hold_s[0:8] = stat_ref[...]
    return jnp.transpose(hold_s[...])


def forward_kernel(layer, *refs):
    (scal, par, hp, w_a, w_b, w_x, w_y, wo_a, wo_b) = refs[:9]
    if layer == 0:
        in_own, in_far = refs[9:11]
        rest = refs[11:]
    else:
        u_prev, p_own, p_far, in_own, in_far = refs[9:14]
        rest = refs[14:]
    (u_out, proj_out, ys_out, st_out, mix_out, sum_out, stat_out) = rest[:7]
    (w_s, wo_s, u_s, n_s, proj_s, conv_s, dt_s, rate_s, cs_s, cst_s, xdt_s,
     y_s, mix_s, st_s, pp_s, g_s, spread_s, stat_s, hold_s, in_s, xlo_s, sems) = rest[7:]
    sec, grp, bound = scal[0], scal[1], scal[2]
    count = u_s.shape[0]
    span = count // 2
    piece = count // 2
    place_own = pl.ds(pl.multiple_of(grp * piece, piece), piece)
    place_far = pl.ds(pl.multiple_of((1 - grp) * piece, piece), piece)
    token_target = u_s if layer == 0 else in_s
    token_in = copies(
        [(in_own, token_target.at[place_own]), (in_far, token_target.at[place_far])], sems, 8
    )
    if layer == 0:
        for copy in token_in:
            copy.start()
    else:
        more = copies([(u_prev, u_s), (p_own, pp_s.at[0]), (p_far, pp_s.at[1])], sems, 10)
        for copy in more:
            copy.start()
    w_in = load_weights(layer, sec, grp, w_a, w_b, w_x, w_y, w_s, sems)
    if layer == 1:
        for copy in token_in:
            copy.start()
        wo_in = load_outer(layer, sec, wo_a, wo_b, wo_s, sems.at[4])
    fill_spread(spread_s, HDIM)
    proj_s[0:HEAD_ROWS] = jnp.zeros((HEAD_ROWS, CP), f32)
    gain_in = par[6:7, :DM]
    if layer == 0:
        for copy in token_in:
            copy.wait()
    else:
        for copy in more:
            copy.wait()

    def norm_rows(index):
        rows = tile_at(index, RC)
        values = u_s[rows].astype(f32)
        if layer == 1:
            total = pp_s[0, rows] + pp_s[1, rows]
            pp_s[0, rows] = total
            low = (values + total).astype(bf16)
            u_s[rows] = low
            values = low.astype(f32)
        scale = lax.rsqrt(jnp.mean(values * values, axis=-1, keepdims=True) + EPS)
        n_s[rows] = (values * scale * gain_in).astype(bf16)

    loop(count // RC, norm_rows)
    out_sum = None
    if layer == 1:
        out_sum = pltpu.make_async_copy(pp_s.at[0], sum_out, sems.at[18])
        out_sum.start()
    out_u = pltpu.make_async_copy(u_s, u_out, sems.at[13])
    out_u.start()
    for copy in w_in:
        copy.wait()

    body_rows = slice(HEAD_ROWS, HEAD_ROWS + count)

    def project(index):
        lane = tile_at(index, TILE)
        proj_s[body_rows, lane] = nt(n_s[...], w_s[lane, :])

    loop(CP // TILE, project)
    proj_s[body_rows, CP - LANE : CP] = nt(n_s[...], w_s[CP - LANE : CP, :])
    out_proj = pltpu.make_async_copy(proj_s, proj_out, sems.at[14])
    out_proj.start()

    conv_phase(proj_s, par, bound, conv_s, None, count)
    step_phase(proj_s, hp, dt_s, rate_s, cs_s, cst_s, count)
    scaled_inputs(conv_s, dt_s, spread_s, xdt_s, xlo_s, count)

    skip = par[7:8, :DH]
    gain_out = par[5:6, :DH]
    lanes = iota((RC, LANE), 1)

    def mix_rows(index):
        rows = tile_at(index, RC)
        shifted_rows = pl.ds(pl.multiple_of(HEAD_ROWS + index * RC, HEAD_ROWS), RC)
        gate = proj_s[shifted_rows, :DH]
        value = y_s[rows] + skip * conv_s[rows, :DH]
        y_s[rows] = value
        mixed = value * (gate * sigmoid(gate))
        conv_s[rows, :DH] = mixed
        if layer == 1:
            mix_s[rows] = (mixed * gain_out).astype(bf16)
        square = jnp.sum(mixed * mixed, axis=-1, keepdims=True)
        stat_s[rows] = jnp.where(lanes == 0, square, 0.0)

    flushed = []
    for block in range(2):
        rows = slice(block * span, (block + 1) * span)
        low_b = conv_s[rows, DH : DH + NS].astype(bf16)
        low_c = conv_s[rows, DH + NS : CH].astype(bf16)
        g_s[...] = nt3(conv_s[rows, DH + NS : CH], conv_s[rows, DH : DH + NS]) * inside_mask(block, bound, span, False)

        def pair(index):
            lane = tile_at(index, LANE)
            near = xdt_s[rows, lane]
            near_low = xlo_s[rows, lane]
            turned_cs = pltpu.roll(cs_s[rows], lax.rem(LANE - 2 * index, LANE), 1)
            for at in range(0, span, LANE):
                size = at + LANE
                here = slice(block * span + at, block * span + at + LANE)
                mixings = []
                for side in range(2):
                    head = 2 * index + side
                    col = jnp.broadcast_to(turned_cs[at : at + LANE, side : side + 1], (LANE, LANE))
                    line = cst_s[block, pl.ds(head, 1), :][:, :size]
                    wide = jnp.concatenate([col] * (size // LANE), axis=1)
                    decay = jnp.exp(jnp.minimum(wide - line, 0.0))
                    mixings.append(decay * g_s[at : at + LANE, :size])
                y_s[here, lane] = mix_tokens(*mixings, near[:size], near_low[:size])

        loop(HL // 2, pair)
        if block == 0:
            weight = pack3(tail_weight(cs_s, bound, span))
            turned = jnp.transpose(conv_s[rows, DH : DH + NS])

            def state_tile(index):
                lane = tile_at(index, TILE)
                scaled = (xdt_s[rows, lane].astype(f32) + xlo_s[rows, lane].astype(f32)) * nn(weight, spread_s[:, lane])
                st_s[:, lane] = nn3(turned, scaled)

            loop(DH // TILE, state_tile)
        else:
            weight = pack3(carry_weight(cs_s, bound, span))

            def carry_tile(index):
                lane = tile_at(index, TILE)
                carried = nn3(conv_s[rows, DH + NS : CH], st_s[:, lane])
                y_s[rows, lane] += carried * nn(weight, spread_s[:, lane])

            loop(DH // TILE, carry_tile)
        first_tile = block * (span // RC)
        loop(span // RC, lambda index: mix_rows(first_tile + index))
        flushed += copies(
            [
                (y_s.at[rows], ys_out.at[rows]),
                (conv_s.at[rows, pl.ds(0, DH)], mix_out.at[rows]),
            ],
            sems,
            16 if block == 0 else 20,
        )
        for copy in flushed[-2:]:
            copy.start()
    out_st = pltpu.make_async_copy(st_s, st_out, sems.at[15])
    out_st.start()

    if layer == 1:
        wo_in.wait()
        for copy in token_in:
            copy.wait()

        def out_tile(index):
            lane = tile_at(index, TILE)
            partial = nn(mix_s[...], wo_s[:, lane])
            dots = jnp.sum(partial * in_s[:, lane].astype(f32), axis=-1, keepdims=True)
            stat_s[...] += jnp.where(iota((count, LANE), 1) == 1, dots, 0.0)

        loop(DM // TILE, out_tile)
    stat_out[...] = jnp.transpose(stat_s[...])[0:8]
    for copy in (out_u, out_proj, out_st, *flushed):
        copy.wait()
    if layer == 1:
        out_sum.wait()


def backward_kernel(layer, *refs):
    (scal, par, hp, w_a, w_b, w_x, w_y, wo_a, wo_b) = refs[:9]
    (u_in, proj_in, ys_in, st_in, stat_own, stat_far, in_own, in_far) = refs[9:17]
    if layer == 1:
        rest = refs[17:]
    else:
        p_sum, up_in, dn_own, dn_far, par_up = refs[17:22]
        rest = refs[22:]
    (n_out, dp_out, gated_out, g_out, dn_out, small_out) = rest[:6]
    (w_s, wo_s, u_s, n_s, proj_s, conv_s, pre_s, dt_s, rate_s, cs_s, cst_s, grad_cs_s, xdt_s,
     y_s, st_s, ad_s, pp_s, dn_s, g_s, up_s, gg_s, dys_s, dx_s, dpre_s, dp_s, gm_s, dg_s,
     spread_s, gather_s, stat_s, hold_s, xlo_s, dlo_s, sems) = rest[6:]
    sec, grp, bound = scal[0], scal[1], scal[2]
    count = u_s.shape[0]
    span = count // 2
    piece = count // 2
    place_own = pl.ds(pl.multiple_of(grp * piece, piece), piece)
    place_far = pl.ds(pl.multiple_of((1 - grp) * piece, piece), piece)
    token_in = copies([(in_own, g_s.at[place_own]), (in_far, g_s.at[place_far])], sems, 8)
    saved_in = copies([(u_in, u_s), (proj_in, proj_s), (ys_in, y_s), (st_in, st_s)], sems, 10)
    for copy in token_in:
        copy.start()
    if layer == 0:
        more = copies(
            [
                (dn_own, dn_s.at[0]),
                (dn_far, dn_s.at[1]),
                (up_in, up_s),
                (p_sum, pp_s),
            ],
            sems,
            14,
        )
        for copy in more:
            copy.start()
    wo_in = load_outer(layer, sec, wo_a, wo_b, wo_s, sems.at[4])
    for copy in saved_in[1:]:
        copy.start()
    fill_spread(spread_s, HDIM)
    fill_gather(gather_s)
    stats = column_of(stat_own, hold_s) + column_of(stat_far, hold_s)
    stat_s[...] = stats
    for copy in token_in:
        copy.wait()
    lane_rc = iota((RC, LANE), 1)
    if layer == 0:
        for copy in more:
            copy.wait()
        gain_up = par_up[6:7, :DM]

        def upstream_rows(index):
            rows = tile_at(index, RC)
            values = up_s[rows].astype(f32)
            scale = lax.rsqrt(jnp.mean(values * values, axis=-1, keepdims=True) + EPS)
            arrived = (dn_s[0, rows].astype(f32) + dn_s[1, rows].astype(f32)) * gain_up
            inner = jnp.mean(arrived * values, axis=-1, keepdims=True)
            total = g_s[rows].astype(f32) + scale * arrived - values * (scale * scale * scale * inner)
            low = total.astype(bf16)
            g_s[rows] = low
            dots = jnp.sum(low.astype(f32) * pp_s[rows], axis=-1, keepdims=True)
            stat_s[rows] = jnp.where(lane_rc == 1, dots, stat_s[rows])

        loop(count // RC, upstream_rows)
    out_g = pltpu.make_async_copy(g_s, g_out, sems.at[19])
    out_g.start()
    wo_in.wait()

    def gated_tile(index):
        lane = tile_at(index, TILE)
        gg_s[:, lane] = nt(g_s[...], wo_s[lane, :])

    loop(DH // TILE, gated_tile)
    for copy in saved_in[1:]:
        copy.wait()
    w_in = load_weights(layer, sec, grp, w_a, w_b, w_x, w_y, w_s, sems)
    saved_in[0].start()

    conv_phase(proj_s, par, bound, conv_s, pre_s, count)
    step_phase(proj_s, hp, dt_s, rate_s, cs_s, cst_s, count)
    scaled_inputs(conv_s, dt_s, spread_s, xdt_s, xlo_s, count)

    skip = par[7:8, :DH]
    gain_out = par[5:6, :DH]
    gain_in = par[6:7, :DM]

    def fold(values):
        return jnp.sum(values.reshape(-1, 8, values.shape[-1]), axis=0)

    def mix_rows(index, carry):
        gain_sum, skip_sum = carry
        rows = tile_at(index, RC)
        shifted_rows = pl.ds(pl.multiple_of(HEAD_ROWS + index * RC, HEAD_ROWS), RC)
        scale = lax.rsqrt(stat_s[rows, 0:1] * (1.0 / DI) + EPS)
        inner = stat_s[rows, 1:2] * (scale * scale * (1.0 / DI))
        if layer == 1:
            inner = inner * scale
        gate = proj_s[shifted_rows, :DH]
        gate_sig = sigmoid(gate)
        gate_act = gate * gate_sig
        value = y_s[rows]
        grad = gg_s[rows]
        mixed = value * gate_act
        scaled = mixed * scale
        dmixed = grad * gain_out * scale - mixed * inner
        mixed_low = (scaled * gain_out).astype(bf16)
        gated_s[rows] = mixed_low
        dys = dmixed * gate_act
        dgate = dmixed * value * (gate_sig + gate_act * (1.0 - gate_sig))
        dp_s[rows, :DH] = dgate.astype(bf16)
        inputs = conv_s[rows, :DH]
        gg_s[rows] = dys
        low = dys.astype(bf16)
        dys_s[rows] = low
        dlo_s[rows] = (dys - low.astype(f32)).astype(bf16)
        y_s[rows] = dys * (value - skip * inputs)
        return (gain_sum + fold(grad * scaled), skip_sum + fold(dys * inputs))

    gated_s = n_s
    zero = jnp.zeros((8, DH), f32)
    gain_sum, skip_sum = lax.fori_loop(0, count // RC, mix_rows, (zero, zero))
    small_out[...] = jnp.zeros_like(small_out)
    small_out[5:6, :DH] = jnp.sum(gain_sum, axis=0, keepdims=True)
    small_out[7:8, :DH] = jnp.sum(skip_sum, axis=0, keepdims=True)
    out_gated = pltpu.make_async_copy(n_s, gated_out, sems.at[20])
    out_gated.start()

    lane_left = iota((span, LANE), 1) < HDIM
    for block in (1, 0):
        rows = slice(block * span, (block + 1) * span)
        low_b = conv_s[rows, DH : DH + NS].astype(bf16)
        low_c = conv_s[rows, DH + NS : CH].astype(bf16)
        keep = inside_mask(block, bound, span, True)
        gm_s[...] = nt3(conv_s[rows, DH : DH + NS], conv_s[rows, DH + NS : CH]) * keep
        dg_s[...] = jnp.zeros_like(dg_s)

        def pair(index):
            lane = tile_at(index, LANE)
            near = xdt_s[rows, lane]
            far = dys_s[rows, lane]
            far_low = dlo_s[rows, lane]
            turned_cs = pltpu.roll(cs_s[rows], lax.rem(LANE - 2 * index, LANE), 1)
            for at in range(0, span, LANE):
                size = span - at
                here = slice(block * span + at, block * span + at + LANE)
                part = near[at : at + LANE]
                mixings, decays, parts = [], [], []
                for side in range(2):
                    head = 2 * index + side
                    col = jnp.broadcast_to(turned_cs[at : at + LANE, side : side + 1], (LANE, LANE))
                    line = cst_s[block, pl.ds(head, 1), :][:, at:]
                    wide = jnp.concatenate([col] * (size // LANE), axis=1)
                    decay = jnp.exp(jnp.minimum(line - wide, 0.0))
                    decays.append(decay)
                    mixings.append(decay * gm_s[at : at + LANE, at:])
                    mine = lane_left[:LANE] if side == 0 else jnp.logical_not(lane_left[:LANE])
                    parts.append(jnp.where(mine, part.astype(f32), 0.0).astype(bf16))
                dx_s[here, lane] = mix_tokens(*mixings, far[at:], far_low[at:])
                pairs = nt(jnp.concatenate(parts, axis=0), far[at:])
                dg_s[at : at + LANE, at:] += pairs[:LANE] * decays[0] + pairs[LANE:] * decays[1]

        loop(HL // 2, pair)
        grad_g = dg_s[...] * keep
        dpre_s[rows, DH : DH + NS] = nn(grad_g.astype(bf16), low_c)
        dpre_s[rows, DH + NS : CH] = nn(jnp.transpose(grad_g).astype(bf16), low_b)
        if block == 1:
            weight = pack3(carry_weight(cs_s, bound, span))
            turned_c = jnp.transpose(conv_s[rows, DH + NS : CH])

            def carry_tile(index):
                lane = tile_at(index, TILE)
                scaled = (dys_s[rows, lane].astype(f32) + dlo_s[rows, lane].astype(f32)) * nn(weight, spread_s[:, lane])
                ad_s[:, lane] = nn3(turned_c, scaled)
                dpre_s[rows, DH + NS : CH] += nt3(scaled, st_s[:, lane])

            loop(DH // TILE, carry_tile)
        else:
            weight = pack3(tail_weight(cs_s, bound, span))

            def state_tile(index):
                lane = tile_at(index, TILE)
                scale = nn(weight, spread_s[:, lane])
                low_a = ad_s[:, lane]
                inputs = xdt_s[rows, lane].astype(f32) + xlo_s[rows, lane].astype(f32)
                extra = nn3(conv_s[rows, DH : DH + NS], low_a) * scale
                dx_s[rows, lane] += extra
                both = inputs * scale
                pre_tail = jnp.sum(fold(inputs * extra), axis=0, keepdims=True)
                dpre_s[count : count + 1, lane] = pre_tail
                dpre_s[rows, DH : DH + NS] += nt3(both, low_a)

            loop(DH // TILE, state_tile)

    def head_rows(index):
        chunk = RC * 2
        rows = tile_at(index, chunk)
        steps = dt_s[rows]
        scale = nn(pack3(steps), spread_s[...])
        grad = dx_s[rows]
        sums = head_sums(jnp.concatenate([conv_s[rows, :DH] * grad, y_s[rows]], axis=0), gather_s)
        per_step = sums[:chunk]
        stat_s[rows] = per_step
        grad_cs_s[rows] = sums[chunk:] - steps * per_step
        dpre_s[rows, :DH] = gg_s[rows] * skip + grad * scale

    loop(count // (RC * 2), head_rows)
    tail = jnp.broadcast_to(dpre_s[count : count + 1, :DH], (8, DH))
    tail_heads = head_sums(tail, gather_s)[0:1]
    last = iota((span, LANE), 0) == span - 1
    upper = jnp.where(iota((span, span), 0) <= iota((span, span), 1), 1.0, 0.0).astype(bf16)
    bias_sum = jnp.zeros((1, LANE), f32)
    decay_sum = jnp.zeros((1, LANE), f32)
    for block in range(2):
        rows = slice(block * span, (block + 1) * span)
        raw = proj_s[HEAD_ROWS + block * span : HEAD_ROWS + (block + 1) * span, DH + CH : CP]
        grad_cs = grad_cs_s[rows]
        if block == 0:
            grad_cs = grad_cs + jnp.where(last, tail_heads, 0.0)
        sums = nn(upper, jnp.concatenate(split3(grad_cs), axis=1))
        grad_rate = sums[:, :LANE] + sums[:, LANE : 2 * LANE] + sums[:, 2 * LANE :]
        grad_step = stat_s[rows] - grad_rate * hp[1:2, :]
        lanes = iota((span, LANE), 1)
        grad_raw = jnp.where(lanes < HL, grad_step * sigmoid(raw + hp[0:1, :]), 0.0)
        dp_s[rows, DH + CH : CP] = grad_raw.astype(bf16)
        bias_sum = bias_sum + jnp.sum(grad_raw, axis=0, keepdims=True)
        decay_sum = decay_sum + jnp.sum(grad_rate * rate_s[rows], axis=0, keepdims=True)
    small_out[8:9, :LANE] = bias_sum
    small_out[9:10, :LANE] = decay_sum

    dpre_s[count : count + 8] = jnp.zeros((8, CH), f32)

    first = seam(bound, 0, 16, 8, count)
    masks = seam_masks(first, 16, bound)
    back = seam(bound, KW - 1, 32, 16, count)
    back_masks = seam_masks(back, 40, bound)

    def conv_back(index):
        src = pl.ds(pl.multiple_of(DH + index * LANE, LANE), LANE)
        dst = tile_at(index, LANE)
        taps = par[0:8, dst]
        sums = [jnp.zeros((8, LANE), f32) for _ in range(KW + 1)]
        for at in range(0, count, 64):
            pre = pre_s[at : at + 64, dst]
            sig = sigmoid(pre)
            grad = dpre_s[at : at + 64, dst] * (sig + pre * sig * (1.0 - sig))
            dpre_s[at : at + 64, dst] = grad
            sums[4] = sums[4] + fold(grad)
            for lag in range(KW):
                begin = HEAD_ROWS + at - lag
                sums[3 - lag] = sums[3 - lag] + fold(grad * proj_s[begin : begin + 64, src])
        window = proj_s[pl.ds(first, 16 + HEAD_ROWS), src]
        grad = dpre_s[pl.ds(first, 16), dst]
        for lag in range(1, KW):
            part = window[HEAD_ROWS - lag : HEAD_ROWS - lag + 16] * (1.0 - masks[lag - 1])
            sums[3 - lag] = sums[3 - lag] - fold(grad * part)
        for at in range(0, count, 64):
            total = taps[3:4] * dpre_s[at : at + 64, dst]
            for lag in range(1, KW):
                begin = at + lag
                total = total + taps[3 - lag : 4 - lag] * dpre_s[begin : begin + 64, dst]
            dp_s[at : at + 64, src] = total.astype(bf16)
        window = dpre_s[pl.ds(back, 40), dst]
        total = taps[3:4] * window[:32]
        for lag in range(1, KW):
            part = window[lag : lag + 32] * back_masks[lag - 1][lag : lag + 32]
            total = total + taps[3 - lag : 4 - lag] * part
        dp_s[pl.ds(back, 32), src] = total.astype(bf16)
        for at in range(KW + 1):
            small_out[at : at + 1, dst] = jnp.sum(sums[at], axis=0, keepdims=True)

    loop(CH // LANE, conv_back)
    out_dp = pltpu.make_async_copy(dp_s, dp_out, sems.at[21])
    out_dp.start()
    for copy in w_in:
        copy.wait()
    saved_in[0].wait()

    def normed_tile(index):
        lane = tile_at(index, TILE)
        gg_s[:, lane] = nn(dp_s[...], w_s[:, lane])

    loop(DM // TILE, normed_tile)
    out_gated.wait()

    def norm_rows(index, gain_sum):
        rows = tile_at(index, RC)
        values = u_s[rows].astype(f32)
        scale = lax.rsqrt(jnp.mean(values * values, axis=-1, keepdims=True) + EPS)
        unit = values * scale
        n_s[rows] = (unit * gain_in).astype(bf16)
        grad = gg_s[rows]
        dys_s[rows] = grad.astype(bf16)
        return gain_sum + fold(grad * unit)

    gain_total = lax.fori_loop(0, count // RC, norm_rows, jnp.zeros((8, DM), f32))
    small_out[6:7, :DM] = jnp.sum(gain_total, axis=0, keepdims=True)
    out_n = pltpu.make_async_copy(n_s, n_out, sems.at[22])
    out_dn = pltpu.make_async_copy(dys_s, dn_out, sems.at[23])
    out_n.start()
    out_dn.start()
    for copy in (out_g, out_dp, out_n, out_dn):
        copy.wait()


def project_kernel(layer, scal, par, wo_a, wo_b, stat_own, stat_far, mix_in, p_out, wo_s, low_s, stat_s, hold_s, sems):
    sec = scal[0]
    count = mix_in.shape[0]
    from_a = pltpu.make_async_copy(wo_a, wo_s, sems.at[0])
    from_b = pltpu.make_async_copy(wo_b, wo_s, sems.at[0])

    @pl.when(sec == layer)
    def _():
        from_a.start()

    @pl.when(sec != layer)
    def _():
        from_b.start()

    stats = column_of(stat_own, hold_s) + column_of(stat_far, hold_s)
    stat_s[...] = lax.rsqrt(stats * (1.0 / DI) + EPS)
    gain_out = par[5:6, :DH]

    def rows_of(index):
        rows = tile_at(index, RC)
        low_s[rows] = (mix_in[rows] * stat_s[rows, 0:1] * gain_out).astype(bf16)

    loop(count // RC, rows_of)
    from_a.wait()

    def out_tile(index):
        lane = tile_at(index, TILE)
        p_out[:, lane] = nn(low_s[...], wo_s[:, lane]).astype(p_out.dtype)

    loop(DM // TILE, out_tile)


ANY = pl.BlockSpec(memory_space=pl.ANY)
VM = pl.BlockSpec(memory_space=pltpu.VMEM)
SM = pl.BlockSpec(memory_space=pltpu.SMEM)


def call(kernel, args, specs, outs, out_specs, scratch, name, flops):
    return pl.pallas_call(
        kernel,
        in_specs=specs,
        out_specs=out_specs,
        out_shape=[jax.ShapeDtypeStruct(shape, dtype) for shape, dtype in outs],
        scratch_shapes=scratch,
        compiler_params=pltpu.CompilerParams(vmem_limit_bytes=VMEM_BYTES),
        cost_estimate=pl.CostEstimate(
            flops=flops, bytes_accessed=20_000_000, transcendentals=4_000_000
        ),
        name=name,
    )(*args)


def vm(shape, dtype):
    return pltpu.VMEM(shape, dtype)


def run_forward(layer, scal, par, hp, weights, tokens, saved):
    count = 2 * tokens[0].shape[0]
    span = count // 2
    args = [scal, par, hp, *weights]
    specs = [SM, VM, VM] + [ANY] * 6
    if layer == 1:
        args += saved
        specs += [ANY, ANY, ANY]
    args += tokens
    specs += [ANY, ANY]
    outs = [
        ((count, DM), bf16),
        ((count + HEAD_ROWS, CP), f32),
        ((count, DH), f32),
        ((NS, DH), f32),
        ((count, DH), f32),
        ((count, DM) if layer == 1 else (8, LANE), f32),
        ((8, count), f32),
    ]
    out_specs = [ANY] * 6 + [VM]
    scratch = [
        vm((CP, DM), bf16),
        vm((DH, DM), bf16),
        vm((count, DM), bf16),
        vm((count, DM), bf16),
        vm((count + HEAD_ROWS, CP), f32),
        vm((count, CH), f32),
        vm((count, LANE), f32),
        vm((count, LANE), f32),
        vm((count, LANE), f32),
        vm((2, LANE, span), f32),
        vm((count, DH), bf16),
        vm((count, DH), f32),
        vm((count, DH), bf16),
        vm((NS, DH), f32),
        vm((2, count, DM), f32),
        vm((span, span), f32),
        vm((LANE, DH), bf16),
        vm((count, LANE), f32),
        vm((LANE, count), f32),
        vm((count, DM), bf16),
        vm((count, DH), bf16),
        pltpu.SemaphoreType.DMA((29,)),
    ]
    return call(
        functools.partial(forward_kernel, layer),
        args,
        specs,
        outs,
        out_specs,
        scratch,
        "forward_%d" % layer,
        35_000_000_000,
    )


def assemble_kernel(scal, *refs):
    got, own = refs[:3], refs[3:6]
    a1, a1_got, came, came_got, b1, b1_got = refs[6:12]
    in_out, out_out, whole_s, outer_s, in_s, out_s, sems = refs[12:]
    sec, grp = scal[0], scal[1]
    half = whole_s.shape[1] // 2
    quart = whole_s.shape[2] // 2
    outer = outer_s.shape[0] // 2
    share = b1.shape[0]

    def first_pairs(blocks, core):
        near, far, wide = blocks
        pairs = []
        for at, block in ((scal[2], near), (1 - scal[2], far)):
            rows = pl.ds(pl.multiple_of(at * half, 16), half)
            pairs.append((block, whole_s.at[core, rows]))
        return pairs + [(wide.at[pl.ds(0, outer)], outer_s.at[pl.ds(core * outer, outer)])]

    def outer_pairs(early, wide, core):
        return [
            (early, outer_s.at[pl.ds(core * outer, share)]),
            (wide.at[pl.ds(outer, share)], outer_s.at[pl.ds(core * outer + share, share)]),
        ]

    def second_pairs(block, moved, core):
        near = pl.ds(pl.multiple_of(grp * quart, quart), quart)
        far = pl.ds(pl.multiple_of((1 - grp) * quart, quart), quart)
        return [
            (block.at[:, near], whole_s.at[core, :, near]),
            (moved, whole_s.at[core, :, far]),
        ]

    def fetch(pairs):
        started = copies(pairs, sems, 0)
        for copy in started:
            copy.start()
        for copy in started:
            copy.wait()

    @pl.when(sec == 0)
    def _():
        fetch(first_pairs(own, 0) + first_pairs(got, 1))

    @pl.when(sec != 0)
    def _():
        fetch(
            second_pairs(a1, came, 1)
            + second_pairs(a1_got, came_got, 0)
            + outer_pairs(b1, own[2], 1)
            + outer_pairs(b1_got, got[2], 0)
        )

    width = in_s.shape[1]
    quarter = width // 2
    step = 64
    started = []

    def send(piece, sem):
        copy = pltpu.make_async_copy(in_s.at[piece], in_out.at[piece], sems.at[sem])
        copy.start()
        started.append(copy)

    def emit(target, source, count, side):
        def body(index):
            at = pl.multiple_of(index * step, step)
            for core in range(2):
                value = whole_s[core, pl.ds(source + at, step), side * quarter : (side + 1) * quarter]
                lane = slice(core * quarter, (core + 1) * quarter)
                in_s[pl.ds(target + at, step), lane] = value.astype(f32)

        loop(count // step, body)

    for at, (target, source, side) in enumerate(
        ((0, 0, 0), (DH, 0, 1), (DI, DH, 0), (DI + DH, DH, 1))
    ):
        emit(target, source, DH, side)
        send(pl.ds(target, DH), 8 + at)
    for core in range(2):
        lane = slice(core * quarter, (core + 1) * quarter)
        left, right = slice(0, quarter), slice(quarter, width)
        shared = slice(2 * DH, 2 * DH + 2 * NS)
        in_s[2 * DI : 2 * DI + 2 * NS, lane] = whole_s[core, shared, left].astype(f32) + whole_s[
            core, shared, right
        ].astype(f32)
        steps = slice(DH + CH, DH + CH + HL)
        in_s[DI + CONVC : DI + CONVC + HL, lane] = whole_s[core, steps, left].astype(f32)
        in_s[DI + CONVC + HL :, lane] = whole_s[core, steps, right].astype(f32)
    send(pl.ds(2 * DI, 2 * NS + HEADS), 12)

    def body(index):
        rows = tile_at(index, step)
        out_s[rows] = outer_s[rows].astype(f32)

    loop(out_s.shape[0] // step, body)
    copy = pltpu.make_async_copy(out_s, out_out, sems.at[13])
    copy.start()
    started.append(copy)
    for copy in started:
        copy.wait()


def run_assemble(scal, got, own, second, columns):
    rows, width = second[0].shape
    outer = (4 * second[-1].shape[0], second[-1].shape[1])
    return call(
        assemble_kernel,
        [scal, *got, *own, *second],
        [SM] + [ANY] * 12,
        [((columns, width), f32), (outer, f32)],
        [ANY, ANY],
        [
            vm((2, rows, width), bf16),
            vm(outer, bf16),
            vm((columns, width), f32),
            vm(outer, f32),
            pltpu.SemaphoreType.DMA((14,)),
        ],
        "assemble",
        6_000_000_000,
    )


def run_project(layer, scal, par, wo_a, wo_b, stat_own, stat_far, mixed):
    count = mixed.shape[0]
    return call(
        functools.partial(project_kernel, layer),
        [scal, par, wo_a, wo_b, stat_own, stat_far, mixed],
        [SM, VM, ANY, ANY, VM, VM, VM],
        [((count, DM), f32)],
        [VM],
        [
            vm((DH, DM), bf16),
            vm((count, DH), bf16),
            vm((count, LANE), f32),
            vm((LANE, count), f32),
            pltpu.SemaphoreType.DMA((1,)),
        ],
        "project_%d" % layer,
        6_000_000_000,
    )[0]


def run_backward(layer, scal, par, hp, weights, saved, tokens, late):
    count = 2 * tokens[0].shape[0]
    span = count // 2
    args = [scal, par, hp, *weights, *saved, *tokens]
    specs = [SM, VM, VM] + [ANY] * 6 + [ANY] * 4 + [VM, VM] + [ANY] * 2
    if layer == 0:
        args += late
        specs += [ANY] * 4 + [VM]
    outs = [
        ((count, DM), bf16),
        ((count, CP), bf16),
        ((count, DH), bf16),
        ((count, DM), bf16),
        ((count, DM), bf16),
        ((16, CH), f32),
    ]
    out_specs = [ANY] * 5 + [VM]
    scratch = [
        vm((CP, DM), bf16),
        vm((DH, DM), bf16),
        vm((count, DM), bf16),
        vm((count, DM), bf16),
        vm((count + HEAD_ROWS, CP), f32),
        vm((count, CH), f32),
        vm((count, CH), f32),
        vm((count, LANE), f32),
        vm((count, LANE), f32),
        vm((count, LANE), f32),
        vm((2, LANE, span), f32),
        vm((count, LANE), f32),
        vm((count, DH), bf16),
        vm((count, DH), f32),
        vm((NS, DH), f32),
        vm((NS, DH), f32),
        vm((count, DM), f32),
        vm((2, count, DM), bf16),
        vm((count, DM), bf16),
        vm((count, DM), bf16),
        vm((count, DM), f32),
        vm((count, DM), bf16),
        vm((count, DH), f32),
        vm((count + 8, CH), f32),
        vm((count, CP), bf16),
        vm((span, span), f32),
        vm((span, span), f32),
        vm((LANE, DH), bf16),
        vm((DH, LANE), bf16),
        vm((count, LANE), f32),
        vm((LANE, count), f32),
        vm((count, DH), bf16),
        vm((count, DH), bf16),
        pltpu.SemaphoreType.DMA((29,)),
    ]
    return call(
        functools.partial(backward_kernel, layer),
        args,
        specs,
        outs,
        out_specs,
        scratch,
        "backward_%d" % layer,
        55_000_000_000,
    )


def swap(block, axis):
    return lax.ppermute(block, axis, [(0, 1), (1, 0)])


def flip(block, mask):
    size = lax.axis_size("replica")
    return lax.ppermute(block, "replica", [(at, at ^ mask) for at in range(size)])


def add_low(left, right):
    return (left.astype(f32) + right.astype(f32)).astype(bf16)


def halves(block, which):
    size = block.shape[0] // 2
    keep = lax.dynamic_slice_in_dim(block, which * size, size, 0)
    send = lax.dynamic_slice_in_dim(block, (1 - which) * size, size, 0)
    return keep, send


def stages_of(bits):
    return [(at,) for at in range(bits)]


def scatter_sum(pieces, stages, rep):
    for (bit,) in stages:
        cut = [halves(piece, (rep >> bit) & 1) for piece in pieces]
        sent = flip(sum_low([send for keep, send in cut]), 1 << bit)
        pieces = [sum_low([keep for keep, send in cut]), sent]
    return sum_low(pieces)


def sum_low(pieces):
    total = pieces[0].astype(f32)
    for piece in pieces[1:]:
        total = total + piece.astype(f32)
    return total.astype(bf16)


def collect(block, stage, rep):
    pieces = [block] + [flip(block, away << stage[0]) for away in range(1, 1 << len(stage))]
    for level in range(len(stage)):
        which = (rep >> stage[level]) & 1
        pieces = [
            in_order(pieces[at], pieces[at + 1], which, 0) for at in range(0, len(pieces), 2)
        ]
    return pieces[0]


def in_order(mine, other, which, dim):
    return jnp.where(
        which == 0,
        jnp.concatenate([mine, other], axis=dim),
        jnp.concatenate([other, mine], axis=dim),
    )


def gather_back(block, order, rep):
    for bit in reversed(order):
        block = in_order(block, flip(block, bit), (rep >> bit) & 1, 0)
    return block


def on_device(
    first_layer_input,
    boundary,
    input_gain,
    in_proj,
    conv_weight,
    conv_bias,
    head_params,
    output_gain,
    out_proj,
    cotangent,
):
    sec = lax.axis_index("section")
    grp = lax.axis_index("group")
    rep = lax.axis_index("replica")
    replicas = lax.axis_size("replica")
    bits = replicas.bit_length() - 1
    order_a = stages_of(bits)
    order_b = order_a[1::-1] + order_a[2:]

    bound = lax.dynamic_index_in_dim(boundary[:, 0], sec, 0, keepdims=False)
    scal = jnp.stack([sec, grp, bound]).astype(jnp.int32)
    u_own = lax.dynamic_index_in_dim(first_layer_input[:, 0], sec, 0, keepdims=False)
    u_far = swap(u_own, "group")
    cot_own = lax.dynamic_index_in_dim(cotangent[:, 0], sec, 0, keepdims=False)

    block = jnp.swapaxes(in_proj, 1, 2)[0]
    far_grp = 1 - grp

    def far_part(which):
        return jnp.concatenate(
            [
                lax.dynamic_slice_in_dim(block, which * DI + far_grp * DH, DH, 0),
                lax.dynamic_slice_in_dim(block, 2 * DI + which * NS, NS, 0),
                lax.dynamic_slice_in_dim(block, DI + CONVC + far_grp * HL, HL, 0),
            ],
            axis=0,
        )

    keep, give = far_part(sec), far_part(1 - sec)
    got = swap(give, "section")
    first_x = swap(jnp.where(sec == 0, keep, got), "group")
    keep, got, cot_own, first_x = lax.optimization_barrier((keep, got, cot_own, first_x))
    second_x = swap(jnp.where(sec == 1, keep, got), "group")
    cot_far = swap(cot_own, "group")
    w_a, w_b = block, swap(block, "section")
    wo_a = out_proj[0]
    wo_b = swap(wo_a, "section")
    weights = [
        (w_a, w_b, w_x, swap(w_x, "section"), wo_a, wo_b) for w_x in (first_x, second_x)
    ]

    width = conv_bias.shape[1]
    half_in = input_gain.shape[1]

    def row_of(*pieces):
        line = jnp.concatenate(pieces)
        return jnp.pad(line, (0, width - line.shape[0]))[None]

    smalls = jnp.concatenate(
        [
            conv_weight[0].T,
            conv_bias,
            row_of(output_gain[0]),
            row_of(input_gain[0], head_params[0].T.reshape(-1)),
            jnp.zeros((1, width), bf16),
        ],
        axis=0,
    )
    both = in_order(smalls[None], swap(smalls, "section")[None], sec, 0)
    far_both = swap(both, "group")
    both = both.astype(f32)
    full = in_order(both, far_both.astype(f32), grp, 2)
    pars, hps = [], []
    for layer in range(2):
        taps = jnp.concatenate(
            [
                lax.dynamic_slice_in_dim(full[layer, 0:5], grp * DH, DH, 1),
                full[layer, 0:5, DI:],
            ],
            axis=1,
        )
        line = both[layer, 6]
        heads = line[half_in : half_in + 3 * HL].reshape(3, HL)
        gain_in = jnp.concatenate(
            [full[layer, 6, :half_in], full[layer, 6, width : width + half_in]]
        )
        rest = jnp.stack([both[layer, 5, :DH], gain_in, jnp.repeat(heads[2], HDIM)])
        pars.append(jnp.concatenate([taps, jnp.pad(rest, ((0, 0), (0, CH - DH)))], axis=0))
        lines = jnp.stack([heads[0], jnp.exp(heads[1]), heads[2]])
        hps.append(jnp.pad(lines, ((0, 5), (0, LANE - HL))))

    tokens = [u_own, u_far]
    cots = [cot_own, cot_far]
    quarter = half_in // 2

    def own_quarter(normed):
        return jnp.concatenate(
            [
                lax.dynamic_slice_in_dim(normed, at * half_in + sec * quarter, quarter, 1)
                for at in range(2)
            ],
            axis=1,
        )

    def own_channels(gated):
        return lax.dynamic_slice_in_dim(gated, sec * (DH // 2), DH // 2, 1)

    def join_in(normed, dproj):
        far_n, far_p = swap(normed, "section"), swap(dproj, "section")
        return (tn(dproj, own_quarter(normed)) + tn(far_p, own_quarter(far_n))).astype(bf16)

    def join_out(gated, upstream):
        far_g, far_u = swap(gated, "section"), swap(upstream, "section")
        return (tn(own_channels(gated), upstream) + tn(own_channels(far_g), far_u)).astype(bf16)

    def guarded(branch, operand):
        shapes = jax.eval_shape(branch, operand)

        def nothing(operand):
            return jax.tree.map(lambda leaf: jnp.zeros(leaf.shape, leaf.dtype), shapes)

        return lax.cond(bound >= 0, branch, nothing, operand)

    u0, proj0, ys0, st0, mix0, unused_sum, stat0 = guarded(
        lambda tokens: run_forward(0, scal, pars[0], hps[0], weights[0], tokens, None), tokens
    )
    stat0_far = swap(stat0, "group")
    p0 = run_project(0, scal, pars[0], wo_a, wo_b, stat0, stat0_far, mix0)
    p0, cot_far = lax.optimization_barrier((p0, cot_far))
    cots = [cot_own, cot_far]
    p0_far = swap(p0.astype(jnp.float16), "group").astype(f32)
    u1, proj1, ys1, st1, mix1, p_total, stat1 = run_forward(
        1, scal, pars[1], hps[1], weights[1], cots, [u0, p0, p0_far]
    )
    stat1_far = swap(stat1, "group")
    piece = u_own.shape[0]

    def own_rows(block):
        return lax.dynamic_slice_in_dim(block, grp * piece, piece, 0)

    def far_rows(block):
        return lax.dynamic_slice_in_dim(block, (1 - grp) * piece, piece, 0)

    scale1 = lax.rsqrt((stat1 + stat1_far)[0] * (1.0 / DI) + EPS)[:, None]
    gated1 = (mix1 * scale1 * pars[1][5:6, :DH]).astype(bf16)
    b1 = join_out(gated1, in_order(cot_own, cot_far, grp, 0))
    stat1_far, b1 = lax.optimization_barrier((stat1_far, b1))
    share = b1.shape[0] // 2
    b1_late = b1[share:]
    b1 = lax.psum(b1[:share], "replica")

    def second_layer(stat1_far):
        n1, dp1, unused_gated, unused_g, dn1, small1 = run_backward(
            1, scal, pars[1], hps[1], weights[1],
            [u1, proj1, ys1, st1, stat1, stat1_far], cots, None,
        )
        dn1_far = swap(dn1, "group")
        dn1_far, a1 = lax.optimization_barrier((dn1_far, join_in(n1, dp1)))
        return dn1, dn1_far, a1, small1

    dn1, dn1_far, a1, small1 = guarded(second_layer, stat1_far)
    a1, b1 = lax.optimization_barrier((a1, b1))
    a1 = lax.psum(a1, "replica")

    def to_sections(first, second):
        held = jnp.where(sec == 0, first, second)
        given = swap(jnp.where(sec == 0, second, first), "section")
        return in_order(held[None], given[None], sec, 0)

    def swap_rows(part_a):
        stay = lax.dynamic_slice_in_dim(part_a, grp * quarter, quarter, 1)
        leave = lax.dynamic_slice_in_dim(part_a, far_grp * quarter, quarter, 1)
        return in_order(stay, swap(leave, "group"), grp, 1)

    def to_owner(block, layer):
        return lax.ppermute(block, "section", [(1 - layer, layer)])

    def gather_back(block, stages):
        for stage in reversed(stages):
            block = collect(block, stage, rep)
        return block

    def first_layer(dn1_far):
        n0, dp0, gated0, g0, dn0, small0 = run_backward(
            0, scal, pars[0], hps[0], weights[0],
            [u0, proj0, ys0, st0, stat0, stat0_far], cots,
            [p_total, u1, dn1, dn1_far, pars[1]],
        )
        a0 = join_in(n0, dp0)
        b0 = jnp.concatenate([join_out(gated0, g0), b1_late], axis=0)
        cut = [halves(block, (rep >> stages[0][0]) & 1) for block, stages in ((a0, order_a), (b0, order_b))]
        cut, dn0, g0, small0, late_gated, late_small = lax.optimization_barrier(
            (cut, dn0, g0, small0, gated1, small1)
        )
        sent = [
            flip(send, 1 << stages[0][0])
            for (keep, send), stages in zip(cut, (order_a, order_b))
        ]
        dn0_far = swap(far_rows(dn0), "group")

        p1 = nn(late_gated, jnp.where(sec == 1, wo_a, wo_b))
        p1_far = swap(far_rows(p1).astype(bf16), "group")
        small = jnp.stack([small0, late_small])
        small = small + swap(small, "section")
        far = swap(small, "group")
        shared = small + far
        own_x = jnp.concatenate([small[:, 0:5, :DH], far[:, 0:5, :LANE]], axis=2)
        own_y = jnp.concatenate([small[:, 0:5, LANE:DH], shared[:, 0:5, DH:]], axis=2)
        conv_part = jnp.where(grp == 0, own_x, own_y)
        gain_in = lax.dynamic_slice_in_dim(shared[:, 6, :DM], grp * half_in, half_in, 1)
        skip = small[:, 7, :DH].reshape(2, HL, HDIM).sum(axis=2)
        line = jnp.concatenate([gain_in, small[:, 8, :HL], small[:, 9, :HL], skip], axis=1)
        packed = jnp.concatenate(
            [
                conv_part,
                jnp.pad(small[:, 5:6, :DH], ((0, 0), (0, 0), (0, width - DH))),
                jnp.pad(line, ((0, 0), (0, width - line.shape[1])))[:, None],
                jnp.zeros((2, 1, width), f32),
            ],
            axis=1,
        )
        sent, dn0_far, p1_far, packed = lax.optimization_barrier((sent, dn0_far, p1_far, packed))
        state = [[keep, came] for (keep, send), came in zip(cut, sent)]
        values = u_own.astype(f32)
        scale = lax.rsqrt(jnp.mean(values * values, axis=-1, keepdims=True) + EPS)
        arrived = (own_rows(dn0).astype(f32) + dn0_far.astype(f32)) * pars[0][6:7, :DM]
        inner = jnp.mean(arrived * values, axis=-1, keepdims=True)
        grad1 = own_rows(g0)
        grad0 = (
            grad1.astype(f32) + scale * arrived - values * (scale * scale * scale * inner)
        ).astype(bf16)

        input_grad = to_sections(grad0, grad1)
        out0 = own_rows(u1)
        out1 = (out0.astype(f32) + own_rows(p1) + p1_far.astype(f32)).astype(bf16)
        segment_output = to_sections(out0, out1)
        for at in range(1, bits):
            cut = [
                [halves(piece, (rep >> stages[at][0]) & 1) for piece in pieces]
                for pieces, stages in zip(state, (order_a, order_b))
            ]
            sent = [
                flip(sum_low([send for keep, send in pair]), 1 << stages[at][0])
                for pair, stages in zip(cut, (order_a, order_b))
            ]
            far_packed = flip(packed, 1 << at)
            state = [
                [sum_low([keep for keep, send in pair]), came] for pair, came in zip(cut, sent)
            ]
            state, far_packed = lax.optimization_barrier((state, far_packed))
            packed = packed + far_packed
        a0, b0 = sum_low(state[0]), sum_low(state[1])
        far_packed = flip(packed, 1)
        a0 = swap_rows(a0)
        a0, far_packed = lax.optimization_barrier((a0, far_packed))
        packed = packed + far_packed
        a0, b0 = gather_back(a0, order_a[1:]), gather_back(b0, order_b[1:])
        packed = jnp.where(sec == 0, packed[0], packed[1])
        heads = packed[6, half_in : half_in + 3 * HL].reshape(3, HL)
        smalls = (packed[6:7, :half_in], packed[0:4], packed[4:5], heads, packed[5:6, :DH])
        return segment_output, input_grad, smalls, a0, b0

    segment_output, input_grad, smalls, a0, b0 = guarded(first_layer, dn1_far)
    a0_far = flip(a0, 1 << order_a[0][0])
    b0 = collect(b0, order_b[0], rep)
    came = swap(lax.dynamic_slice_in_dim(a1, far_grp * quarter, quarter, 1), "group")
    side = (rep >> order_a[0][0]) & 1
    grad_in_proj, grad_out_proj = run_assemble(
        jnp.stack([sec, grp, side]).astype(jnp.int32),
        [to_owner(a0, 0), to_owner(a0_far, 0), swap(b0, "section")],
        [a0, a0_far, b0],
        [a1, to_owner(a1, 1), came, to_owner(came, 1), b1, to_owner(b1, 1)],
        in_proj.shape[2],
    )
    grad_in_proj = jnp.swapaxes(grad_in_proj, 0, 1)
    return (
        segment_output[None, :, None],
        input_grad[None, :, None],
        smalls[0],
        grad_in_proj[None],
        smalls[1].T[None],
        smalls[2],
        smalls[3].T[None],
        smalls[4],
        grad_out_proj[None],
    )


def solution(mesh):
    placed = (
        P(None, "replica", "group", None),
        P(None, "replica"),
        P("section", "group"),
        P("section", "group", None),
        P("section", "group", None),
        P("section", "group"),
        P("section", "group", None),
        P("section", "group"),
        P("section", "group", None),
        P(None, "replica", "group", None),
    )
    return jax.shard_map(
        on_device,
        mesh=mesh,
        in_specs=placed,
        out_specs=(
            P("section", None, "replica", "group", None),
            P("section", None, "replica", "group", None),
            P("section", "group"),
            P("section", "group", None),
            P("section", "group", None),
            P("section", "group"),
            P("section", "group", None),
            P("section", "group"),
            P("section", "group", None),
        ),
        check_vma=False,
    )
```
